32 devices in a mesh: groups: 2 (over y), panels: 4 (over z), nodes: 2 (over x), rhs: 2 (over core).
Axes of the slice: x: 2, y: 2, z: 4, core: 2. Of those that a mesh axis runs over, the one named last changes fastest.
Arguments:
- residual: float32 [8, 2, 16, 2048], P(('groups', 'nodes'), None, 'rhs', 'panels'), parts along dimension 0, may hold values from -30 to 30
- iterate: float32 [8, 2, 16, 2048], P(('groups', 'nodes'), None, 'rhs', 'panels'), parts along dimension 0, may hold values from -6 to 6
- probe: float32 [4, 16, 2048], P('groups', 'rhs', 'panels'), parts along dimension 0, may hold values from -6 to 6
- contour: float32 [6], P('groups'), parts along dimension 0, may hold values from 0.5 to 1.5
- near_tiles: bfloat16 [256, 2, 128, 128], P(('groups', 'panels')), parts along dimension 0, may hold values from -0.5 to 0.5
- near_col: int32 [256], P(('groups', 'panels')), parts along dimension 0, may hold values from 0 to 3
- near_row: int32 [256], P(('groups', 'panels')), parts along dimension 0, may hold values from 0 to 3
- near_dest: int32 [256, 1], P(('groups', 'panels')), parts along dimension 0, may hold values from 0 to 3; in each aligned block of 32 rows (0 to 31, 32 to 63, ...) at most 16 rows name the same one
- far_right: bfloat16 [128, 2, 32, 128], P(('groups', 'panels')), parts along dimension 0, may hold values from -0.5 to 0.5
- far_col: int32 [128], P(('groups', 'panels')), parts along dimension 0, may hold values from 0 to 3
- far_rank: int32 [128], P(('groups', 'panels')), parts along dimension 0, may hold values from 8 to 32
- far_target: int32 [128], P(('groups', 'panels')), parts along dimension 0, may hold values from 0 to 15
- far_left: bfloat16 [32, 2, 128, 32], P(('groups', 'panels')), parts along dimension 0, may hold values from -1 to 1
Outputs:
- residual_next: float32 [8, 2, 16, 2048], P(('groups', 'nodes'), None, 'rhs', 'panels'), parts along dimension 0
- moments: float32 [8, 2, 16, 2048], P(('groups', 'nodes'), None, 'rhs', 'panels'), parts along dimension 0
- hankel: float32 [8, 2, 16, 16], P(('groups', 'nodes'), None, None, 'rhs'), parts along dimension 0
The draws below stay inside these ranges and needn't reach their ends.
There are 2 independent parts, one for each index of `groups`. The reference program is written for one: setup_inputs(seed, part) draws one part's arguments, and reference() takes and returns one part's arrays. A program takes and returns all parts, laid end to end along the dimension named above; each array names one. Nothing has to cross between parts.
Inputs may be any that keep to these rules, and one draw needn't show every extreme that they name: `near_dest`: the tiles stored with one device (aligned blocks of 32) aim at most 16 tiles at one device; some device receives exactly 16 from some device.
All inputs are finite; a program needn't handle non-finite values.
Results may differ from the reference program's by a relative error of at most 0.0012.
Values sent between devices are 32-bit elements; how exact they have to be, the bound alone decides.
No kernel may reach another device: no remote copies, remote signals or barrier semaphores. Data moves between devices by JAX's collectives and lax.ppermute only.
A program may use at most 64 MiB of HBM per device.

```python
import math
import jax
import jax.numpy as jnp
import numpy as np
from jax import lax

TB = 128
BLK_DEV = 4
RANK = 32
PANELS = 2048
NBLOCKS = 16
TILES_DEV = 32
TILES = 128
FAR_DEV = 16
FAR = 64
CAP = 16
NODES = 4
RHS = 16
MOMENTS = 4
N_PANELS = 4


def draw_residual(key, part):
    key = jax.random.fold_in(key, 11)
    key_noise, key_spread = jax.random.split(key, 2)
    positions = jnp.arange(PANELS, dtype=jnp.float32)
    rising = 1.0 + 2.0 * positions / PANELS
    spread = jnp.exp(jax.random.uniform(key_spread, (PANELS,), dtype=jnp.float32) * math.log(10.0))
    noise = jnp.clip(jax.random.normal(key_noise, (NODES, 2, RHS, PANELS), dtype=jnp.float32), -6.0, 6.0)
    return (noise * spread * rising / 6.0).astype(jnp.float32)


def set_ends(values, rng, smallest, largest):
    longest = values.shape.index(max(values.shape))
    spots = []
    for shift in (0, 1):
        where = [jax.random.randint(jax.random.fold_in(rng, axis), (), 0, length) for axis, length in enumerate(values.shape)]
        where[longest] = (where[longest] + shift) % values.shape[longest]
        spots.append(tuple(where))
    return values.at[spots[0]].set(smallest).at[spots[1]].set(largest)


def level_of(own_key, dims, shards, smallest, top_value):
    level = 1.0
    for dim, blocks in shards:
        heights = jax.random.uniform(jax.random.fold_in(jax.random.fold_in(own_key, 6), dim), (blocks,), jnp.float32, smallest / len(shards), top_value / len(shards))
        level = level * jnp.repeat(jnp.exp(heights), dims[dim] // blocks).reshape((-1,) + (1,) * (len(dims) - 1 - dim))
    return level


def shared_out(key, own, number, rows, number_of, top, bound, lean):
    ranking = jax.random.permutation(key, number_of)
    crowded, usual = load_shares(number_of, rows * top, bound, lean, True), load_shares(number_of, rows * top, bound, lean, False)
    places = jnp.arange(number_of)

    def named(tallies, offset_by):
        used = int((tallies > 0).sum())
        fixed = max(1, used // 4)
        shifted = fixed + (places - fixed + offset_by * (used - fixed)) % max(1, number_of - fixed)
        return jnp.zeros((number_of,), jnp.int32).at[ranking[jnp.where(places < fixed, places, shifted)]].set(jnp.asarray(tallies, jnp.int32))

    tallies = jnp.where(number % 4 == 0, named(crowded, number // 4), named(usual, number - number // 4 - 1))
    mixed = jax.random.permutation(jax.random.fold_in(own, 3), number_of)
    donor, taker = mixed[0:number_of // 2 * 2:2], mixed[1:number_of // 2 * 2:2]
    margin = jnp.minimum(tallies[donor] - 1, bound - tallies[taker]) // 2
    margin = jnp.where((donor == ranking[0]) | (taker == ranking[0]) | (tallies[taker] == 0), 0, jnp.maximum(margin, 0))
    shifted = jax.random.randint(jax.random.fold_in(own, 4), (number_of // 2,), 0, 1 << 20) % (margin + 1)
    tallies = tallies.at[donor].add(-shifted).at[taker].add(shifted)
    labels = jnp.searchsorted(jnp.cumsum(tallies), jnp.arange(rows * top), side="right").astype(jnp.int32)
    listing = labels.reshape(top, rows).T
    listing = listing[jax.random.permutation(jax.random.fold_in(own, 1), rows)]
    offset_by = jax.random.randint(jax.random.fold_in(own, 2), (rows, 1), 0, top)
    return jnp.take_along_axis(listing, (jnp.arange(top)[None, :] + offset_by) % top, axis=1)


def load_shares(count, total, most, slope, full):
    loads = [(1 << 20) // math.isqrt(rank ** slope) + 1 for rank in range(1, count + 1)]
    largest = most if full else min(most, max(-(-total // count), total * loads[0] // sum(loads)))
    least = 1 if total - largest >= count - 1 else 0
    counts, spare = [largest] + [least] * (count - 1), total - largest - least * (count - 1)
    while spare > 0:
        movable = [i for i in range(1, count) if counts[i] < largest] or [i for i in range(1, count) if counts[i] < most]
        whole, budget = sum([loads[i] for i in movable]), spare
        for i in movable:
            extra = min(most - counts[i], max(1, budget * loads[i] // whole), spare)
            counts[i] = counts[i] + extra
            spare = spare - extra
    return np.array(counts)


def centred(stream_key, dims, deviation, reach, shards=(), held_as=jnp.bfloat16):
    drawn = jax.random.normal(stream_key, dims, jnp.float32) * deviation
    if len(shards) > 0:
        drawn = level_of(stream_key, dims, shards, -0.22, 0.18) * drawn
    return jnp.clip(drawn, min=-reach, max=reach).astype(held_as)


def setup_inputs(seed: int = 0, part: int = 0) -> dict:
    keys = jax.random.split(jax.random.key(seed), 14)
    part_keys = jax.random.split(jax.random.fold_in(keys[13], part), 14)
    residual = draw_residual(jax.random.fold_in(jax.random.fold_in(keys[13], part), 71), part)
    iterate = centred(part_keys[1], (NODES, 2, RHS, PANELS), 1.0, 6.0, ((0, 2), (2, 2), (3, 4)), jnp.float32)
    probe = centred(part_keys[2], (2, RHS, PANELS), 1.0, 6.0, ((1, 2), (2, 4)), jnp.float32)
    contour = jnp.clip(jax.random.uniform(part_keys[3], (3,), jnp.float32, 0.5, 1.5), 0.5, 1.5)
    near_tiles = centred(part_keys[4], (TILES, 2, TB, TB), TB ** -0.5, 0.5, ((0, 4),))
    near_col = set_ends(jax.random.randint(part_keys[5], (TILES,), 0, BLK_DEV), jax.random.fold_in(part_keys[5], 1), 0, BLK_DEV - 1).astype(jnp.int32)
    near_row = set_ends(jax.random.randint(part_keys[6], (TILES,), 0, BLK_DEV), jax.random.fold_in(part_keys[6], 1), 0, BLK_DEV - 1).astype(jnp.int32)
    near_dest_keys = jax.random.split(jax.random.fold_in(part_keys[7], 1), TILES // TILES_DEV)
    near_dest_turns = jax.random.permutation(jax.random.fold_in(part_keys[7], 3), TILES // TILES_DEV)
    near_dest = jax.vmap(lambda own, number: shared_out(jax.random.fold_in(part_keys[7], 2), own, number, TILES_DEV, N_PANELS, 1, CAP, 2))(near_dest_keys, near_dest_turns).reshape((TILES, 1))
    far_right = centred(part_keys[8], (FAR, 2, RANK, TB), TB ** -0.5, 0.5, ((0, 4),))
    far_col = set_ends(jax.random.randint(part_keys[9], (FAR,), 0, BLK_DEV), jax.random.fold_in(part_keys[9], 1), 0, BLK_DEV - 1).astype(jnp.int32)
    far_rank = set_ends(jax.random.randint(part_keys[10], (FAR,), RANK // 4, RANK + 1), jax.random.fold_in(part_keys[10], 1), RANK // 4, RANK).astype(jnp.int32)
    far_target = set_ends(jax.random.randint(part_keys[11], (FAR,), 0, NBLOCKS), jax.random.fold_in(part_keys[11], 1), 0, NBLOCKS - 1).astype(jnp.int32)
    far_left = centred(part_keys[12], (NBLOCKS, 2, TB, RANK), RANK ** -0.5, 1.0, ((0, 4),))
    return {"residual": residual, "iterate": iterate, "probe": probe, "contour": contour, "near_tiles": near_tiles, "near_col": near_col, "near_row": near_row, "near_dest": near_dest, "far_right": far_right, "far_col": far_col, "far_rank": far_rank, "far_target": far_target, "far_left": far_left}


highest = lax.Precision.HIGHEST

def complex_apply(vec_in, mat_in):

    def single(vec_part, mat_part):
        return jnp.einsum('tcj,tij->tci', vec_part.astype(jnp.float32), mat_part.astype(jnp.float32))
    real_part = single(vec_in[:, 0], mat_in[:, 0]) - single(vec_in[:, 1], mat_in[:, 1])
    imag_part = single(vec_in[:, 0], mat_in[:, 1]) + single(vec_in[:, 1], mat_in[:, 0])
    return jnp.stack([real_part, imag_part], axis=1)

def gram_pair(product, source):

    def inner_sum(one_side, other_side):
        return jnp.einsum('kan,kbn->kab', one_side, other_side, precision=highest)
    prod_re, prod_im = (product[:, 0], product[:, 1])
    src_re, src_im = (source[:, 0], source[:, 1])
    gram_re = inner_sum(prod_re, prod_re) + inner_sum(prod_im, prod_im)
    gram_im = inner_sum(prod_re, prod_im) - inner_sum(prod_im, prod_re)
    cross_re = inner_sum(prod_re, src_re) + inner_sum(prod_im, src_im)
    cross_im = inner_sum(prod_re, src_im) - inner_sum(prod_im, src_re)
    return (gram_re, gram_im, cross_re, cross_im)

def solve_block(gram_re, gram_im, cross_re, cross_im):
    upper_half = jnp.concatenate([gram_re, -gram_im], axis=2)
    lower_half = jnp.concatenate([gram_im, gram_re], axis=2)
    system = jnp.concatenate([upper_half, lower_half], axis=1)
    target = jnp.concatenate([cross_re, cross_im], axis=1)
    factor = jnp.linalg.cholesky(system)
    half_solved = lax.linalg.triangular_solve(factor, target, left_side=True, lower=True)
    coeffs = lax.linalg.triangular_solve(factor, half_solved, left_side=True, lower=True, transpose_a=True)
    width = gram_re.shape[1]
    return (coeffs[:, :width], coeffs[:, width:])

def apply_coeffs(source, coef_re, coef_im):

    def mix_rows(src_part, coef_part):
        return jnp.einsum('kan,kab->kbn', src_part, coef_part, precision=highest)
    out_re = mix_rows(source[:, 0], coef_re) - mix_rows(source[:, 1], coef_im)
    out_im = mix_rows(source[:, 0], coef_im) + mix_rows(source[:, 1], coef_re)
    return jnp.stack([out_re, out_im], axis=1)

def moment_terms(iterate_new, angles, radius, nodes_all, powers):
    angle_grid = (powers[:, None] + 1.0) * angles[None, :]
    weight_re = radius / nodes_all * jnp.cos(angle_grid)
    weight_im = radius / nodes_all * jnp.sin(angle_grid)

    def mix_nodes(weight_part, src_part):
        return jnp.einsum('pk,kbn->pbn', weight_part, src_part, precision=highest)
    out_re = mix_nodes(weight_re, iterate_new[:, 0]) - mix_nodes(weight_im, iterate_new[:, 1])
    out_im = mix_nodes(weight_re, iterate_new[:, 1]) + mix_nodes(weight_im, iterate_new[:, 0])
    return jnp.stack([out_re, out_im], axis=1)

def hankel_terms(probe_full, moment_part, scale_factor):

    def inner_sum(one_side, other_side):
        return jnp.einsum('an,pbn->pab', one_side, other_side, precision=highest)
    out_re = inner_sum(probe_full[0], moment_part[:, 0]) + inner_sum(probe_full[1], moment_part[:, 1])
    out_im = inner_sum(probe_full[0], moment_part[:, 1]) - inner_sum(probe_full[1], moment_part[:, 0])
    return jnp.stack([out_re, out_im], axis=1) * scale_factor

def reference(residual, iterate, probe, contour, near_tiles, near_col, near_row, near_dest, far_right, far_col, far_rank, far_target, far_left):
    nblocks = PANELS // TB
    cols_all = NODES * RHS
    lowered = residual.astype(jnp.bfloat16).reshape(NODES, 2, RHS, nblocks, TB)
    lowered = lowered.transpose(3, 1, 0, 2, 4).reshape(nblocks, 2, cols_all, TB)
    tile_source = jnp.arange(TILES, dtype=jnp.int32) // TILES_DEV * BLK_DEV + near_col
    tile_target = near_dest[:, 0] * BLK_DEV + near_row
    near_terms = complex_apply(lowered[tile_source], near_tiles)
    near_sum = jax.ops.segment_sum(near_terms, tile_target, num_segments=nblocks)
    far_source = jnp.arange(FAR, dtype=jnp.int32) // FAR_DEV * BLK_DEV + far_col
    skeleton = complex_apply(lowered[far_source], far_right)
    rank_mask = (jnp.arange(RANK, dtype=jnp.int32)[None, :] < far_rank[:, None]).astype(jnp.float32)
    skeleton = skeleton * rank_mask[:, None, None, :]
    summed = jax.ops.segment_sum(skeleton, far_target, num_segments=nblocks).astype(jnp.bfloat16)
    far_part = complex_apply(summed, far_left)
    applied = (near_sum + far_part).reshape(nblocks, 2, NODES, RHS, TB)
    applied = applied.transpose(2, 1, 3, 0, 4).reshape(NODES, 2, RHS, PANELS)
    angles = 2.0 * math.pi * (jnp.arange(NODES, dtype=jnp.int32).astype(jnp.float32) + 0.5) / NODES
    shift_re = (contour[0] + contour[2] * jnp.cos(angles))[:, None, None]
    shift_im = (contour[1] + contour[2] * jnp.sin(angles))[:, None, None]
    res_re, res_im = (residual[:, 0], residual[:, 1])
    prod_re = applied[:, 0] - (shift_re * res_re - shift_im * res_im)
    prod_im = applied[:, 1] - (shift_re * res_im + shift_im * res_re)
    product = jnp.stack([prod_re, prod_im], axis=1)
    coef_re, coef_im = solve_block(*gram_pair(product, residual))
    iterate_new = iterate + apply_coeffs(residual, coef_re, coef_im)
    residual_next = residual - apply_coeffs(product, coef_re, coef_im)
    powers = jnp.arange(MOMENTS, dtype=jnp.int32).astype(jnp.float32)
    moments = moment_terms(iterate_new, angles, contour[2], NODES, powers)
    hankel = hankel_terms(probe, moments, 1.0 / math.sqrt(PANELS))
    return (residual_next, moments, hankel)
```

```python
import functools
import math

import jax
import jax.numpy as jnp
import numpy as np
from jax import lax
from jax.experimental import pallas as pl
from jax.experimental.pallas import tpu as pltpu
from jax.sharding import PartitionSpec as P

MOM_DEV = 2
LANES = 128
DIRECT_PEERS = 8
TILE_CHUNK = 4

f32 = jnp.float32
bf16 = jnp.bfloat16

PARAMS = pltpu.CompilerParams(vmem_limit_bytes=40 * 1024 * 1024)
VMEM = pl.BlockSpec(memory_space=pltpu.VMEM)
SMEM = pl.BlockSpec(memory_space=pltpu.SMEM)
ANY = pl.BlockSpec(memory_space=pl.ANY)


def dot_t(left, right):
    return lax.dot_general(left, right, (((1,), (1,)), ((), ())), preferred_element_type=f32)


def dot_n(left, right):
    return lax.dot_general(left, right, (((1,), (0,)), ((), ())), preferred_element_type=f32)


def split(value):
    high = value.astype(bf16)
    return high, (value - high.astype(f32)).astype(bf16)


def dot3_t(left, right):
    (l_hi, l_lo), (r_hi, r_lo) = left, right
    rows = l_hi.shape[0]
    both = dot_t(jnp.concatenate([l_hi, l_lo], axis=0), r_hi)
    return both[:rows] + both[rows:] + dot_t(l_hi, r_lo)


def dot3_n(left, right):
    (l_hi, l_lo), (r_hi, r_lo) = left, right
    rows = l_hi.shape[0]
    both = dot_n(jnp.concatenate([l_hi, l_lo], axis=0), r_hi)
    return both[:rows] + both[rows:] + dot_n(l_hi, r_lo)


def pick(index, values):
    result = f32(values[0])
    for i in range(1, len(values)):
        result = jnp.where(index == i, f32(values[i]), result)
    return result


def node_angle(node, nodes_all):
    return np.float32(2.0 * math.pi) * (np.float32(node) + np.float32(0.5)) / np.float32(nodes_all)


def terms_kernel(dims, *refs):
    panel_devs, blk_dev, direct = dims
    col, row, dest, fcol, frank, ftgt, res_hbm, tiles_hbm, fr_hbm = refs[:9]
    n_out = panel_devs if direct else 1
    outs = refs[9 : 9 + n_out]
    res, tiles, fright, vec, terms, skel, acc, facc, sems = refs[9 + n_out :]
    tile_count = tiles.shape[0]
    far_count, _, rank, size = fright.shape
    node_dev = res.shape[0]
    chunk = TILE_CHUNK

    res_copy = pltpu.make_async_copy(res_hbm, res, sems.at[0])
    res_copy.start()
    tile_copies = []
    for i in range(tile_count // chunk):
        part = pl.ds(i * chunk, chunk)
        copy = pltpu.make_async_copy(tiles_hbm.at[part], tiles.at[part], sems.at[2 + i])
        copy.start()
        tile_copies.append(copy)
    far_copy = pltpu.make_async_copy(fr_hbm, fright, sems.at[1])
    far_copy.start()

    zero = jnp.zeros(acc.shape[1:], f32)
    for b in range(acc.shape[0]):
        acc[b] = zero
    for d in range(facc.shape[0]):
        facc[d] = zero

    here = lax.axis_index("panels")

    def slot_of(owner):
        if direct:
            owner = owner - here
            owner = jnp.where(owner < 0, owner + panel_devs, owner)
        return owner

    res_copy.wait()
    for b in range(blk_dev):
        lanes = slice(b * size, (b + 1) * size)
        re = jnp.concatenate([res[k, 0, :, lanes] for k in range(node_dev)], axis=0)
        im = jnp.concatenate([res[k, 1, :, lanes] for k in range(node_dev)], axis=0)
        upper = jnp.concatenate([re, -im], axis=1)
        lower = jnp.concatenate([im, re], axis=1)
        vec[b] = jnp.concatenate([upper, lower], axis=0).astype(bf16)

    rows = vec.shape[1]
    for i, copy in enumerate(tile_copies):
        copy.wait()
        for t in range(i * chunk, (i + 1) * chunk):
            tile = jnp.concatenate([tiles[t, 0], tiles[t, 1]], axis=1)
            terms[t] = dot_t(vec[col[t]], tile)
    for t in range(tile_count):
        target = slot_of(dest[t]) * blk_dev + row[t]
        acc[target] = acc[target] + terms[t]

    far_copy.wait()
    group = LANES // rank
    sources = vec[...].reshape(blk_dev * rows, 2 * size)
    for g in range(far_count // group):
        mats = [
            jnp.concatenate([fright[f, 0], fright[f, 1]], axis=1)
            for f in range(g * group, (g + 1) * group)
        ]
        skel[g] = dot_t(sources, jnp.concatenate(mats, axis=0)).reshape(blk_dev, rows, LANES)
    lane = lax.broadcasted_iota(jnp.int32, (rows, LANES), 1)
    for f in range(far_count):
        target = ftgt[f]
        owner = target // blk_dev
        place = (target - owner * blk_dev) * rank
        held = skel[f // group, fcol[f]]
        moved = pltpu.roll(held, lax.rem(place - (f % group) * rank + LANES, LANES), 1)
        kept = (lane >= place) & (lane < place + frank[f])
        slot = slot_of(owner)
        facc[slot] = facc[slot] + jnp.where(kept, moved, 0.0)

    near_rows = blk_dev * rows
    for d in range(panel_devs):
        out = outs[d] if direct else outs[0].at[d]
        for b in range(blk_dev):
            out[b * rows : (b + 1) * rows, :] = acc[d * blk_dev + b]
        out[near_rows:, :] = facc[d]


def product_kernel(dims, *refs):
    n_parts, node_devs, nodes_all = dims
    parts = refs[:n_parts]
    left, res, contour, out = refs[n_parts:]
    node_dev, _, rhs_dev, _ = res.shape
    blk_dev, _, rank, size = left.shape
    rows = 2 * node_dev * rhs_dev
    half = rows // 2

    total = parts[0][...]
    for part in parts[1:]:
        total = total + part[...]
    near = total[: blk_dev * rows]
    summed = total[blk_dev * rows :]
    re, im = summed[:half], summed[half:]
    upper = jnp.concatenate([re, -im], axis=1)
    lower = jnp.concatenate([im, re], axis=1)
    whole = jnp.concatenate([upper, lower], axis=0)
    lane = lax.broadcasted_iota(jnp.int32, whole.shape, 1)
    block = lax.rem(lane, LANES) // rank
    picked = [jnp.where(block == b, whole, 0.0) for b in range(blk_dev)]
    mats = left[...]
    stacked = jnp.concatenate(
        [mats[:, 0].reshape(blk_dev * rank, size), mats[:, 1].reshape(blk_dev * rank, size)], axis=0
    )
    applied = near + dot_n(jnp.concatenate(picked, axis=0).astype(bf16), stacked)

    here = lax.axis_index("nodes")
    for k in range(node_dev):
        cosines, sines = [], []
        for x in range(node_devs):
            angle = node_angle(x * node_dev + k, nodes_all)
            cosines.append(float(np.cos(angle)))
            sines.append(float(np.sin(angle)))
        shift_re = contour[0] + contour[2] * pick(here, cosines)
        shift_im = contour[1] + contour[2] * pick(here, sines)
        for b in range(blk_dev):
            lanes = slice(b * size, (b + 1) * size)
            top = b * rows + k * rhs_dev
            r_re, r_im = res[k, 0, :, lanes], res[k, 1, :, lanes]
            out[k, 0, :, lanes] = applied[top : top + rhs_dev] - (shift_re * r_re - shift_im * r_im)
            top = top + half
            out[k, 1, :, lanes] = applied[top : top + rhs_dev] - (shift_re * r_im + shift_im * r_re)


def side_by_side(pair, row, count):
    return jnp.concatenate([pair[row : row + count], pair[row + count : row + 2 * count]], axis=1)


def turned(pair, row, count):
    return jnp.concatenate([-pair[row + count : row + 2 * count], pair[row : row + count]], axis=1)


def ahead_kernel(dims, *refs):
    node_devs, nodes_all = dims
    it = iter(refs)
    res = [(next(it), next(it)) for _ in range(node_devs)]
    iterate = [next(it) for _ in range(node_devs)]
    probe_own, probe_other, contour, res_hi, res_lo, mixed, message = it
    node_dev, _, rhs_dev, width = res[0][0].shape
    cols = 2 * rhs_dev
    here = lax.axis_index("nodes")
    core = lax.axis_index("rhs")

    for s in range(node_devs):
        own, other = res[s]
        for k in range(node_dev):
            for c in range(2):
                both = jnp.concatenate([own[k, c], other[k, c]], axis=0)
                top = ((s * node_dev + k) * 2 + c) * cols
                high, low = split(both)
                res_hi[top : top + cols, :] = high
                res_lo[top : top + cols, :] = low

    scale = contour[2] / nodes_all
    for p in range(MOM_DEV):
        sum_re = jnp.zeros((rhs_dev, width), f32)
        sum_im = jnp.zeros((rhs_dev, width), f32)
        for s in range(node_devs):
            for k in range(node_dev):
                w_re, w_im = node_weight(here, scale, node_devs, node_dev, nodes_all, p, s, k)
                i_re, i_im = iterate[s][k, 0], iterate[s][k, 1]
                sum_re = sum_re + (w_re * i_re - w_im * i_im)
                sum_im = sum_im + (w_re * i_im + w_im * i_re)
        mixed[p, 0] = sum_re
        mixed[p, 1] = sum_im

    first = core == 0
    probe = []
    for c in range(2):
        own, other = probe_own[c], probe_other[c]
        top = jnp.where(first, own, other)
        bottom = jnp.where(first, other, own)
        probe.append(jnp.concatenate([top, bottom], axis=0))
    probe = split(jnp.concatenate(probe, axis=1))
    highs, lows = [], []
    for k in range(node_dev):
        top = k * 2 * cols
        for held, rows in ((res_hi, highs), (res_lo, lows)):
            here_rows = held[: node_dev * 2 * cols, :]
            rows.append(side_by_side(here_rows, top, cols))
            rows.append(-turned(here_rows, top, cols))
    right = (jnp.concatenate(highs, axis=0), jnp.concatenate(lows, axis=0))
    probe_res = dot3_t(probe, right)
    rows = []
    for p in range(MOM_DEV):
        rows.append(jnp.concatenate([mixed[p, 0], mixed[p, 1]], axis=1))
        rows.append(jnp.concatenate([mixed[p, 1], -mixed[p, 0]], axis=1))
    probe_mix = dot3_t(split(jnp.concatenate(rows, axis=0)), probe)

    message[0:rhs_dev, :] = jnp.zeros((rhs_dev, LANES), f32)
    pieces = [jnp.zeros((rhs_dev, LANES // 2), f32)]
    for q in range(2 * MOM_DEV):
        pieces.append(probe_mix[q * rhs_dev : (q + 1) * rhs_dev])
    message[rhs_dev : 2 * rhs_dev, :] = jnp.concatenate(pieces, axis=1)
    message[2 * rhs_dev :, :] = jnp.concatenate([probe_res[:rhs_dev], probe_res[rhs_dev:]], axis=1)


def node_weight(here, scale, node_devs, node_dev, nodes_all, p, s, k):
    cosines, sines = [], []
    for x in range(node_devs):
        node = (x - s) % node_devs * node_dev + k
        power = x * MOM_DEV + p
        angle = np.float32(power + 1) * node_angle(node, nodes_all)
        cosines.append(float(np.cos(angle)))
        sines.append(float(np.sin(angle)))
    return scale * pick(here, cosines), scale * pick(here, sines)


def gram_kernel(own, other, res_hi, res_lo, ahead, message, prod_hi, prod_lo):
    node_dev, _, rhs_dev, _ = own.shape
    cols = 2 * rhs_dev
    for k in range(node_dev):
        for c in range(2):
            high, low = split(jnp.concatenate([own[k, c], other[k, c]], axis=0))
            top = (k * 2 + c) * cols
            prod_hi[top : top + cols, :] = high
            prod_lo[top : top + cols, :] = low
    sums = []
    for k in range(node_dev):
        top = k * 2 * cols
        left, right = [], []
        for p_ref, r_ref in ((prod_hi, res_hi), (prod_lo, res_lo)):
            product, source = p_ref[...], r_ref[: node_dev * 2 * cols, :]
            plain = side_by_side(product, top, cols)
            left.append(jnp.concatenate([plain, side_by_side(source, top, cols)], axis=0))
            right.append(jnp.concatenate([plain, turned(product, top, cols)], axis=0))
        sums.append(dot3_t(tuple(left), tuple(right)))
    gram = jnp.concatenate(sums, axis=1)
    half = LANES // 2
    message[0:rhs_dev, :] = jnp.concatenate([gram[:rhs_dev], gram[rhs_dev:cols]], axis=1)
    message[rhs_dev:cols, :half] = gram[cols : cols + rhs_dev]
    message[rhs_dev:cols, half:] = ahead[rhs_dev:cols, half:]
    message[cols:, :] = ahead[cols:, :]


def finish_kernel(dims, *refs):
    n_parts, node_devs, nodes_all, scale_factor = dims
    it = iter(refs)
    parts = [[next(it) for _ in range(n_parts)] for _ in range(node_devs)]
    res, prod_hi, prod_lo, res_hi, res_lo, mixed, contour, next_out, mom_out, hankel_out = it
    node_dev, _, rhs_dev, width = res.shape
    cols = 2 * rhs_dev
    half = LANES // 2
    here = lax.axis_index("nodes")

    sums = []
    for group in parts:
        total = group[0][...]
        for part in group[1:]:
            total = total + part[...]
        sums.append(total)
    if node_devs % 2:
        sums.append(sums[0])

    shape = (rhs_dev, LANES)
    lane = lax.broadcasted_iota(jnp.int32, shape, 1)
    low_half = lane < half
    base = (lane // (2 * cols)) * (2 * cols)
    spot = lax.rem(lane, cols)
    real_lane = lax.rem(lane, 2 * cols) < cols
    swapped = jnp.where(real_lane, lane + cols, lane - cols)
    sign = jnp.where(real_lane, -1.0, 1.0)

    def gathered(value, index):
        return jnp.take_along_axis(value, index, axis=1, mode="promise_in_bounds")

    solved, probe_res = [], []
    for g in range(len(sums) // 2):
        s0, s1 = sums[2 * g], sums[2 * g + 1]
        r0, r1 = pltpu.roll(s0, half, 1), pltpu.roll(s1, half, 1)
        v0, v1, v2 = slice(0, rhs_dev), slice(rhs_dev, cols), slice(cols, cols + rhs_dev)
        block = [
            jnp.where(low_half, s0[v0], r1[v0]),
            jnp.where(low_half, r0[v0], s1[v0]),
            jnp.where(low_half, s0[v1], r1[v1]),
        ]
        probe_res.append(
            jnp.concatenate(
                [jnp.where(low_half, s0[v2], r1[v2]), jnp.where(low_half, r0[v2], s1[v2])], axis=0
            )
        )
        inverse_diag = jnp.ones(shape, f32)
        for j in range(cols):
            at, r = divmod(j, rhs_dev)
            line = block[at][r : r + 1]
            crossed = (gathered(block[at], swapped) * sign)[r : r + 1]
            col_re = [gathered(b, base + j) for b in block[at:]]
            col_im = [gathered(b, base + cols + j) for b in block[at:]]
            inverse = 1.0 / col_re[0][r : r + 1]
            kept = (spot != j)[:1]
            scaled = jnp.where(kept, inverse, 0.0)
            f1, f2 = line * scaled, crossed * scaled
            for i in range(at, 3):
                block[i] = block[i] - (col_re[i - at] * f1 + col_im[i - at] * f2)
            inverse_diag = jnp.where(spot == j, inverse, inverse_diag)
        solved.append(block[2] * inverse_diag)

    coef = solved[0]
    cross = gathered(coef, swapped)
    plain = jnp.where(real_lane, coef, -coef)
    node_of = lane // (2 * cols)
    rows = []
    for k in range(node_dev):
        rows.append(jnp.where(node_of == k, plain, 0.0))
        rows.append(jnp.where(node_of == k, cross, 0.0))
    used = node_dev * 2 * cols
    left = split(jnp.concatenate(rows, axis=0)[:, :used])
    change = dot3_n(left, (prod_hi[...], prod_lo[...]))
    for k in range(node_dev):
        for c in range(2):
            top = (k * 2 + c) * rhs_dev
            next_out[k, c] = res[k, c] - change[top : top + rhs_dev]

    scale = contour[2] / nodes_all
    weighted = []
    for g, coef in enumerate(solved):
        cross = gathered(coef, swapped)
        rows = []
        for p in range(MOM_DEV):
            w_re = jnp.zeros(shape, f32)
            w_im = jnp.zeros(shape, f32)
            for i in range(2):
                s = 2 * g + i
                if s >= node_devs:
                    continue
                for k in range(node_dev):
                    n_re, n_im = node_weight(here, scale, node_devs, node_dev, nodes_all, p, s, k)
                    mine = node_of == i * node_dev + k
                    w_re = jnp.where(mine, n_re, w_re)
                    w_im = jnp.where(mine, n_im, w_im)
            rows.append(-sign * w_re * coef - w_im * cross)
            rows.append(-sign * w_im * coef + w_re * cross)
        weighted.append(jnp.concatenate(rows, axis=0))
    total = [mixed[p, c] for p in range(MOM_DEV) for c in range(2)]
    total = jnp.concatenate(total, axis=0)
    hankel = None
    for g, value in enumerate(weighted):
        depth = min(LANES, node_devs * used - g * LANES)
        left = split(value)
        span = slice(g * LANES, g * LANES + depth)
        cut = tuple(part[:, :depth] for part in left)
        total = total + dot3_n(cut, (res_hi[span, :], res_lo[span, :]))
        term = dot3_t(left, split(probe_res[g]))
        hankel = term if hankel is None else hankel + term
    for p in range(MOM_DEV):
        for c in range(2):
            q = 2 * p + c
            top = q * rhs_dev
            mom_out[p, c] = total[top : top + rhs_dev]
            start = half + q * cols
            moved = pltpu.roll(sums[0][rhs_dev:cols], LANES - start, 1)[:, :cols]
            hankel_out[p, c] = (hankel[top : top + rhs_dev] + moved) * scale_factor


def call(kernel, out_shape, args, in_specs=None, scratch=(), cost=None):
    multiple = isinstance(out_shape, (list, tuple))
    return pl.pallas_call(
        kernel,
        out_shape=out_shape,
        in_specs=[VMEM] * len(args) if in_specs is None else in_specs,
        out_specs=[VMEM] * len(out_shape) if multiple else VMEM,
        scratch_shapes=list(scratch),
        compiler_params=PARAMS,
        cost_estimate=cost,
    )(*args)


def struct(shape, dtype=f32):
    return jax.ShapeDtypeStruct(shape, dtype)


def per_device(
    residual,
    iterate,
    probe,
    contour,
    near_tiles,
    near_col,
    near_row,
    near_dest,
    far_right,
    far_col,
    far_rank,
    far_target,
    far_left,
):
    node_dev, _, rhs_dev, rows_dev = residual.shape
    tile_count, _, size, _ = near_tiles.shape
    far_count, _, rank, _ = far_right.shape
    blk_dev = rows_dev // size
    panel_devs = lax.axis_size("panels")
    node_devs = lax.axis_size("nodes")
    rhs_devs = lax.axis_size("rhs")
    nodes_all = node_dev * node_devs
    vec_rows = 2 * node_dev * rhs_dev
    cols = 2 * rhs_dev
    direct = panel_devs * node_devs <= DIRECT_PEERS

    def moved(value, panel_shift, node_shift, rhs_shift):
        axes = [("panels", panel_shift, panel_devs), ("nodes", node_shift, node_devs), ("rhs", rhs_shift, rhs_devs)]
        axes = [a for a in axes if a[1]]
        if not axes:
            return value
        names = tuple(a[0] for a in axes)
        sizes = tuple(a[2] for a in axes)
        pairs = []
        for index in np.ndindex(*sizes):
            target = tuple((i + a[1]) % a[2] for i, a in zip(index, axes))
            pairs.append((int(np.ravel_multi_index(index, sizes)), int(np.ravel_multi_index(target, sizes))))
        return lax.ppermute(value, names, pairs)

    part_rows = blk_dev * vec_rows + vec_rows
    if direct:
        out_shape = [struct((part_rows, LANES)) for _ in range(panel_devs)]
    else:
        out_shape = [struct((panel_devs, part_rows, LANES))]
    terms = call(
        functools.partial(terms_kernel, (panel_devs, blk_dev, direct)),
        out_shape,
        (
            near_col,
            near_row,
            near_dest.reshape(tile_count),
            far_col,
            far_rank,
            far_target,
            residual,
            near_tiles,
            far_right,
        ),
        in_specs=[SMEM] * 6 + [ANY] * 3,
        scratch=[
            pltpu.VMEM(residual.shape, f32),
            pltpu.VMEM(near_tiles.shape, bf16),
            pltpu.VMEM(far_right.shape, bf16),
            pltpu.VMEM((blk_dev, vec_rows, 2 * size), bf16),
            pltpu.VMEM((tile_count, vec_rows, size), f32),
            pltpu.VMEM((far_count * rank // LANES, blk_dev, vec_rows, LANES), f32),
            pltpu.VMEM((panel_devs * blk_dev, vec_rows, size), f32),
            pltpu.VMEM((panel_devs, vec_rows, LANES), f32),
            pltpu.SemaphoreType.DMA((2 + tile_count // TILE_CHUNK,)),
        ],
    )
    if direct:
        parts = [moved(terms[d], d, 0, 0) for d in range(panel_devs)]
    else:
        parts = [lax.psum_scatter(terms[0], "panels", scatter_dimension=0)]

    sources = []
    for s in range(node_devs):
        sources.extend([moved(residual, 0, s, 0), moved(residual, 0, s, 1)])
    iterates = [moved(iterate, 0, s, 0) for s in range(node_devs)]
    span = 2 * node_dev * cols
    res_hi, res_lo, mixed, ahead = call(
        functools.partial(ahead_kernel, (node_devs, nodes_all)),
        [
            struct((node_devs * span, rows_dev), bf16),
            struct((node_devs * span, rows_dev), bf16),
            struct((MOM_DEV, 2, rhs_dev, rows_dev)),
            struct((3 * rhs_dev, LANES)),
        ],
        (*sources, *iterates, probe, moved(probe, 0, 0, 1), contour),
        in_specs=[VMEM] * (3 * node_devs + 2) + [SMEM],
    )

    product = call(
        functools.partial(product_kernel, (len(parts), node_devs, nodes_all)),
        struct(residual.shape),
        (*parts, far_left.transpose(0, 1, 3, 2), residual, contour),
        in_specs=[VMEM] * (len(parts) + 2) + [SMEM],
    )
    message, prod_hi, prod_lo = call(
        gram_kernel,
        [struct((3 * rhs_dev, LANES)), struct((span, rows_dev), bf16), struct((span, rows_dev), bf16)],
        (product, moved(product, 0, 0, 1), res_hi, res_lo, ahead),
    )

    if direct:
        sums = [moved(message, d, s, 0) for s in range(node_devs) for d in range(panel_devs)]
    else:
        summed = lax.psum(message, "panels")
        sums = [moved(summed, 0, s, 0) for s in range(node_devs)]
    n_parts = len(sums) // node_devs
    scale_factor = 1.0 / math.sqrt(rows_dev * panel_devs)
    residual_next, moments, hankel = call(
        functools.partial(finish_kernel, (n_parts, node_devs, nodes_all, scale_factor)),
        [
            struct(residual.shape),
            struct((MOM_DEV, 2, rhs_dev, rows_dev)),
            struct((MOM_DEV, 2, rhs_dev, cols)),
        ],
        (*sums, residual, prod_hi, prod_lo, res_hi, res_lo, mixed, contour),
        in_specs=[VMEM] * (len(sums) + 6) + [SMEM],
    )
    return residual_next, moments, hankel.transpose(0, 1, 3, 2)


def solution(mesh):
    return jax.shard_map(
        per_device,
        mesh=mesh,
        in_specs=(
            P(("groups", "nodes"), None, "rhs", "panels"),
            P(("groups", "nodes"), None, "rhs", "panels"),
            P("groups", "rhs", "panels"),
            P("groups"),
            P(("groups", "panels"), None, None, None),
            P(("groups", "panels")),
            P(("groups", "panels")),
            P(("groups", "panels"), None),
            P(("groups", "panels"), None, None, None),
            P(("groups", "panels")),
            P(("groups", "panels")),
            P(("groups", "panels")),
            P(("groups", "panels"), None, None, None),
        ),
        out_specs=(
            P(("groups", "nodes"), None, "rhs", "panels"),
            P(("groups", "nodes"), None, "rhs", "panels"),
            P(("groups", "nodes"), None, None, "rhs"),
        ),
        check_vma=False,
    )
```

```python
import functools
import math

import jax
import jax.numpy as jnp
import numpy as np
from jax import lax
from jax.experimental import pallas as pl
from jax.experimental.pallas import tpu as pltpu
from jax.sharding import PartitionSpec as P

MOM_DEV = 2
LANES = 128
TILE_CHUNK = 4

f32 = jnp.float32
bf16 = jnp.bfloat16

PARAMS = pltpu.CompilerParams(vmem_limit_bytes=40 * 1024 * 1024)
VMEM = pl.BlockSpec(memory_space=pltpu.VMEM)
HBM = pl.BlockSpec(memory_space=pltpu.HBM)


def dot_t(left, right):
    return lax.dot_general(left, right, (((1,), (1,)), ((), ())), preferred_element_type=f32)


def dot_n(left, right):
    return lax.dot_general(left, right, (((1,), (0,)), ((), ())), preferred_element_type=f32)


def split(value):
    high = value.astype(bf16)
    return high, (value - high.astype(f32)).astype(bf16)


def dot3_t(left, right):
    (l_hi, l_lo), (r_hi, r_lo) = left, right
    rows = l_hi.shape[0]
    both = dot_t(jnp.concatenate([l_hi, l_lo], axis=0), r_hi)
    return both[:rows] + both[rows:] + dot_t(l_hi, r_lo)


def dot3_n(left, right):
    (l_hi, l_lo), (r_hi, r_lo) = left, right
    rows = l_hi.shape[0]
    both = dot_n(jnp.concatenate([l_hi, l_lo], axis=0), r_hi)
    return both[:rows] + both[rows:] + dot_n(l_hi, r_lo)


def pick(index, values):
    result = f32(values[0])
    for i in range(1, len(values)):
        result = jnp.where(index == i, f32(values[i]), result)
    return result


def node_angle(node, nodes_all):
    return np.float32(2.0 * math.pi) * (np.float32(node) + np.float32(0.5)) / np.float32(nodes_all)


def terms_kernel(dims, *refs):
    panel_devs, blk_dev = dims
    indices, (contour_hbm, res_hbm, iter_hbm, probe_hbm, tiles_hbm, fr_hbm) = refs[:6], refs[6:12]
    out, pack, consts = refs[12:15]
    held, (contour, tiles, fright, vec, terms, skel, acc, facc, sems) = refs[15:21], refs[21:]
    tile_count = tiles.shape[0]
    far_count, _, rank, size = fright.shape
    res_rows, iter_rows = res_hbm.shape[0], iter_hbm.shape[0]
    node_dev = res_rows // 2
    chunk = TILE_CHUNK

    copies = []

    def start(source, target):
        copy = pltpu.make_async_copy(source, target, sems.at[len(copies)])
        copy.start()
        copies.append(copy)
        return copy

    res_copy = start(res_hbm, pack.at[pl.ds(0, res_rows)])
    small = [start(source, target) for source, target in zip(indices, held)]
    small.append(start(contour_hbm, contour))
    tile_copies = []
    for i in range(tile_count // chunk):
        part = pl.ds(i * chunk, chunk)
        tile_copies.append(start(tiles_hbm.at[part], tiles.at[part]))
    far_copy = start(fr_hbm, fright)
    rest = [
        start(iter_hbm, pack.at[pl.ds(res_rows, iter_rows)]),
        start(probe_hbm, pack.at[pl.ds(res_rows + iter_rows, 2)]),
    ]
    col, row, dest, fcol, frank, ftgt = held

    zero = jnp.zeros(acc.shape[1:], f32)
    for b in range(acc.shape[0]):
        acc[b] = zero
    for d in range(facc.shape[0]):
        facc[d] = zero

    res_copy.wait()
    for b in range(blk_dev):
        lanes = slice(b * size, (b + 1) * size)
        re = jnp.concatenate([pack[2 * k, :, lanes] for k in range(node_dev)], axis=0)
        im = jnp.concatenate([pack[2 * k + 1, :, lanes] for k in range(node_dev)], axis=0)
        upper = jnp.concatenate([re, -im], axis=1)
        lower = jnp.concatenate([im, re], axis=1)
        vec[b] = jnp.concatenate([upper, lower], axis=0).astype(bf16)

    for copy in small:
        copy.wait()
    for i in range(consts.shape[0]):
        consts[i : i + 1, :] = jnp.full((1, LANES), contour[min(i, 2)], f32)

    rows = vec.shape[1]
    for i, copy in enumerate(tile_copies):
        copy.wait()
        for t in range(i * chunk, (i + 1) * chunk):
            tile = jnp.concatenate([tiles[t, 0], tiles[t, 1]], axis=1)
            terms[t] = dot_t(vec[col[t]], tile)
    far_copy.wait()
    group = LANES // rank
    sources = vec[...].reshape(blk_dev * rows, 2 * size)
    for g in range(far_count // group):
        mats = [
            jnp.concatenate([fright[f, 0], fright[f, 1]], axis=1)
            for f in range(g * group, (g + 1) * group)
        ]
        skel[g] = dot_t(sources, jnp.concatenate(mats, axis=0)).reshape(blk_dev, rows, LANES)

    for t in range(tile_count):
        target = dest[t] * blk_dev + row[t]
        acc[target] = acc[target] + terms[t]
    lane = lax.broadcasted_iota(jnp.int32, (rows, LANES), 1)
    for f in range(far_count):
        target = ftgt[f]
        owner = target // blk_dev
        place = (target - owner * blk_dev) * rank
        moved = pltpu.roll(
            skel[f // group, fcol[f]], lax.rem(place - (f % group) * rank + LANES, LANES), 1
        )
        kept = (lane >= place) & (lane < place + frank[f])
        facc[owner] = facc[owner] + jnp.where(kept, moved, 0.0)

    near_rows = blk_dev * rows
    for d in range(panel_devs):
        for b in range(blk_dev):
            out[d, b * rows : (b + 1) * rows, :] = acc[d * blk_dev + b]
        out[d, near_rows:, :] = facc[d]
    for copy in rest:
        copy.wait()


def product_kernel(dims, *refs):
    node_devs, nodes_all = dims
    parts, left, pack, contour, out = refs
    node_dev, _, rhs_dev, _ = out.shape
    blk_dev, _, rank, size = left.shape
    rows = 2 * node_dev * rhs_dev
    half = rows // 2

    total = parts[0]
    for d in range(1, parts.shape[0]):
        total = total + parts[d]
    near = total[: blk_dev * rows]
    summed = total[blk_dev * rows :]
    re, im = summed[:half], summed[half:]
    upper = jnp.concatenate([re, -im], axis=1)
    lower = jnp.concatenate([im, re], axis=1)
    whole = jnp.concatenate([upper, lower], axis=0)
    lane = lax.broadcasted_iota(jnp.int32, whole.shape, 1)
    block = lax.rem(lane, LANES) // rank
    picked = [jnp.where(block == b, whole, 0.0) for b in range(blk_dev)]
    mats = left[...]
    stacked = jnp.concatenate(
        [mats[:, 0].reshape(blk_dev * rank, size), mats[:, 1].reshape(blk_dev * rank, size)], axis=0
    )
    applied = near + dot_n(jnp.concatenate(picked, axis=0).astype(bf16), stacked)

    here = lax.axis_index("nodes")
    for k in range(node_dev):
        cosines, sines = [], []
        for x in range(node_devs):
            angle = node_angle(x * node_dev + k, nodes_all)
            cosines.append(float(np.cos(angle)))
            sines.append(float(np.sin(angle)))
        shift_re = contour[0:1, :] + contour[2:3, :] * pick(here, cosines)
        shift_im = contour[1:2, :] + contour[2:3, :] * pick(here, sines)
        for b in range(blk_dev):
            lanes = slice(b * size, (b + 1) * size)
            top = b * rows + k * rhs_dev
            r_re, r_im = pack[2 * k, :, lanes], pack[2 * k + 1, :, lanes]
            out[k, 0, :, lanes] = applied[top : top + rhs_dev] - (shift_re * r_re - shift_im * r_im)
            top = top + half
            out[k, 1, :, lanes] = applied[top : top + rhs_dev] - (shift_re * r_im + shift_im * r_re)


def side_by_side(pair, row, count):
    return jnp.concatenate([pair[row : row + count], pair[row + count : row + 2 * count]], axis=1)


def turned(pair, row, count):
    return jnp.concatenate([-pair[row + count : row + 2 * count], pair[row : row + count]], axis=1)


def joined(own, other, row):
    return jnp.concatenate([own[row], other[row]], axis=0)


def ahead_kernel(own, other, res_hi, res_lo, message):
    _, rhs_dev, _ = own.shape
    cols = 2 * rhs_dev
    res_rows = res_hi.shape[0] // cols
    node_dev = res_rows // 2

    for i in range(res_rows):
        high, low = split(joined(own, other, i))
        res_hi[i * cols : (i + 1) * cols, :] = high
        res_lo[i * cols : (i + 1) * cols, :] = low

    first = lax.axis_index("rhs") == 0
    probe = []
    for c in range(2):
        mine, theirs = own[2 * res_rows + c], other[2 * res_rows + c]
        top = jnp.where(first, mine, theirs)
        bottom = jnp.where(first, theirs, mine)
        probe.append(jnp.concatenate([top, bottom], axis=0))
    probe = split(jnp.concatenate(probe, axis=1))
    pair = []
    for held in (res_hi[...], res_lo[...]):
        rows = []
        for k in range(node_dev):
            rows.append(side_by_side(held, k * 2 * cols, cols))
            rows.append(-turned(held, k * 2 * cols, cols))
        pair.append(jnp.concatenate(rows, axis=0))
    probe_res = dot3_t(probe, tuple(pair))
    rows = []
    for k in range(node_dev):
        i_re, i_im = own[res_rows + 2 * k], own[res_rows + 2 * k + 1]
        rows.append(jnp.concatenate([i_re, i_im], axis=1))
        rows.append(jnp.concatenate([i_im, -i_re], axis=1))
    probe_iter = dot3_t(split(jnp.concatenate(rows, axis=0)), probe)

    message[0:rhs_dev, :] = jnp.zeros((rhs_dev, LANES), f32)
    pieces = [jnp.zeros((rhs_dev, LANES // 2), f32)]
    for q in range(res_rows):
        pieces.append(probe_iter[q * rhs_dev : (q + 1) * rhs_dev])
    message[rhs_dev : 2 * rhs_dev, :] = jnp.concatenate(pieces, axis=1)
    message[2 * rhs_dev :, :] = jnp.concatenate([probe_res[:rhs_dev], probe_res[rhs_dev:]], axis=1)


def node_weight(here, scale, node_devs, node_dev, nodes_all, p, s, k):
    cosines, sines = [], []
    for x in range(node_devs):
        node = (x - s) % node_devs * node_dev + k
        power = x * MOM_DEV + p
        angle = np.float32(power + 1) * node_angle(node, nodes_all)
        cosines.append(float(np.cos(angle)))
        sines.append(float(np.sin(angle)))
    return scale * pick(here, cosines), scale * pick(here, sines)


def gram_kernel(own, other, res_hi, res_lo, ahead, message, prod_hi, prod_lo):
    node_dev, _, rhs_dev, _ = own.shape
    cols = 2 * rhs_dev
    for k in range(node_dev):
        for c in range(2):
            high, low = split(jnp.concatenate([own[k, c], other[k, c]], axis=0))
            top = (k * 2 + c) * cols
            prod_hi[top : top + cols, :] = high
            prod_lo[top : top + cols, :] = low
    sums = []
    for k in range(node_dev):
        top = k * 2 * cols
        left, right = [], []
        for p_ref, r_ref in ((prod_hi, res_hi), (prod_lo, res_lo)):
            product, source = p_ref[...], r_ref[: node_dev * 2 * cols, :]
            plain = side_by_side(product, top, cols)
            left.append(jnp.concatenate([plain, side_by_side(source, top, cols)], axis=0))
            right.append(jnp.concatenate([plain, turned(product, top, cols)], axis=0))
        sums.append(dot3_t(tuple(left), tuple(right)))
    gram = jnp.concatenate(sums, axis=1)
    half = LANES // 2
    top = jnp.concatenate([gram[:rhs_dev], gram[rhs_dev:cols]], axis=1)
    middle = jnp.concatenate([gram[cols : cols + rhs_dev], ahead[rhs_dev:cols, half:]], axis=1)
    bottom = ahead[cols:, :]
    for i in range(message.shape[0]):
        message[i, 0:rhs_dev, :] = top
        message[i, rhs_dev:cols, :] = middle
        message[i, cols:, :] = bottom


def finish_kernel(dims, *refs):
    node_devs, nodes_all, scale_factor = dims
    it = iter(refs)
    parts = next(it)
    packs = [(next(it), next(it)) for _ in range(node_devs)]
    prod_hi, prod_lo, res_hi, res_lo, contour, next_out, mom_out, hankel_out = it
    node_dev, _, rhs_dev, width = next_out.shape
    cols = 2 * rhs_dev
    half = LANES // 2
    res_rows = 2 * node_dev
    here = lax.axis_index("nodes")

    sums = []
    for s in range(node_devs):
        group = here - s
        group = jnp.where(group < 0, group + node_devs, group)
        total = parts[group]
        for d in range(1, parts.shape[0] // node_devs):
            total = total + parts[d * node_devs + group]
        sums.append(total)
    if node_devs % 2:
        sums.append(sums[0])

    shape = (rhs_dev, LANES)
    lane = lax.broadcasted_iota(jnp.int32, shape, 1)
    low_half = lane < half
    base = (lane // (2 * cols)) * (2 * cols)
    spot = lax.rem(lane, cols)
    real_lane = lax.rem(lane, 2 * cols) < cols
    swapped = jnp.where(real_lane, lane + cols, lane - cols)
    sign = jnp.where(real_lane, -1.0, 1.0)

    def gathered(value, index):
        return jnp.take_along_axis(value, index, axis=1, mode="promise_in_bounds")

    solved, probe_res = [], []
    for g in range(len(sums) // 2):
        s0, s1 = sums[2 * g], sums[2 * g + 1]
        r0, r1 = pltpu.roll(s0, half, 1), pltpu.roll(s1, half, 1)
        v0, v1, v2 = slice(0, rhs_dev), slice(rhs_dev, cols), slice(cols, cols + rhs_dev)
        block = [
            jnp.where(low_half, s0[v0], r1[v0]),
            jnp.where(low_half, r0[v0], s1[v0]),
            jnp.where(low_half, s0[v1], r1[v1]),
        ]
        probe_res.append(
            jnp.concatenate(
                [jnp.where(low_half, s0[v2], r1[v2]), jnp.where(low_half, r0[v2], s1[v2])], axis=0
            )
        )
        inverse_diag = jnp.ones(shape, f32)
        for j in range(cols):
            at, r = divmod(j, rhs_dev)
            line = block[at][r : r + 1]
            crossed = (gathered(block[at], swapped) * sign)[r : r + 1]
            col_re = [gathered(b, base + j) for b in block[at:]]
            col_im = [gathered(b, base + cols + j) for b in block[at:]]
            inverse = 1.0 / col_re[0][r : r + 1]
            kept = (spot != j)[:1]
            scaled = jnp.where(kept, inverse, 0.0)
            f1, f2 = line * scaled, crossed * scaled
            for i in range(at, 3):
                block[i] = block[i] - (col_re[i - at] * f1 + col_im[i - at] * f2)
            inverse_diag = jnp.where(spot == j, inverse, inverse_diag)
        solved.append(block[2] * inverse_diag)

    coef = solved[0]
    cross = gathered(coef, swapped)
    plain = jnp.where(real_lane, coef, -coef)
    node_of = lane // (2 * cols)
    rows = []
    for k in range(node_dev):
        rows.append(jnp.where(node_of == k, plain, 0.0))
        rows.append(jnp.where(node_of == k, cross, 0.0))
    used = node_dev * 2 * cols
    left = split(jnp.concatenate(rows, axis=0)[:, :used])
    change = dot3_n(left, (prod_hi[...], prod_lo[...]))
    for k in range(node_dev):
        for c in range(2):
            top = (k * 2 + c) * rhs_dev
            next_out[k, c] = packs[0][0][2 * k + c] - change[top : top + rhs_dev]

    scale = contour[2:3, :] / nodes_all
    weighted = []
    for g, coef in enumerate(solved):
        cross = gathered(coef, swapped)
        rows = []
        for p in range(MOM_DEV):
            w_re = jnp.zeros(shape, f32)
            w_im = jnp.zeros(shape, f32)
            for i in range(2):
                s = 2 * g + i
                if s >= node_devs:
                    continue
                for k in range(node_dev):
                    n_re, n_im = node_weight(here, scale, node_devs, node_dev, nodes_all, p, s, k)
                    mine = node_of == i * node_dev + k
                    w_re = jnp.where(mine, n_re, w_re)
                    w_im = jnp.where(mine, n_im, w_im)
            rows.append(-sign * w_re * coef - w_im * cross)
            rows.append(-sign * w_im * coef + w_re * cross)
        weighted.append(jnp.concatenate(rows, axis=0))
    hankel = None
    products = None
    for g, value in enumerate(weighted):
        depth = min(LANES, node_devs * used - g * LANES)
        left = split(value)
        cut = tuple(part[:, :depth] for part in left)
        highs, lows = [], []
        for i in range(depth // used):
            s = 2 * g + i
            if s == 0:
                highs.append(res_hi[...])
                lows.append(res_lo[...])
                continue
            for q in range(res_rows):
                high, low = split(joined(packs[s][0], packs[s][1], q))
                highs.append(high)
                lows.append(low)
        term = dot3_n(cut, (jnp.concatenate(highs, axis=0), jnp.concatenate(lows, axis=0)))
        products = term if products is None else products + term
        term = dot3_t(left, split(probe_res[g]))
        hankel = term if hankel is None else hankel + term

    wide = jnp.concatenate([scale] * (width // LANES), axis=1)
    for p in range(MOM_DEV):
        mom = [products[(2 * p + c) * rhs_dev : (2 * p + c + 1) * rhs_dev] for c in range(2)]
        han = [hankel[(2 * p + c) * rhs_dev : (2 * p + c + 1) * rhs_dev] for c in range(2)]
        for s in range(node_devs):
            for k in range(node_dev):
                w_re, w_im = node_weight(here, wide, node_devs, node_dev, nodes_all, p, s, k)
                i_re, i_im = packs[s][0][res_rows + 2 * k], packs[s][0][res_rows + 2 * k + 1]
                mom[0] = mom[0] + (w_re * i_re - w_im * i_im)
                mom[1] = mom[1] + (w_re * i_im + w_im * i_re)
                i_re, i_im = [
                    pltpu.roll(sums[s][rhs_dev:cols], half - (2 * k + c) * cols, 1)[:, :cols]
                    for c in range(2)
                ]
                w_re, w_im = w_re[:, :cols], w_im[:, :cols]
                han[0] = han[0] + (w_re * i_re - w_im * i_im)
                han[1] = han[1] + (w_re * i_im + w_im * i_re)
        for c in range(2):
            mom_out[p, c] = mom[c]
            hankel_out[p, c] = han[c] * scale_factor


def call(kernel, out_shape, args, in_specs=None, scratch=(), cost=None):
    multiple = isinstance(out_shape, (list, tuple))
    return pl.pallas_call(
        kernel,
        out_shape=out_shape,
        in_specs=[VMEM] * len(args) if in_specs is None else in_specs,
        out_specs=[VMEM] * len(out_shape) if multiple else VMEM,
        scratch_shapes=list(scratch),
        compiler_params=PARAMS,
        cost_estimate=cost,
    )(*args)


def struct(shape, dtype=f32):
    return jax.ShapeDtypeStruct(shape, dtype)


def per_device(
    residual,
    iterate,
    probe,
    contour,
    near_tiles,
    near_col,
    near_row,
    near_dest,
    far_right,
    far_col,
    far_rank,
    far_target,
    far_left,
):
    node_dev, _, rhs_dev, rows_dev = residual.shape
    tile_count, _, size, _ = near_tiles.shape
    far_count, _, rank, _ = far_right.shape
    blk_dev = rows_dev // size
    panel_devs = lax.axis_size("panels")
    node_devs = lax.axis_size("nodes")
    nodes_all = node_dev * node_devs
    vec_rows = 2 * node_dev * rhs_dev
    cols = 2 * rhs_dev
    res_rows = 2 * node_dev
    span = res_rows * cols

    part_rows = blk_dev * vec_rows + vec_rows
    copies = 6 + 1 + tile_count // TILE_CHUNK + 4
    pack_shape = (2 * res_rows + 2, rhs_dev, rows_dev)
    indices = (near_col, near_row, near_dest.reshape(tile_count), far_col, far_rank, far_target)
    terms, pack, consts = call(
        functools.partial(terms_kernel, (panel_devs, blk_dev)),
        [struct((panel_devs, part_rows, LANES)), struct(pack_shape), struct((8, LANES))],
        (
            *indices,
            contour,
            residual.reshape(res_rows, rhs_dev, rows_dev),
            iterate.reshape(res_rows, rhs_dev, rows_dev),
            probe,
            near_tiles,
            far_right,
        ),
        in_specs=[HBM] * 12,
        scratch=[
            *[pltpu.SMEM(index.shape, jnp.int32) for index in indices],
            pltpu.SMEM(contour.shape, f32),
            pltpu.VMEM(near_tiles.shape, bf16),
            pltpu.VMEM(far_right.shape, bf16),
            pltpu.VMEM((blk_dev, vec_rows, 2 * size), bf16),
            pltpu.VMEM((tile_count, vec_rows, size), f32),
            pltpu.VMEM((far_count * rank // LANES, blk_dev, vec_rows, LANES), f32),
            pltpu.VMEM((panel_devs * blk_dev, vec_rows, size), f32),
            pltpu.VMEM((panel_devs, vec_rows, LANES), f32),
            pltpu.SemaphoreType.DMA((copies,)),
        ],
    )

    swap = [(0, 1), (1, 0)]
    packs = []
    for s in range(node_devs):
        pairs = [(i, (i + s) % node_devs) for i in range(node_devs)]
        there = lax.ppermute(pack, "nodes", pairs) if s else pack
        packs.append((there, lax.ppermute(there, "rhs", swap)))

    parts = lax.all_to_all(terms, "panels", split_axis=0, concat_axis=0, tiled=True)
    product = call(
        functools.partial(product_kernel, (node_devs, nodes_all)),
        struct(residual.shape),
        (parts, far_left.transpose(0, 1, 3, 2), pack, consts),
    )
    res_hi, res_lo, ahead = call(
        ahead_kernel,
        [struct((span, rows_dev), bf16), struct((span, rows_dev), bf16), struct((3 * rhs_dev, LANES))],
        packs[0],
    )
    peers = panel_devs * node_devs
    message, prod_hi, prod_lo = call(
        gram_kernel,
        [
            struct((peers, 3 * rhs_dev, LANES)),
            struct((span, rows_dev), bf16),
            struct((span, rows_dev), bf16),
        ],
        (product, lax.ppermute(product, "rhs", swap), res_hi, res_lo, ahead),
    )
    sums = lax.all_to_all(message, ("panels", "nodes"), split_axis=0, concat_axis=0, tiled=True)
    scale_factor = 1.0 / math.sqrt(rows_dev * panel_devs)
    residual_next, moments, hankel = call(
        functools.partial(finish_kernel, (node_devs, nodes_all, scale_factor)),
        [
            struct(residual.shape),
            struct((MOM_DEV, 2, rhs_dev, rows_dev)),
            struct((MOM_DEV, 2, rhs_dev, cols)),
        ],
        (sums, *[p for pair in packs for p in pair], prod_hi, prod_lo, res_hi, res_lo, consts),
    )
    return residual_next, moments, hankel.transpose(0, 1, 3, 2)


def solution(mesh):
    return jax.shard_map(
        per_device,
        mesh=mesh,
        in_specs=(
            P(("groups", "nodes"), None, "rhs", "panels"),
            P(("groups", "nodes"), None, "rhs", "panels"),
            P("groups", "rhs", "panels"),
            P("groups"),
            P(("groups", "panels"), None, None, None),
            P(("groups", "panels")),
            P(("groups", "panels")),
            P(("groups", "panels"), None),
            P(("groups", "panels"), None, None, None),
            P(("groups", "panels")),
            P(("groups", "panels")),
            P(("groups", "panels")),
            P(("groups", "panels"), None, None, None),
        ),
        out_specs=(
            P(("groups", "nodes"), None, "rhs", "panels"),
            P(("groups", "nodes"), None, "rhs", "panels"),
            P(("groups", "nodes"), None, None, "rhs"),
        ),
        check_vma=False,
    )
```

```python
import functools
import math

import jax
import jax.numpy as jnp
import numpy as np
from jax import lax
from jax.experimental import pallas as pl
from jax.experimental.pallas import tpu as pltpu
from jax.sharding import PartitionSpec as P

MOM_DEV = 2
LANES = 128
TILE_CHUNK = 4
MOST_SHIFTS = 8

f32 = jnp.float32
bf16 = jnp.bfloat16

PARAMS = pltpu.CompilerParams(vmem_limit_bytes=40 * 1024 * 1024)
VMEM = pl.BlockSpec(memory_space=pltpu.VMEM)
HBM = pl.BlockSpec(memory_space=pltpu.HBM)


def dot_t(left, right):
    return lax.dot_general(left, right, (((1,), (1,)), ((), ())), preferred_element_type=f32)


def dot_n(left, right):
    return lax.dot_general(left, right, (((1,), (0,)), ((), ())), preferred_element_type=f32)


def split(value):
    high = value.astype(bf16)
    return high, (value - high.astype(f32)).astype(bf16)


def dot3_t(left, right):
    (l_hi, l_lo), (r_hi, r_lo) = left, right
    rows = l_hi.shape[0]
    both = dot_t(jnp.concatenate([l_hi, l_lo], axis=0), r_hi)
    return both[:rows] + both[rows:] + dot_t(l_hi, r_lo)


def dot3_n(left, right):
    (l_hi, l_lo), (r_hi, r_lo) = left, right
    rows = l_hi.shape[0]
    both = dot_n(jnp.concatenate([l_hi, l_lo], axis=0), r_hi)
    return both[:rows] + both[rows:] + dot_n(l_hi, r_lo)


def pick(index, values):
    result = f32(values[0])
    for i in range(1, len(values)):
        result = jnp.where(index == i, f32(values[i]), result)
    return result


def node_angle(node, nodes_all):
    return np.float32(2.0 * math.pi) * (np.float32(node) + np.float32(0.5)) / np.float32(nodes_all)


def terms_kernel(dims, *refs):
    panel_devs, blk_dev, shifted = dims
    n_out = panel_devs if shifted else 1
    indices, (contour_hbm, res_hbm, iter_hbm, probe_hbm, tiles_hbm, fr_hbm) = refs[:6], refs[6:12]
    outs, (pack, consts), refs = refs[12 : 12 + n_out], refs[12 + n_out : 14 + n_out], refs[14 + n_out :]
    held, (contour, tiles, fright, vec, terms, skel, acc, facc, sems) = refs[:6], refs[6:]
    tile_count = tiles.shape[0]
    far_count, _, rank, size = fright.shape
    res_rows, iter_rows = res_hbm.shape[0], iter_hbm.shape[0]
    node_dev = res_rows // 2
    chunk = TILE_CHUNK

    copies = []

    def start(source, target):
        copy = pltpu.make_async_copy(source, target, sems.at[len(copies)])
        copy.start()
        copies.append(copy)
        return copy

    res_copy = start(res_hbm, pack.at[pl.ds(0, res_rows)])
    small = [start(source, target) for source, target in zip(indices, held)]
    small.append(start(contour_hbm, contour))
    tile_copies = []
    for i in range(tile_count // chunk):
        part = pl.ds(i * chunk, chunk)
        tile_copies.append(start(tiles_hbm.at[part], tiles.at[part]))
    far_copy = start(fr_hbm, fright)
    rest = [
        start(iter_hbm, pack.at[pl.ds(res_rows, iter_rows)]),
        start(probe_hbm, pack.at[pl.ds(res_rows + iter_rows, 2)]),
    ]
    col, row, dest, fcol, frank, ftgt = held
    here = lax.axis_index("panels")

    def slot_of(owner):
        if shifted:
            owner = owner - here
            owner = jnp.where(owner < 0, owner + panel_devs, owner)
        return owner

    zero = jnp.zeros(acc.shape[1:], f32)
    for b in range(acc.shape[0]):
        acc[b] = zero
    for d in range(facc.shape[0]):
        facc[d] = zero

    res_copy.wait()
    for b in range(blk_dev):
        lanes = slice(b * size, (b + 1) * size)
        re = jnp.concatenate([pack[2 * k, :, lanes] for k in range(node_dev)], axis=0)
        im = jnp.concatenate([pack[2 * k + 1, :, lanes] for k in range(node_dev)], axis=0)
        upper = jnp.concatenate([re, -im], axis=1)
        lower = jnp.concatenate([im, re], axis=1)
        vec[b] = jnp.concatenate([upper, lower], axis=0).astype(bf16)

    for copy in small:
        copy.wait()
    for i in range(consts.shape[0]):
        consts[i : i + 1, :] = jnp.full((1, LANES), contour[min(i, 2)], f32)

    rows = vec.shape[1]
    for i, copy in enumerate(tile_copies):
        copy.wait()
        for t in range(i * chunk, (i + 1) * chunk):
            tile = jnp.concatenate([tiles[t, 0], tiles[t, 1]], axis=1)
            terms[t] = dot_t(vec[col[t]], tile)
    far_copy.wait()
    group = LANES // rank
    sources = vec[...].reshape(blk_dev * rows, 2 * size)
    for g in range(far_count // group):
        mats = [
            jnp.concatenate([fright[f, 0], fright[f, 1]], axis=1)
            for f in range(g * group, (g + 1) * group)
        ]
        skel[g] = dot_t(sources, jnp.concatenate(mats, axis=0)).reshape(blk_dev, rows, LANES)

    for t in range(tile_count):
        target = slot_of(dest[t]) * blk_dev + row[t]
        acc[target] = acc[target] + terms[t]
    lane = lax.broadcasted_iota(jnp.int32, (rows, LANES), 1)
    for f in range(far_count):
        target = ftgt[f]
        owner = target // blk_dev
        place = (target - owner * blk_dev) * rank
        moved = pltpu.roll(
            skel[f // group, fcol[f]], lax.rem(place - (f % group) * rank + LANES, LANES), 1
        )
        kept = (lane >= place) & (lane < place + frank[f])
        slot = slot_of(owner)
        facc[slot] = facc[slot] + jnp.where(kept, moved, 0.0)

    near_rows = blk_dev * rows
    for d in range(panel_devs):
        out = outs[d] if shifted else outs[0].at[d]
        for b in range(blk_dev):
            out[b * rows : (b + 1) * rows, :] = acc[d * blk_dev + b]
        out[near_rows:, :] = facc[d]
    for copy in rest:
        copy.wait()


def product_kernel(dims, *refs):
    node_devs, nodes_all = dims
    parts, (left, pack, contour, out) = refs[:-4], refs[-4:]
    parts = [p for part in parts for p in ([part[d] for d in range(part.shape[0])] if len(part.shape) == 3 else [part[...]])]
    node_dev, _, rhs_dev, _ = out.shape
    blk_dev, _, rank, size = left.shape
    rows = 2 * node_dev * rhs_dev
    half = rows // 2

    total = parts[0]
    for part in parts[1:]:
        total = total + part
    near = total[: blk_dev * rows]
    summed = total[blk_dev * rows :]
    re, im = summed[:half], summed[half:]
    upper = jnp.concatenate([re, -im], axis=1)
    lower = jnp.concatenate([im, re], axis=1)
    whole = jnp.concatenate([upper, lower], axis=0)
    lane = lax.broadcasted_iota(jnp.int32, whole.shape, 1)
    block = lax.rem(lane, LANES) // rank
    picked = [jnp.where(block == b, whole, 0.0) for b in range(blk_dev)]
    mats = left[...]
    stacked = jnp.concatenate(
        [mats[:, 0].reshape(blk_dev * rank, size), mats[:, 1].reshape(blk_dev * rank, size)], axis=0
    )
    applied = near + dot_n(jnp.concatenate(picked, axis=0).astype(bf16), stacked)

    here = lax.axis_index("nodes")
    for k in range(node_dev):
        cosines, sines = [], []
        for x in range(node_devs):
            angle = node_angle(x * node_dev + k, nodes_all)
            cosines.append(float(np.cos(angle)))
            sines.append(float(np.sin(angle)))
        shift_re = contour[0:1, :] + contour[2:3, :] * pick(here, cosines)
        shift_im = contour[1:2, :] + contour[2:3, :] * pick(here, sines)
        for b in range(blk_dev):
            lanes = slice(b * size, (b + 1) * size)
            top = b * rows + k * rhs_dev
            r_re, r_im = pack[2 * k, :, lanes], pack[2 * k + 1, :, lanes]
            out[k, 0, :, lanes] = applied[top : top + rhs_dev] - (shift_re * r_re - shift_im * r_im)
            top = top + half
            out[k, 1, :, lanes] = applied[top : top + rhs_dev] - (shift_re * r_im + shift_im * r_re)


def side_by_side(pair, row, count):
    return jnp.concatenate([pair[row : row + count], pair[row + count : row + 2 * count]], axis=1)


def turned(pair, row, count):
    return jnp.concatenate([-pair[row + count : row + 2 * count], pair[row : row + count]], axis=1)


def joined(own, other, row):
    return jnp.concatenate([own[row], other[row]], axis=0)


def ahead_kernel(own, other, res_hi, res_lo, message):
    _, rhs_dev, _ = own.shape
    cols = 2 * rhs_dev
    res_rows = res_hi.shape[0] // cols
    node_dev = res_rows // 2

    for i in range(res_rows):
        high, low = split(joined(own, other, i))
        res_hi[i * cols : (i + 1) * cols, :] = high
        res_lo[i * cols : (i + 1) * cols, :] = low

    first = lax.axis_index("rhs") == 0
    probe = []
    for c in range(2):
        mine, theirs = own[2 * res_rows + c], other[2 * res_rows + c]
        top = jnp.where(first, mine, theirs)
        bottom = jnp.where(first, theirs, mine)
        probe.append(jnp.concatenate([top, bottom], axis=0))
    probe = split(jnp.concatenate(probe, axis=1))
    pair = []
    for held in (res_hi[...], res_lo[...]):
        rows = []
        for k in range(node_dev):
            rows.append(side_by_side(held, k * 2 * cols, cols))
            rows.append(-turned(held, k * 2 * cols, cols))
        pair.append(jnp.concatenate(rows, axis=0))
    probe_res = dot3_t(probe, tuple(pair))
    rows = []
    for k in range(node_dev):
        i_re, i_im = own[res_rows + 2 * k], own[res_rows + 2 * k + 1]
        rows.append(jnp.concatenate([i_re, i_im], axis=1))
        rows.append(jnp.concatenate([i_im, -i_re], axis=1))
    probe_iter = dot3_t(split(jnp.concatenate(rows, axis=0)), probe)

    message[0:rhs_dev, :] = jnp.zeros((rhs_dev, LANES), f32)
    pieces = [jnp.zeros((rhs_dev, LANES // 2), f32)]
    for q in range(res_rows):
        pieces.append(probe_iter[q * rhs_dev : (q + 1) * rhs_dev])
    message[rhs_dev : 2 * rhs_dev, :] = jnp.concatenate(pieces, axis=1)
    message[2 * rhs_dev :, :] = jnp.concatenate([probe_res[:rhs_dev], probe_res[rhs_dev:]], axis=1)


def node_weight(here, scale, node_devs, node_dev, nodes_all, p, s, k):
    cosines, sines = [], []
    for x in range(node_devs):
        node = (x - s) % node_devs * node_dev + k
        power = x * MOM_DEV + p
        angle = np.float32(power + 1) * node_angle(node, nodes_all)
        cosines.append(float(np.cos(angle)))
        sines.append(float(np.sin(angle)))
    return scale * pick(here, cosines), scale * pick(here, sines)


def gram_kernel(own, other, res_hi, res_lo, ahead, message, prod_hi, prod_lo):
    node_dev, _, rhs_dev, _ = own.shape
    cols = 2 * rhs_dev
    for k in range(node_dev):
        for c in range(2):
            high, low = split(jnp.concatenate([own[k, c], other[k, c]], axis=0))
            top = (k * 2 + c) * cols
            prod_hi[top : top + cols, :] = high
            prod_lo[top : top + cols, :] = low
    sums = []
    for k in range(node_dev):
        top = k * 2 * cols
        left, right = [], []
        for p_ref, r_ref in ((prod_hi, res_hi), (prod_lo, res_lo)):
            product, source = p_ref[...], r_ref[: node_dev * 2 * cols, :]
            plain = side_by_side(product, top, cols)
            left.append(jnp.concatenate([plain, side_by_side(source, top, cols)], axis=0))
            right.append(jnp.concatenate([plain, turned(product, top, cols)], axis=0))
        sums.append(dot3_t(tuple(left), tuple(right)))
    gram = jnp.concatenate(sums, axis=1)
    half = LANES // 2
    top = jnp.concatenate([gram[:rhs_dev], gram[rhs_dev:cols]], axis=1)
    middle = jnp.concatenate([gram[cols : cols + rhs_dev], ahead[rhs_dev:cols, half:]], axis=1)
    bottom = ahead[cols:, :]
    message[0:rhs_dev, :] = top
    message[rhs_dev:cols, :] = middle
    message[cols:, :] = bottom


def finish_kernel(dims, *refs):
    node_devs, nodes_all, scale_factor = dims
    it = iter(refs)
    parts = [next(it) for _ in range(node_devs)]
    packs = [(next(it), next(it)) for _ in range(node_devs)]
    prod_hi, prod_lo, res_hi, res_lo, contour, next_out, mom_out, hankel_out = it
    node_dev, _, rhs_dev, width = next_out.shape
    cols = 2 * rhs_dev
    half = LANES // 2
    res_rows = 2 * node_dev
    here = lax.axis_index("nodes")

    sums = [part[...] for part in parts]
    if node_devs % 2:
        sums.append(sums[0])

    shape = (rhs_dev, LANES)
    lane = lax.broadcasted_iota(jnp.int32, shape, 1)
    low_half = lane < half
    base = (lane // (2 * cols)) * (2 * cols)
    spot = lax.rem(lane, cols)
    real_lane = lax.rem(lane, 2 * cols) < cols
    swapped = jnp.where(real_lane, lane + cols, lane - cols)
    sign = jnp.where(real_lane, -1.0, 1.0)

    def gathered(value, index):
        return jnp.take_along_axis(value, index, axis=1, mode="promise_in_bounds")

    solved, probe_res = [], []
    for g in range(len(sums) // 2):
        s0, s1 = sums[2 * g], sums[2 * g + 1]
        r0, r1 = pltpu.roll(s0, half, 1), pltpu.roll(s1, half, 1)
        v0, v1, v2 = slice(0, rhs_dev), slice(rhs_dev, cols), slice(cols, cols + rhs_dev)
        block = [
            jnp.where(low_half, s0[v0], r1[v0]),
            jnp.where(low_half, r0[v0], s1[v0]),
            jnp.where(low_half, s0[v1], r1[v1]),
        ]
        probe_res.append(
            jnp.concatenate(
                [jnp.where(low_half, s0[v2], r1[v2]), jnp.where(low_half, r0[v2], s1[v2])], axis=0
            )
        )
        inverse_diag = jnp.ones(shape, f32)
        for j in range(cols):
            at, r = divmod(j, rhs_dev)
            line = block[at][r : r + 1]
            crossed = (gathered(block[at], swapped) * sign)[r : r + 1]
            col_re = [gathered(b, base + j) for b in block[at:]]
            col_im = [gathered(b, base + cols + j) for b in block[at:]]
            inverse = 1.0 / col_re[0][r : r + 1]
            kept = (spot != j)[:1]
            scaled = jnp.where(kept, inverse, 0.0)
            f1, f2 = line * scaled, crossed * scaled
            for i in range(at, 3):
                block[i] = block[i] - (col_re[i - at] * f1 + col_im[i - at] * f2)
            inverse_diag = jnp.where(spot == j, inverse, inverse_diag)
        solved.append(block[2] * inverse_diag)

    coef = solved[0]
    cross = gathered(coef, swapped)
    plain = jnp.where(real_lane, coef, -coef)
    node_of = lane // (2 * cols)
    rows = []
    for k in range(node_dev):
        rows.append(jnp.where(node_of == k, plain, 0.0))
        rows.append(jnp.where(node_of == k, cross, 0.0))
    used = node_dev * 2 * cols
    left = split(jnp.concatenate(rows, axis=0)[:, :used])
    change = dot3_n(left, (prod_hi[...], prod_lo[...]))
    for k in range(node_dev):
        for c in range(2):
            top = (k * 2 + c) * rhs_dev
            next_out[k, c] = packs[0][0][2 * k + c] - change[top : top + rhs_dev]

    scale = contour[2:3, :] / nodes_all
    weighted = []
    for g, coef in enumerate(solved):
        cross = gathered(coef, swapped)
        rows = []
        for p in range(MOM_DEV):
            w_re = jnp.zeros(shape, f32)
            w_im = jnp.zeros(shape, f32)
            for i in range(2):
                s = 2 * g + i
                if s >= node_devs:
                    continue
                for k in range(node_dev):
                    n_re, n_im = node_weight(here, scale, node_devs, node_dev, nodes_all, p, s, k)
                    mine = node_of == i * node_dev + k
                    w_re = jnp.where(mine, n_re, w_re)
                    w_im = jnp.where(mine, n_im, w_im)
            rows.append(-sign * w_re * coef - w_im * cross)
            rows.append(-sign * w_im * coef + w_re * cross)
        weighted.append(jnp.concatenate(rows, axis=0))
    hankel = None
    products = None
    for g, value in enumerate(weighted):
        depth = min(LANES, node_devs * used - g * LANES)
        left = split(value)
        cut = tuple(part[:, :depth] for part in left)
        highs, lows = [], []
        for i in range(depth // used):
            s = 2 * g + i
            if s == 0:
                highs.append(res_hi[...])
                lows.append(res_lo[...])
                continue
            for q in range(res_rows):
                high, low = split(joined(packs[s][0], packs[s][1], q))
                highs.append(high)
                lows.append(low)
        term = dot3_n(cut, (jnp.concatenate(highs, axis=0), jnp.concatenate(lows, axis=0)))
        products = term if products is None else products + term
        term = dot3_t(left, split(probe_res[g]))
        hankel = term if hankel is None else hankel + term

    wide = jnp.concatenate([scale] * (width // LANES), axis=1)
    for p in range(MOM_DEV):
        mom = [products[(2 * p + c) * rhs_dev : (2 * p + c + 1) * rhs_dev] for c in range(2)]
        han = [hankel[(2 * p + c) * rhs_dev : (2 * p + c + 1) * rhs_dev] for c in range(2)]
        for s in range(node_devs):
            for k in range(node_dev):
                w_re, w_im = node_weight(here, wide, node_devs, node_dev, nodes_all, p, s, k)
                i_re, i_im = packs[s][0][res_rows + 2 * k], packs[s][0][res_rows + 2 * k + 1]
                mom[0] = mom[0] + (w_re * i_re - w_im * i_im)
                mom[1] = mom[1] + (w_re * i_im + w_im * i_re)
                i_re, i_im = [
                    pltpu.roll(sums[s][rhs_dev:cols], half - (2 * k + c) * cols, 1)[:, :cols]
                    for c in range(2)
                ]
                w_re, w_im = w_re[:, :cols], w_im[:, :cols]
                han[0] = han[0] + (w_re * i_re - w_im * i_im)
                han[1] = han[1] + (w_re * i_im + w_im * i_re)
        for c in range(2):
            mom_out[p, c] = mom[c]
            hankel_out[p, c] = han[c] * scale_factor


def call(kernel, out_shape, args, in_specs=None, scratch=(), cost=None):
    args = tuple(args)
    multiple = isinstance(out_shape, (list, tuple))
    return pl.pallas_call(
        kernel,
        out_shape=out_shape,
        in_specs=[VMEM] * len(args) if in_specs is None else in_specs,
        out_specs=[VMEM] * len(out_shape) if multiple else VMEM,
        scratch_shapes=list(scratch),
        compiler_params=PARAMS,
        cost_estimate=cost,
    )(*args)


def struct(shape, dtype=f32):
    return jax.ShapeDtypeStruct(shape, dtype)


def per_device(
    residual,
    iterate,
    probe,
    contour,
    near_tiles,
    near_col,
    near_row,
    near_dest,
    far_right,
    far_col,
    far_rank,
    far_target,
    far_left,
):
    node_dev, _, rhs_dev, rows_dev = residual.shape
    tile_count, _, size, _ = near_tiles.shape
    far_count, _, rank, _ = far_right.shape
    blk_dev = rows_dev // size
    panel_devs = lax.axis_size("panels")
    node_devs = lax.axis_size("nodes")
    nodes_all = node_dev * node_devs
    vec_rows = 2 * node_dev * rhs_dev
    cols = 2 * rhs_dev
    res_rows = 2 * node_dev
    span = res_rows * cols

    part_rows = blk_dev * vec_rows + vec_rows
    copies = 6 + 1 + tile_count // TILE_CHUNK + 4
    pack_shape = (2 * res_rows + 2, rhs_dev, rows_dev)
    indices = (near_col, near_row, near_dest.reshape(tile_count), far_col, far_rank, far_target)
    shifted = panel_devs <= MOST_SHIFTS
    out_shape = [struct((part_rows, LANES))] * panel_devs if shifted else [struct((panel_devs, part_rows, LANES))]
    in_hbm = functools.partial(pltpu.with_memory_space_constraint, memory_space=pltpu.HBM)
    *terms, pack, consts = call(
        functools.partial(terms_kernel, (panel_devs, blk_dev, shifted)),
        [*out_shape, struct(pack_shape), struct((8, LANES))],
        map(in_hbm, (
            *indices,
            contour,
            residual.reshape(res_rows, rhs_dev, rows_dev),
            iterate.reshape(res_rows, rhs_dev, rows_dev),
            probe,
            near_tiles,
            far_right,
        )),
        in_specs=[HBM] * 12,
        scratch=[
            *[pltpu.SMEM(index.shape, jnp.int32) for index in indices],
            pltpu.SMEM(contour.shape, f32),
            pltpu.VMEM(near_tiles.shape, bf16),
            pltpu.VMEM(far_right.shape, bf16),
            pltpu.VMEM((blk_dev, vec_rows, 2 * size), bf16),
            pltpu.VMEM((tile_count, vec_rows, size), f32),
            pltpu.VMEM((far_count * rank // LANES, blk_dev, vec_rows, LANES), f32),
            pltpu.VMEM((panel_devs * blk_dev, vec_rows, size), f32),
            pltpu.VMEM((panel_devs, vec_rows, LANES), f32),
            pltpu.SemaphoreType.DMA((copies,)),
        ],
    )

    swap = [(0, 1), (1, 0)]
    packs = []
    for s in range(node_devs):
        pairs = [(i, (i + s) % node_devs) for i in range(node_devs)]
        there = lax.ppermute(pack, "nodes", pairs) if s else pack
        packs.append((there, lax.ppermute(there, "rhs", swap)))

    if shifted:
        parts = terms[:1]
        for d in range(1, panel_devs):
            pairs = [(i, (i + d) % panel_devs) for i in range(panel_devs)]
            parts.append(lax.ppermute(terms[d], "panels", pairs))
    else:
        parts = [lax.all_to_all(terms[0], "panels", split_axis=0, concat_axis=0, tiled=True)]
    product = call(
        functools.partial(product_kernel, (node_devs, nodes_all)),
        struct(residual.shape),
        (*parts, far_left.transpose(0, 1, 3, 2), pack, consts),
    )
    res_hi, res_lo, ahead = call(
        ahead_kernel,
        [struct((span, rows_dev), bf16), struct((span, rows_dev), bf16), struct((3 * rhs_dev, LANES))],
        packs[0],
    )
    message, prod_hi, prod_lo = call(
        gram_kernel,
        [
            struct((3 * rhs_dev, LANES)),
            struct((span, rows_dev), bf16),
            struct((span, rows_dev), bf16),
        ],
        (product, lax.ppermute(product, "rhs", swap), res_hi, res_lo, ahead),
    )
    if panel_devs & (panel_devs - 1):
        message = lax.psum(message, "panels")
    else:
        step = 1
        while step < panel_devs:
            pairs = [(i, i ^ step) for i in range(panel_devs)]
            message = message + lax.ppermute(message, "panels", pairs)
            step *= 2
    sums = [message]
    for s in range(1, node_devs):
        pairs = [(i, (i + s) % node_devs) for i in range(node_devs)]
        sums.append(lax.ppermute(message, "nodes", pairs))
    scale_factor = 1.0 / math.sqrt(rows_dev * panel_devs)
    residual_next, moments, hankel = call(
        functools.partial(finish_kernel, (node_devs, nodes_all, scale_factor)),
        [
            struct(residual.shape),
            struct((MOM_DEV, 2, rhs_dev, rows_dev)),
            struct((MOM_DEV, 2, rhs_dev, cols)),
        ],
        (*sums, *[p for pair in packs for p in pair], prod_hi, prod_lo, res_hi, res_lo, consts),
    )
    return residual_next, moments, hankel.transpose(0, 1, 3, 2)


def solution(mesh):
    return jax.shard_map(
        per_device,
        mesh=mesh,
        in_specs=(
            P(("groups", "nodes"), None, "rhs", "panels"),
            P(("groups", "nodes"), None, "rhs", "panels"),
            P("groups", "rhs", "panels"),
            P("groups"),
            P(("groups", "panels"), None, None, None),
            P(("groups", "panels")),
            P(("groups", "panels")),
            P(("groups", "panels"), None),
            P(("groups", "panels"), None, None, None),
            P(("groups", "panels")),
            P(("groups", "panels")),
            P(("groups", "panels")),
            P(("groups", "panels"), None, None, None),
        ),
        out_specs=(
            P(("groups", "nodes"), None, "rhs", "panels"),
            P(("groups", "nodes"), None, "rhs", "panels"),
            P(("groups", "nodes"), None, None, "rhs"),
        ),
        check_vma=False,
    )
```

```python
import functools
import math

import jax
import jax.numpy as jnp
import numpy as np
from jax import lax
from jax.experimental import pallas as pl
from jax.experimental.pallas import tpu as pltpu
from jax.sharding import PartitionSpec as P

MOM_DEV = 2
LANES = 128
TILE_CHUNK = 4
MOST_SHIFTS = 8

f32 = jnp.float32
bf16 = jnp.bfloat16

PARAMS = pltpu.CompilerParams(vmem_limit_bytes=40 * 1024 * 1024)
VMEM = pl.BlockSpec(memory_space=pltpu.VMEM)
HBM = pl.BlockSpec(memory_space=pltpu.HBM)


def dot_t(left, right):
    return lax.dot_general(left, right, (((1,), (1,)), ((), ())), preferred_element_type=f32)


def dot_n(left, right):
    return lax.dot_general(left, right, (((1,), (0,)), ((), ())), preferred_element_type=f32)


def split(value):
    high = value.astype(bf16)
    return high, (value - high.astype(f32)).astype(bf16)


def dot3_t(left, right):
    (l_hi, l_lo), (r_hi, r_lo) = left, right
    rows = l_hi.shape[0]
    both = dot_t(jnp.concatenate([l_hi, l_lo], axis=0), r_hi)
    return both[:rows] + both[rows:] + dot_t(l_hi, r_lo)


def dot3_n(left, right):
    (l_hi, l_lo), (r_hi, r_lo) = left, right
    rows = l_hi.shape[0]
    both = dot_n(jnp.concatenate([l_hi, l_lo], axis=0), r_hi)
    return both[:rows] + both[rows:] + dot_n(l_hi, r_lo)


def pick(index, values):
    result = f32(values[0])
    for i in range(1, len(values)):
        result = jnp.where(index == i, f32(values[i]), result)
    return result


def node_angle(node, nodes_all):
    return np.float32(2.0 * math.pi) * (np.float32(node) + np.float32(0.5)) / np.float32(nodes_all)


def terms_kernel(dims, *refs):
    panel_devs, blk_dev, shifted = dims
    n_out = panel_devs if shifted else 1
    indices, (contour_hbm, res_hbm, iter_hbm, probe_hbm, tiles_hbm, fr_hbm) = refs[:6], refs[6:12]
    outs, refs = refs[12 : 12 + n_out], refs[12 + n_out :]
    (pack, fields, consts), refs = refs[:3], refs[3:]
    held, (contour, tiles, fright, vec, terms, skel, acc, facc, sems) = refs[:6], refs[6:]
    tile_count = tiles.shape[0]
    far_count, _, rank, size = fright.shape
    res_rows, iter_rows = res_hbm.shape[0], iter_hbm.shape[0]
    node_dev = res_rows // 2
    chunk = TILE_CHUNK

    copies = []

    def start(source, target):
        copy = pltpu.make_async_copy(source, target, sems.at[len(copies)])
        copy.start()
        copies.append(copy)
        return copy

    res_copy = start(res_hbm, pack.at[pl.ds(0, res_rows)])
    small = [start(source, target) for source, target in zip(indices, held)]
    small.append(start(contour_hbm, contour))
    tile_copies = []
    for i in range(tile_count // chunk):
        part = pl.ds(i * chunk, chunk)
        tile_copies.append(start(tiles_hbm.at[part], tiles.at[part]))
    far_copy = start(fr_hbm, fright)
    rest = [
        start(iter_hbm, pack.at[pl.ds(res_rows, iter_rows)]),
        start(probe_hbm, pack.at[pl.ds(res_rows + iter_rows, 2)]),
    ]
    col, row, dest, fcol, frank, ftgt = held
    here = lax.axis_index("panels")

    def slot_of(owner):
        if shifted:
            owner = owner - here
            owner = jnp.where(owner < 0, owner + panel_devs, owner)
        return owner

    zero = jnp.zeros(acc.shape[1:], f32)
    for b in range(acc.shape[0]):
        acc[b] = zero
    for d in range(facc.shape[0]):
        facc[d] = zero

    res_copy.wait()
    for i in range(res_rows):
        fields[i] = pack[i]
    for b in range(blk_dev):
        lanes = slice(b * size, (b + 1) * size)
        re = jnp.concatenate([pack[2 * k, :, lanes] for k in range(node_dev)], axis=0)
        im = jnp.concatenate([pack[2 * k + 1, :, lanes] for k in range(node_dev)], axis=0)
        upper = jnp.concatenate([re, -im], axis=1)
        lower = jnp.concatenate([im, re], axis=1)
        vec[b] = jnp.concatenate([upper, lower], axis=0).astype(bf16)

    for copy in small:
        copy.wait()
    for i in range(consts.shape[0]):
        consts[i : i + 1, :] = jnp.full((1, LANES), contour[min(i, 2)], f32)

    rows = vec.shape[1]
    for i, copy in enumerate(tile_copies):
        copy.wait()
        for t in range(i * chunk, (i + 1) * chunk):
            tile = jnp.concatenate([tiles[t, 0], tiles[t, 1]], axis=1)
            terms[t] = dot_t(vec[col[t]], tile)
    far_copy.wait()
    group = LANES // rank
    sources = vec[...].reshape(blk_dev * rows, 2 * size)
    for g in range(far_count // group):
        mats = [
            jnp.concatenate([fright[f, 0], fright[f, 1]], axis=1)
            for f in range(g * group, (g + 1) * group)
        ]
        skel[g] = dot_t(sources, jnp.concatenate(mats, axis=0)).reshape(blk_dev, rows, LANES)

    for t in range(tile_count):
        target = slot_of(dest[t]) * blk_dev + row[t]
        acc[target] = acc[target] + terms[t]
    lane = lax.broadcasted_iota(jnp.int32, (rows, LANES), 1)
    for f in range(far_count):
        target = ftgt[f]
        owner = target // blk_dev
        place = (target - owner * blk_dev) * rank
        moved = pltpu.roll(
            skel[f // group, fcol[f]], lax.rem(place - (f % group) * rank + LANES, LANES), 1
        )
        kept = (lane >= place) & (lane < place + frank[f])
        slot = slot_of(owner)
        facc[slot] = facc[slot] + jnp.where(kept, moved, 0.0)

    near_rows = blk_dev * rows
    for d in range(panel_devs):
        out = outs[d] if shifted else outs[0].at[d]
        for b in range(blk_dev):
            out[b * rows : (b + 1) * rows, :] = acc[d * blk_dev + b]
        out[near_rows:, :] = facc[d]
    for copy in rest:
        copy.wait()


def product_kernel(dims, *refs):
    node_devs, nodes_all = dims
    parts, (left, pack, contour, out) = refs[:-4], refs[-4:]
    parts = [p for part in parts for p in ([part[d] for d in range(part.shape[0])] if len(part.shape) == 3 else [part[...]])]
    node_dev, _, rhs_dev, _ = out.shape
    blk_dev, _, rank, size = left.shape
    rows = 2 * node_dev * rhs_dev
    half = rows // 2

    total = parts[0]
    for part in parts[1:]:
        total = total + part
    near = total[: blk_dev * rows]
    summed = total[blk_dev * rows :]
    re, im = summed[:half], summed[half:]
    upper = jnp.concatenate([re, -im], axis=1)
    lower = jnp.concatenate([im, re], axis=1)
    whole = jnp.concatenate([upper, lower], axis=0)
    lane = lax.broadcasted_iota(jnp.int32, whole.shape, 1)
    block = lax.rem(lane, LANES) // rank
    picked = [jnp.where(block == b, whole, 0.0) for b in range(blk_dev)]
    mats = left[...]
    stacked = jnp.concatenate(
        [mats[:, 0].reshape(blk_dev * rank, size), mats[:, 1].reshape(blk_dev * rank, size)], axis=0
    )
    applied = near + dot_n(jnp.concatenate(picked, axis=0).astype(bf16), stacked)

    here = lax.axis_index("nodes")
    for k in range(node_dev):
        cosines, sines = [], []
        for x in range(node_devs):
            angle = node_angle(x * node_dev + k, nodes_all)
            cosines.append(float(np.cos(angle)))
            sines.append(float(np.sin(angle)))
        shift_re = contour[0:1, :] + contour[2:3, :] * pick(here, cosines)
        shift_im = contour[1:2, :] + contour[2:3, :] * pick(here, sines)
        for b in range(blk_dev):
            lanes = slice(b * size, (b + 1) * size)
            top = b * rows + k * rhs_dev
            r_re, r_im = pack[2 * k, :, lanes], pack[2 * k + 1, :, lanes]
            out[k, 0, :, lanes] = applied[top : top + rhs_dev] - (shift_re * r_re - shift_im * r_im)
            top = top + half
            out[k, 1, :, lanes] = applied[top : top + rhs_dev] - (shift_re * r_im + shift_im * r_re)


def side_by_side(pair, row, count):
    return jnp.concatenate([pair[row : row + count], pair[row + count : row + 2 * count]], axis=1)


def turned(pair, row, count):
    return jnp.concatenate([-pair[row + count : row + 2 * count], pair[row : row + count]], axis=1)


def joined(own, other, row):
    first = lax.axis_index("rhs") == 0
    mine, theirs = own[row], other[row]
    top = jnp.where(first, mine, theirs)
    bottom = jnp.where(first, theirs, mine)
    return jnp.concatenate([top, bottom], axis=0)


def ahead_kernel(own, other, res_hi, res_lo, message):
    _, rhs_dev, _ = own.shape
    cols = 2 * rhs_dev
    res_rows = res_hi.shape[0] // cols
    node_dev = res_rows // 2

    for i in range(res_rows):
        high, low = split(joined(own, other, i))
        res_hi[i * cols : (i + 1) * cols, :] = high
        res_lo[i * cols : (i + 1) * cols, :] = low

    probe = [joined(own, other, 2 * res_rows + c) for c in range(2)]
    probe = split(jnp.concatenate(probe, axis=1))
    pair = []
    for held in (res_hi[...], res_lo[...]):
        rows = []
        for k in range(node_dev):
            rows.append(side_by_side(held, k * 2 * cols, cols))
            rows.append(-turned(held, k * 2 * cols, cols))
        pair.append(jnp.concatenate(rows, axis=0))
    probe_res = dot3_t(probe, tuple(pair))
    rows = []
    for k in range(node_dev):
        i_re, i_im = [joined(own, other, res_rows + 2 * k + c) for c in range(2)]
        rows.append(jnp.concatenate([i_re, i_im], axis=1))
        rows.append(jnp.concatenate([i_im, -i_re], axis=1))
    probe_iter = dot3_t(split(jnp.concatenate(rows, axis=0)), probe)

    message[: 2 * rhs_dev, :] = jnp.zeros((2 * rhs_dev, LANES), f32)
    message[2 * rhs_dev : 3 * rhs_dev, :] = jnp.concatenate(
        [probe_res[:rhs_dev], probe_res[rhs_dev:]], axis=1
    )
    pieces = []
    for top in (0, rhs_dev):
        pieces.extend(probe_iter[q * cols + top : q * cols + top + rhs_dev] for q in range(res_rows))
    message[3 * rhs_dev :, :] = jnp.concatenate(pieces, axis=1)


def node_weight(here, scale, node_devs, node_dev, nodes_all, p, s, k):
    cosines, sines = [], []
    for x in range(node_devs):
        node = (x - s) % node_devs * node_dev + k
        power = x * MOM_DEV + p
        angle = np.float32(power + 1) * node_angle(node, nodes_all)
        cosines.append(float(np.cos(angle)))
        sines.append(float(np.sin(angle)))
    return scale * pick(here, cosines), scale * pick(here, sines)


def gram_kernel(own, other, res_hi, res_lo, ahead, message, prod_hi, prod_lo):
    node_dev, _, rhs_dev, _ = own.shape
    cols = 2 * rhs_dev
    for k in range(node_dev):
        for c in range(2):
            high, low = split(joined(own, other, (k, c)))
            top = (k * 2 + c) * cols
            prod_hi[top : top + cols, :] = high
            prod_lo[top : top + cols, :] = low
    sums = []
    for k in range(node_dev):
        top = k * 2 * cols
        left, right = [], []
        for p_ref, r_ref in ((prod_hi, res_hi), (prod_lo, res_lo)):
            product, source = p_ref[...], r_ref[: node_dev * 2 * cols, :]
            plain = side_by_side(product, top, cols)
            left.append(jnp.concatenate([plain, side_by_side(source, top, cols)], axis=0))
            right.append(jnp.concatenate([plain, turned(product, top, cols)], axis=0))
        sums.append(dot3_t(tuple(left), tuple(right)))
    gram = jnp.concatenate(sums, axis=1)
    message[:rhs_dev, :] = jnp.concatenate([gram[:rhs_dev], gram[rhs_dev:cols]], axis=1)
    message[rhs_dev:cols, :] = jnp.concatenate(
        [gram[cols : cols + rhs_dev], gram[cols + rhs_dev :]], axis=1
    )
    message[cols:, :] = ahead[cols:, :]


def finish_kernel(dims, *refs):
    node_devs, nodes_all, scale_factor = dims
    it = iter(refs)
    parts = [(next(it), next(it)) for _ in range(node_devs)]
    packs = [(next(it), next(it)) for _ in range(node_devs)]
    prod_hi, prod_lo, res_hi, res_lo, contour, next_out, mom_out, hankel_out = it
    node_dev, _, rhs_dev, width = next_out.shape
    cols = 2 * rhs_dev
    half = LANES // 2
    res_rows = 2 * node_dev
    here = lax.axis_index("nodes")

    first = lax.axis_index("rhs") == 0
    sums = [jnp.where(first, relayed[...], held[...]) for held, relayed in parts]
    if node_devs % 2:
        sums.append(sums[0])

    shape = (rhs_dev, LANES)
    lane = lax.broadcasted_iota(jnp.int32, shape, 1)
    low_half = lane < half
    base = (lane // (2 * cols)) * (2 * cols)
    spot = lax.rem(lane, cols)
    real_lane = lax.rem(lane, 2 * cols) < cols
    swapped = jnp.where(real_lane, lane + cols, lane - cols)
    sign = jnp.where(real_lane, -1.0, 1.0)

    def gathered(value, index):
        return jnp.take_along_axis(value, index, axis=1, mode="promise_in_bounds")

    solved, probe_res = [], []
    for g in range(len(sums) // 2):
        s0, s1 = sums[2 * g], sums[2 * g + 1]
        r0, r1 = pltpu.roll(s0, half, 1), pltpu.roll(s1, half, 1)
        v0, v1, v2 = [slice(i * rhs_dev, (i + 1) * rhs_dev) for i in range(3)]
        block = [
            jnp.where(low_half, s0[v0], r1[v0]),
            jnp.where(low_half, r0[v0], s1[v0]),
            jnp.where(
                low_half, jnp.where(first, s0[v1], r0[v1]), jnp.where(first, r1[v1], s1[v1])
            ),
        ]
        probe_res.append(
            jnp.concatenate(
                [jnp.where(low_half, s0[v2], r1[v2]), jnp.where(low_half, r0[v2], s1[v2])], axis=0
            )
        )
        inverse_diag = jnp.ones(shape, f32)
        for j in range(cols):
            at, r = divmod(j, rhs_dev)
            line = block[at][r : r + 1]
            crossed = (gathered(block[at], swapped) * sign)[r : r + 1]
            col_re = [gathered(b, base + j) for b in block[at:]]
            col_im = [gathered(b, base + cols + j) for b in block[at:]]
            inverse = 1.0 / col_re[0][r : r + 1]
            kept = (spot != j)[:1]
            scaled = jnp.where(kept, inverse, 0.0)
            f1, f2 = line * scaled, crossed * scaled
            for i in range(at, 3):
                block[i] = block[i] - (col_re[i - at] * f1 + col_im[i - at] * f2)
            inverse_diag = jnp.where(spot == j, inverse, inverse_diag)
        solved.append(block[2] * inverse_diag)

    coef = solved[0]
    cross = gathered(coef, swapped)
    plain = jnp.where(real_lane, coef, -coef)
    node_of = lane // (2 * cols)
    rows = []
    for k in range(node_dev):
        rows.append(jnp.where(node_of == k, plain, 0.0))
        rows.append(jnp.where(node_of == k, cross, 0.0))
    used = node_dev * 2 * cols
    left = split(jnp.concatenate(rows, axis=0)[:, :used])
    change = dot3_n(left, (prod_hi[...], prod_lo[...]))
    for k in range(node_dev):
        for c in range(2):
            top = (k * 2 + c) * rhs_dev
            next_out[k, c] = packs[0][0][2 * k + c] - change[top : top + rhs_dev]

    scale = contour[2:3, :] / nodes_all
    weighted = []
    for g, coef in enumerate(solved):
        cross = gathered(coef, swapped)
        rows = []
        for p in range(MOM_DEV):
            w_re = jnp.zeros(shape, f32)
            w_im = jnp.zeros(shape, f32)
            for i in range(2):
                s = 2 * g + i
                if s >= node_devs:
                    continue
                for k in range(node_dev):
                    n_re, n_im = node_weight(here, scale, node_devs, node_dev, nodes_all, p, s, k)
                    mine = node_of == i * node_dev + k
                    w_re = jnp.where(mine, n_re, w_re)
                    w_im = jnp.where(mine, n_im, w_im)
            rows.append(-sign * w_re * coef - w_im * cross)
            rows.append(-sign * w_im * coef + w_re * cross)
        weighted.append(jnp.concatenate(rows, axis=0))
    hankel = None
    products = None
    for g, value in enumerate(weighted):
        depth = min(LANES, node_devs * used - g * LANES)
        left = split(value)
        cut = tuple(part[:, :depth] for part in left)
        highs, lows = [], []
        for i in range(depth // used):
            s = 2 * g + i
            if s == 0:
                highs.append(res_hi[...])
                lows.append(res_lo[...])
                continue
            for q in range(res_rows):
                high, low = split(joined(packs[s][0], packs[s][1], q))
                highs.append(high)
                lows.append(low)
        term = dot3_n(cut, (jnp.concatenate(highs, axis=0), jnp.concatenate(lows, axis=0)))
        products = term if products is None else products + term
        term = dot3_t(left, split(probe_res[g]))
        hankel = term if hankel is None else hankel + term

    projected = []
    for s in range(node_devs):
        value = sums[s][3 * rhs_dev :]
        projected.append(jnp.where(first, value, pltpu.roll(value, half, 1)))
    wide = jnp.concatenate([scale] * (width // LANES), axis=1)
    for p in range(MOM_DEV):
        mom = [products[(2 * p + c) * rhs_dev : (2 * p + c + 1) * rhs_dev] for c in range(2)]
        han = [hankel[(2 * p + c) * rhs_dev : (2 * p + c + 1) * rhs_dev] for c in range(2)]
        for s in range(node_devs):
            for k in range(node_dev):
                w_re, w_im = node_weight(here, wide, node_devs, node_dev, nodes_all, p, s, k)
                i_re, i_im = packs[s][0][res_rows + 2 * k], packs[s][0][res_rows + 2 * k + 1]
                mom[0] = mom[0] + (w_re * i_re - w_im * i_im)
                mom[1] = mom[1] + (w_re * i_im + w_im * i_re)
                i_re, i_im = [
                    pltpu.roll(projected[s], LANES - (2 * k + c) * cols, 1)[:, :cols]
                    if k + c
                    else projected[s][:, :cols]
                    for c in range(2)
                ]
                w_re, w_im = w_re[:, :cols], w_im[:, :cols]
                han[0] = han[0] + (w_re * i_re - w_im * i_im)
                han[1] = han[1] + (w_re * i_im + w_im * i_re)
        for c in range(2):
            mom_out[p, c] = mom[c]
            hankel_out[p, c] = han[c] * scale_factor


def call(kernel, out_shape, args, in_specs=None, scratch=(), cost=None):
    args = tuple(args)
    multiple = isinstance(out_shape, (list, tuple))
    return pl.pallas_call(
        kernel,
        out_shape=out_shape,
        in_specs=[VMEM] * len(args) if in_specs is None else in_specs,
        out_specs=[VMEM] * len(out_shape) if multiple else VMEM,
        scratch_shapes=list(scratch),
        compiler_params=PARAMS,
        cost_estimate=cost,
    )(*args)


def struct(shape, dtype=f32):
    return jax.ShapeDtypeStruct(shape, dtype)


def per_device(
    residual,
    iterate,
    probe,
    contour,
    near_tiles,
    near_col,
    near_row,
    near_dest,
    far_right,
    far_col,
    far_rank,
    far_target,
    far_left,
):
    node_dev, _, rhs_dev, rows_dev = residual.shape
    tile_count, _, size, _ = near_tiles.shape
    far_count, _, rank, _ = far_right.shape
    blk_dev = rows_dev // size
    panel_devs = lax.axis_size("panels")
    node_devs = lax.axis_size("nodes")
    nodes_all = node_dev * node_devs
    vec_rows = 2 * node_dev * rhs_dev
    cols = 2 * rhs_dev
    res_rows = 2 * node_dev
    span = res_rows * cols

    part_rows = blk_dev * vec_rows + vec_rows
    copies = 6 + 1 + tile_count // TILE_CHUNK + 4
    pack_shape = (2 * res_rows + 2, rhs_dev, rows_dev)
    indices = (near_col, near_row, near_dest.reshape(tile_count), far_col, far_rank, far_target)
    shifted = panel_devs <= MOST_SHIFTS
    out_shape = [struct((part_rows, LANES))] * panel_devs if shifted else [struct((panel_devs, part_rows, LANES))]
    in_hbm = functools.partial(pltpu.with_memory_space_constraint, memory_space=pltpu.HBM)
    *terms, pack, fields, consts = call(
        functools.partial(terms_kernel, (panel_devs, blk_dev, shifted)),
        [*out_shape, struct(pack_shape), struct((res_rows, rhs_dev, rows_dev)), struct((8, LANES))],
        map(in_hbm, (
            *indices,
            contour,
            residual.reshape(res_rows, rhs_dev, rows_dev),
            iterate.reshape(res_rows, rhs_dev, rows_dev),
            probe,
            near_tiles,
            far_right,
        )),
        in_specs=[HBM] * 12,
        scratch=[
            *[pltpu.SMEM(index.shape, jnp.int32) for index in indices],
            pltpu.SMEM(contour.shape, f32),
            pltpu.VMEM(near_tiles.shape, bf16),
            pltpu.VMEM(far_right.shape, bf16),
            pltpu.VMEM((blk_dev, vec_rows, 2 * size), bf16),
            pltpu.VMEM((tile_count, vec_rows, size), f32),
            pltpu.VMEM((far_count * rank // LANES, blk_dev, vec_rows, LANES), f32),
            pltpu.VMEM((panel_devs * blk_dev, vec_rows, size), f32),
            pltpu.VMEM((panel_devs, vec_rows, LANES), f32),
            pltpu.SemaphoreType.DMA((copies,)),
        ],
    )

    if shifted:
        parts = terms[:1]
        for d in range(1, panel_devs):
            pairs = [(i, (i + d) % panel_devs) for i in range(panel_devs)]
            parts.append(lax.ppermute(terms[d], "panels", pairs))
    else:
        parts = [lax.all_to_all(terms[0], "panels", split_axis=0, concat_axis=0, tiled=True)]

    packs = [(pack, lax.ppermute(pack, "rhs", [(0, 1), (1, 0)]))]
    for s in range(1, node_devs):
        pairs = [(i, (i + s) % node_devs) for i in range(node_devs)]
        crossed = [(2 * i + c, 2 * j + 1 - c) for i, j in pairs for c in range(2)]
        packs.append((lax.ppermute(pack, "nodes", pairs), lax.ppermute(fields, ("nodes", "rhs"), crossed)))

    product = call(
        functools.partial(product_kernel, (node_devs, nodes_all)),
        struct(residual.shape),
        (*parts, far_left.transpose(0, 1, 3, 2), pack, consts),
    )
    res_hi, res_lo, ahead = call(
        ahead_kernel,
        [struct((span, rows_dev), bf16), struct((span, rows_dev), bf16), struct((4 * rhs_dev, LANES))],
        packs[0],
    )
    message, prod_hi, prod_lo = call(
        gram_kernel,
        [
            struct((4 * rhs_dev, LANES)),
            struct((span, rows_dev), bf16),
            struct((span, rows_dev), bf16),
        ],
        (product, lax.ppermute(product, "rhs", [(0, 1), (1, 0)]), res_hi, res_lo, ahead),
    )
    def last_core(pairs):
        return [(2 * i + 1, 2 * j + 1) for i, j in pairs]

    if panel_devs & (panel_devs - 1):
        message = lax.psum(message, "panels")
    else:
        step = 1
        while step < panel_devs:
            pairs = last_core([(i, i ^ step) for i in range(panel_devs)])
            message = message + lax.ppermute(message, ("panels", "rhs"), pairs)
            step *= 2
    sums = [message]
    for s in range(1, node_devs):
        pairs = last_core([(i, (i + s) % node_devs) for i in range(node_devs)])
        sums.append(lax.ppermute(message, ("nodes", "rhs"), pairs))
    sums = [part for value in sums for part in (value, lax.ppermute(value, "rhs", [(1, 0)]))]
    scale_factor = 1.0 / math.sqrt(rows_dev * panel_devs)
    residual_next, moments, hankel = call(
        functools.partial(finish_kernel, (node_devs, nodes_all, scale_factor)),
        [
            struct(residual.shape),
            struct((MOM_DEV, 2, rhs_dev, rows_dev)),
            struct((MOM_DEV, 2, rhs_dev, cols)),
        ],
        (*sums, *[p for pair in packs for p in pair], prod_hi, prod_lo, res_hi, res_lo, consts),
    )
    return residual_next, moments, hankel.transpose(0, 1, 3, 2)


def solution(mesh):
    return jax.shard_map(
        per_device,
        mesh=mesh,
        in_specs=(
            P(("groups", "nodes"), None, "rhs", "panels"),
            P(("groups", "nodes"), None, "rhs", "panels"),
            P("groups", "rhs", "panels"),
            P("groups"),
            P(("groups", "panels"), None, None, None),
            P(("groups", "panels")),
            P(("groups", "panels")),
            P(("groups", "panels"), None),
            P(("groups", "panels"), None, None, None),
            P(("groups", "panels")),
            P(("groups", "panels")),
            P(("groups", "panels")),
            P(("groups", "panels"), None, None, None),
        ),
        out_specs=(
            P(("groups", "nodes"), None, "rhs", "panels"),
            P(("groups", "nodes"), None, "rhs", "panels"),
            P(("groups", "nodes"), None, None, "rhs"),
        ),
        check_vma=False,
    )
```

```python
import functools
import math

import jax
import jax.numpy as jnp
import numpy as np
from jax import lax
from jax.experimental import pallas as pl
from jax.experimental.pallas import tpu as pltpu
from jax.sharding import PartitionSpec as P

MOM_DEV = 2
LANES = 128
TILE_CHUNK = 4
MOST_SHIFTS = 8

f32 = jnp.float32
bf16 = jnp.bfloat16

PARAMS = pltpu.CompilerParams(vmem_limit_bytes=40 * 1024 * 1024)
VMEM = pl.BlockSpec(memory_space=pltpu.VMEM)
HBM = pl.BlockSpec(memory_space=pltpu.HBM)


def dot_t(left, right):
    return lax.dot_general(left, right, (((1,), (1,)), ((), ())), preferred_element_type=f32)


def dot_n(left, right):
    return lax.dot_general(left, right, (((1,), (0,)), ((), ())), preferred_element_type=f32)


def split(value):
    high = value.astype(bf16)
    return high, (value - high.astype(f32)).astype(bf16)


def dot3_t(left, right):
    (l_hi, l_lo), (r_hi, r_lo) = left, right
    rows = l_hi.shape[0]
    both = dot_t(jnp.concatenate([l_hi, l_lo], axis=0), r_hi)
    return both[:rows] + both[rows:] + dot_t(l_hi, r_lo)


def dot3_n(left, right):
    (l_hi, l_lo), (r_hi, r_lo) = left, right
    rows = l_hi.shape[0]
    both = dot_n(jnp.concatenate([l_hi, l_lo], axis=0), r_hi)
    return both[:rows] + both[rows:] + dot_n(l_hi, r_lo)


def pick(index, values):
    result = f32(values[0])
    for i in range(1, len(values)):
        result = jnp.where(index == i, f32(values[i]), result)
    return result


def node_angle(node, nodes_all):
    return np.float32(2.0 * math.pi) * (np.float32(node) + np.float32(0.5)) / np.float32(nodes_all)


def terms_kernel(dims, *refs):
    panel_devs, blk_dev, shifted = dims
    n_out = panel_devs if shifted else 1
    indices, (contour_hbm, res_hbm, iter_hbm, probe_hbm, tiles_hbm, fr_hbm) = refs[:6], refs[6:12]
    outs, refs = refs[12 : 12 + n_out], refs[12 + n_out :]
    (pack, fields, consts), refs = refs[:3], refs[3:]
    held, (contour, tiles, fright, vec, terms, skel, acc, facc, sems) = refs[:6], refs[6:]
    tile_count = tiles.shape[0]
    far_count, _, rank, size = fright.shape
    res_rows, iter_rows = res_hbm.shape[0], iter_hbm.shape[0]
    node_dev = res_rows // 2
    chunk = TILE_CHUNK

    copies = []

    def start(source, target):
        copy = pltpu.make_async_copy(source, target, sems.at[len(copies)])
        copy.start()
        copies.append(copy)
        return copy

    res_copy = start(res_hbm, pack.at[pl.ds(0, res_rows)])
    small = [start(source, target) for source, target in zip(indices, held)]
    small.append(start(contour_hbm, contour))
    tile_copies = []
    for i in range(tile_count // chunk):
        part = pl.ds(i * chunk, chunk)
        tile_copies.append(start(tiles_hbm.at[part], tiles.at[part]))
    far_copy = start(fr_hbm, fright)
    rest = [
        start(iter_hbm, pack.at[pl.ds(res_rows, iter_rows)]),
        start(probe_hbm, pack.at[pl.ds(res_rows + iter_rows, 2)]),
    ]
    col, row, dest, fcol, frank, ftgt = held
    here = lax.axis_index("panels")

    def slot_of(owner):
        if shifted:
            owner = owner - here
            owner = jnp.where(owner < 0, owner + panel_devs, owner)
        return owner

    zero = jnp.zeros(acc.shape[1:], f32)
    for b in range(acc.shape[0]):
        acc[b] = zero
    for d in range(facc.shape[0]):
        facc[d] = zero

    res_copy.wait()
    for i in range(res_rows):
        fields[i] = pack[i]
    for b in range(blk_dev):
        lanes = slice(b * size, (b + 1) * size)
        re = jnp.concatenate([pack[2 * k, :, lanes] for k in range(node_dev)], axis=0)
        im = jnp.concatenate([pack[2 * k + 1, :, lanes] for k in range(node_dev)], axis=0)
        upper = jnp.concatenate([re, -im], axis=1)
        lower = jnp.concatenate([im, re], axis=1)
        vec[b] = jnp.concatenate([upper, lower], axis=0).astype(bf16)

    for copy in small:
        copy.wait()
    for i in range(consts.shape[0]):
        consts[i : i + 1, :] = jnp.full((1, LANES), contour[min(i, 2)], f32)

    rows = vec.shape[1]
    for i, copy in enumerate(tile_copies):
        copy.wait()
        for t in range(i * chunk, (i + 1) * chunk):
            tile = jnp.concatenate([tiles[t, 0], tiles[t, 1]], axis=1)
            terms[t] = dot_t(vec[col[t]], tile)
    far_copy.wait()
    group = LANES // rank
    sources = vec[...].reshape(blk_dev * rows, 2 * size)
    for g in range(far_count // group):
        mats = [
            jnp.concatenate([fright[f, 0], fright[f, 1]], axis=1)
            for f in range(g * group, (g + 1) * group)
        ]
        skel[g] = dot_t(sources, jnp.concatenate(mats, axis=0)).reshape(blk_dev, rows, LANES)

    for t in range(tile_count):
        target = slot_of(dest[t]) * blk_dev + row[t]
        acc[target] = acc[target] + terms[t]
    lane = lax.broadcasted_iota(jnp.int32, (rows, LANES), 1)
    for f in range(far_count):
        target = ftgt[f]
        owner = target // blk_dev
        place = (target - owner * blk_dev) * rank
        moved = pltpu.roll(
            skel[f // group, fcol[f]], lax.rem(place - (f % group) * rank + LANES, LANES), 1
        )
        kept = (lane >= place) & (lane < place + frank[f])
        slot = slot_of(owner)
        facc[slot] = facc[slot] + jnp.where(kept, moved, 0.0)

    near_rows = blk_dev * rows
    for d in range(panel_devs):
        out = outs[d] if shifted else outs[0].at[d]
        for b in range(blk_dev):
            out[b * rows : (b + 1) * rows, :] = acc[d * blk_dev + b]
        out[near_rows:, :] = facc[d]
    for copy in rest:
        copy.wait()


def product_kernel(dims, *refs):
    node_devs, nodes_all = dims
    parts, (left, pack, contour, out) = refs[:-4], refs[-4:]
    parts = [p for part in parts for p in ([part[d] for d in range(part.shape[0])] if len(part.shape) == 3 else [part[...]])]
    node_dev, _, rhs_dev, _ = out.shape
    blk_dev, _, rank, size = left.shape
    rows = 2 * node_dev * rhs_dev
    half = rows // 2

    total = parts[0]
    for part in parts[1:]:
        total = total + part
    near = total[: blk_dev * rows]
    summed = total[blk_dev * rows :]
    re, im = summed[:half], summed[half:]
    upper = jnp.concatenate([re, -im], axis=1)
    lower = jnp.concatenate([im, re], axis=1)
    whole = jnp.concatenate([upper, lower], axis=0)
    lane = lax.broadcasted_iota(jnp.int32, whole.shape, 1)
    block = lax.rem(lane, LANES) // rank
    picked = [jnp.where(block == b, whole, 0.0) for b in range(blk_dev)]
    mats = left[...]
    stacked = jnp.concatenate(
        [mats[:, 0].reshape(blk_dev * rank, size), mats[:, 1].reshape(blk_dev * rank, size)], axis=0
    )
    applied = near + dot_n(jnp.concatenate(picked, axis=0).astype(bf16), stacked)

    here = lax.axis_index("nodes")
    for k in range(node_dev):
        cosines, sines = [], []
        for x in range(node_devs):
            angle = node_angle(x * node_dev + k, nodes_all)
            cosines.append(float(np.cos(angle)))
            sines.append(float(np.sin(angle)))
        shift_re = contour[0:1, :] + contour[2:3, :] * pick(here, cosines)
        shift_im = contour[1:2, :] + contour[2:3, :] * pick(here, sines)
        for b in range(blk_dev):
            lanes = slice(b * size, (b + 1) * size)
            top = b * rows + k * rhs_dev
            r_re, r_im = pack[2 * k, :, lanes], pack[2 * k + 1, :, lanes]
            out[k, 0, :, lanes] = applied[top : top + rhs_dev] - (shift_re * r_re - shift_im * r_im)
            top = top + half
            out[k, 1, :, lanes] = applied[top : top + rhs_dev] - (shift_re * r_im + shift_im * r_re)


def side_by_side(pair, row, count):
    return jnp.concatenate([pair[row : row + count], pair[row + count : row + 2 * count]], axis=1)


def turned(pair, row, count):
    return jnp.concatenate([-pair[row + count : row + 2 * count], pair[row : row + count]], axis=1)


def joined(own, other, row):
    first = lax.axis_index("rhs") == 0
    mine, theirs = own[row], other[row]
    top = jnp.where(first, mine, theirs)
    bottom = jnp.where(first, theirs, mine)
    return jnp.concatenate([top, bottom], axis=0)


def ahead_kernel(own, other, res_hi, res_lo, message):
    _, rhs_dev, _ = own.shape
    cols = 2 * rhs_dev
    res_rows = res_hi.shape[0] // cols
    node_dev = res_rows // 2

    for i in range(res_rows):
        high, low = split(joined(own, other, i))
        res_hi[i * cols : (i + 1) * cols, :] = high
        res_lo[i * cols : (i + 1) * cols, :] = low

    probe = [joined(own, other, 2 * res_rows + c) for c in range(2)]
    probe = split(jnp.concatenate(probe, axis=1))
    pair = []
    for held in (res_hi[...], res_lo[...]):
        rows = []
        for k in range(node_dev):
            rows.append(side_by_side(held, k * 2 * cols, cols))
            rows.append(-turned(held, k * 2 * cols, cols))
        pair.append(jnp.concatenate(rows, axis=0))
    probe_res = dot3_t(probe, tuple(pair))
    rows = []
    for k in range(node_dev):
        i_re, i_im = [joined(own, other, res_rows + 2 * k + c) for c in range(2)]
        rows.append(jnp.concatenate([i_re, i_im], axis=1))
        rows.append(jnp.concatenate([i_im, -i_re], axis=1))
    probe_iter = dot3_t(split(jnp.concatenate(rows, axis=0)), probe)

    message[: 2 * rhs_dev, :] = jnp.zeros((2 * rhs_dev, LANES), f32)
    message[2 * rhs_dev : 3 * rhs_dev, :] = jnp.concatenate(
        [probe_res[:rhs_dev], probe_res[rhs_dev:]], axis=1
    )
    pieces = []
    for top in (0, rhs_dev):
        pieces.extend(probe_iter[q * cols + top : q * cols + top + rhs_dev] for q in range(res_rows))
    message[3 * rhs_dev :, :] = jnp.concatenate(pieces, axis=1)


def node_weight(here, scale, node_devs, node_dev, nodes_all, p, s, k):
    cosines, sines = [], []
    for x in range(node_devs):
        node = (x - s) % node_devs * node_dev + k
        power = x * MOM_DEV + p
        angle = np.float32(power + 1) * node_angle(node, nodes_all)
        cosines.append(float(np.cos(angle)))
        sines.append(float(np.sin(angle)))
    return scale * pick(here, cosines), scale * pick(here, sines)


def gram_kernel(own, other, res_hi, res_lo, ahead, message, prod_hi, prod_lo):
    node_dev, _, rhs_dev, _ = own.shape
    cols = 2 * rhs_dev
    for k in range(node_dev):
        for c in range(2):
            high, low = split(joined(own, other, (k, c)))
            top = (k * 2 + c) * cols
            prod_hi[top : top + cols, :] = high
            prod_lo[top : top + cols, :] = low
    sums = []
    for k in range(node_dev):
        top = k * 2 * cols
        left, right = [], []
        for p_ref, r_ref in ((prod_hi, res_hi), (prod_lo, res_lo)):
            product, source = p_ref[...], r_ref[: node_dev * 2 * cols, :]
            plain = side_by_side(product, top, cols)
            left.append(jnp.concatenate([plain, side_by_side(source, top, cols)], axis=0))
            right.append(jnp.concatenate([plain, turned(product, top, cols)], axis=0))
        sums.append(dot3_t(tuple(left), tuple(right)))
    gram = jnp.concatenate(sums, axis=1)
    message[:rhs_dev, :] = jnp.concatenate([gram[:rhs_dev], gram[rhs_dev:cols]], axis=1)
    message[rhs_dev:cols, :] = jnp.concatenate(
        [gram[cols : cols + rhs_dev], gram[cols + rhs_dev :]], axis=1
    )
    message[cols:, :] = ahead[cols:, :]


def finish_kernel(dims, *refs):
    node_devs, nodes_all, scale_factor = dims
    it = iter(refs)
    parts = [(next(it), next(it)) for _ in range(node_devs)]
    packs = [(next(it), next(it)) for _ in range(node_devs)]
    prod_hi, prod_lo, res_hi, res_lo, contour, next_out, mom_out, hankel_out = it
    node_dev, _, rhs_dev, width = next_out.shape
    cols = 2 * rhs_dev
    half = LANES // 2
    res_rows = 2 * node_dev
    here = lax.axis_index("nodes")

    first = lax.axis_index("rhs") == 0
    sums = [jnp.where(first, relayed[...], held[...]) for held, relayed in parts]
    if node_devs % 2:
        sums.append(sums[0])

    shape = (rhs_dev, LANES)
    lane = lax.broadcasted_iota(jnp.int32, shape, 1)
    low_half = lane < half
    base = (lane // (2 * cols)) * (2 * cols)
    spot = lax.rem(lane, cols)
    real_lane = lax.rem(lane, 2 * cols) < cols
    swapped = jnp.where(real_lane, lane + cols, lane - cols)
    sign = jnp.where(real_lane, -1.0, 1.0)

    def gathered(value, index):
        return jnp.take_along_axis(value, index, axis=1, mode="promise_in_bounds")

    solved, probe_res = [], []
    for g in range(len(sums) // 2):
        s0, s1 = sums[2 * g], sums[2 * g + 1]
        r0, r1 = pltpu.roll(s0, half, 1), pltpu.roll(s1, half, 1)
        v0, v1, v2 = [slice(i * rhs_dev, (i + 1) * rhs_dev) for i in range(3)]
        block = [
            jnp.where(low_half, s0[v0], r1[v0]),
            jnp.where(low_half, r0[v0], s1[v0]),
            jnp.where(
                low_half, jnp.where(first, s0[v1], r0[v1]), jnp.where(first, r1[v1], s1[v1])
            ),
        ]
        probe_res.append(
            jnp.concatenate(
                [jnp.where(low_half, s0[v2], r1[v2]), jnp.where(low_half, r0[v2], s1[v2])], axis=0
            )
        )
        inverse_diag = jnp.ones(shape, f32)
        for j in range(cols):
            at, r = divmod(j, rhs_dev)
            line = block[at][r : r + 1]
            crossed = (gathered(block[at], swapped) * sign)[r : r + 1]
            col_re = [gathered(b, base + j) for b in block[at:]]
            col_im = [gathered(b, base + cols + j) for b in block[at:]]
            inverse = 1.0 / col_re[0][r : r + 1]
            kept = (spot != j)[:1]
            scaled = jnp.where(kept, inverse, 0.0)
            f1, f2 = line * scaled, crossed * scaled
            for i in range(at, 3):
                block[i] = block[i] - (col_re[i - at] * f1 + col_im[i - at] * f2)
            inverse_diag = jnp.where(spot == j, inverse, inverse_diag)
        solved.append(block[2] * inverse_diag)

    coef = solved[0]
    cross = gathered(coef, swapped)
    plain = jnp.where(real_lane, coef, -coef)
    node_of = lane // (2 * cols)
    rows = []
    for k in range(node_dev):
        rows.append(jnp.where(node_of == k, plain, 0.0))
        rows.append(jnp.where(node_of == k, cross, 0.0))
    used = node_dev * 2 * cols
    left = split(jnp.concatenate(rows, axis=0)[:, :used])
    change = dot3_n(left, (prod_hi[...], prod_lo[...]))
    for k in range(node_dev):
        for c in range(2):
            top = (k * 2 + c) * rhs_dev
            next_out[k, c] = packs[0][0][2 * k + c] - change[top : top + rhs_dev]

    scale = contour[2:3, :] / nodes_all
    weighted = []
    for g, coef in enumerate(solved):
        cross = gathered(coef, swapped)
        rows = []
        for p in range(MOM_DEV):
            w_re = jnp.zeros(shape, f32)
            w_im = jnp.zeros(shape, f32)
            for i in range(2):
                s = 2 * g + i
                if s >= node_devs:
                    continue
                for k in range(node_dev):
                    n_re, n_im = node_weight(here, scale, node_devs, node_dev, nodes_all, p, s, k)
                    mine = node_of == i * node_dev + k
                    w_re = jnp.where(mine, n_re, w_re)
                    w_im = jnp.where(mine, n_im, w_im)
            rows.append(-sign * w_re * coef - w_im * cross)
            rows.append(-sign * w_im * coef + w_re * cross)
        weighted.append(jnp.concatenate(rows, axis=0))
    hankel = None
    products = None
    for g, value in enumerate(weighted):
        depth = min(LANES, node_devs * used - g * LANES)
        left = split(value)
        cut = tuple(part[:, :depth] for part in left)
        highs, lows = [], []
        for i in range(depth // used):
            s = 2 * g + i
            if s == 0:
                highs.append(res_hi[...])
                lows.append(res_lo[...])
                continue
            for q in range(res_rows):
                high, low = split(joined(packs[s][0], packs[s][1], q))
                highs.append(high)
                lows.append(low)
        term = dot3_n(cut, (jnp.concatenate(highs, axis=0), jnp.concatenate(lows, axis=0)))
        products = term if products is None else products + term
        term = dot3_t(left, split(probe_res[g]))
        hankel = term if hankel is None else hankel + term

    projected = []
    for s in range(node_devs):
        value = sums[s][3 * rhs_dev :]
        projected.append(jnp.where(first, value, pltpu.roll(value, half, 1)))
    wide = jnp.concatenate([scale] * (width // LANES), axis=1)
    for p in range(MOM_DEV):
        mom = [products[(2 * p + c) * rhs_dev : (2 * p + c + 1) * rhs_dev] for c in range(2)]
        han = [hankel[(2 * p + c) * rhs_dev : (2 * p + c + 1) * rhs_dev] for c in range(2)]
        for s in range(node_devs):
            for k in range(node_dev):
                w_re, w_im = node_weight(here, wide, node_devs, node_dev, nodes_all, p, s, k)
                i_re, i_im = packs[s][0][res_rows + 2 * k], packs[s][0][res_rows + 2 * k + 1]
                mom[0] = mom[0] + (w_re * i_re - w_im * i_im)
                mom[1] = mom[1] + (w_re * i_im + w_im * i_re)
                i_re, i_im = [
                    pltpu.roll(projected[s], LANES - (2 * k + c) * cols, 1)[:, :cols]
                    if k + c
                    else projected[s][:, :cols]
                    for c in range(2)
                ]
                w_re, w_im = w_re[:, :cols], w_im[:, :cols]
                han[0] = han[0] + (w_re * i_re - w_im * i_im)
                han[1] = han[1] + (w_re * i_im + w_im * i_re)
        for c in range(2):
            mom_out[p, c] = mom[c]
            hankel_out[p, c] = han[c] * scale_factor


def call(kernel, out_shape, args, in_specs=None, scratch=(), cost=None):
    args = tuple(args)
    multiple = isinstance(out_shape, (list, tuple))
    return pl.pallas_call(
        kernel,
        out_shape=out_shape,
        in_specs=[VMEM] * len(args) if in_specs is None else in_specs,
        out_specs=[VMEM] * len(out_shape) if multiple else VMEM,
        scratch_shapes=list(scratch),
        compiler_params=PARAMS,
        cost_estimate=cost,
    )(*args)


def struct(shape, dtype=f32):
    return jax.ShapeDtypeStruct(shape, dtype)


def per_device(
    residual,
    iterate,
    probe,
    contour,
    near_tiles,
    near_col,
    near_row,
    near_dest,
    far_right,
    far_col,
    far_rank,
    far_target,
    far_left,
):
    node_dev, _, rhs_dev, rows_dev = residual.shape
    tile_count, _, size, _ = near_tiles.shape
    far_count, _, rank, _ = far_right.shape
    blk_dev = rows_dev // size
    panel_devs = lax.axis_size("panels")
    node_devs = lax.axis_size("nodes")
    nodes_all = node_dev * node_devs
    vec_rows = 2 * node_dev * rhs_dev
    cols = 2 * rhs_dev
    res_rows = 2 * node_dev
    span = res_rows * cols

    part_rows = blk_dev * vec_rows + vec_rows
    copies = 6 + 1 + tile_count // TILE_CHUNK + 4
    pack_shape = (2 * res_rows + 2, rhs_dev, rows_dev)
    indices = (near_col, near_row, near_dest.reshape(tile_count), far_col, far_rank, far_target)
    shifted = panel_devs <= MOST_SHIFTS
    out_shape = [struct((part_rows, LANES))] * panel_devs if shifted else [struct((panel_devs, part_rows, LANES))]
    in_hbm = functools.partial(pltpu.with_memory_space_constraint, memory_space=pltpu.HBM)
    *terms, pack, fields, consts = call(
        functools.partial(terms_kernel, (panel_devs, blk_dev, shifted)),
        [*out_shape, struct(pack_shape), struct((res_rows, rhs_dev, rows_dev)), struct((8, LANES))],
        map(in_hbm, (
            *indices,
            contour,
            residual.reshape(res_rows, rhs_dev, rows_dev),
            iterate.reshape(res_rows, rhs_dev, rows_dev),
            probe,
            near_tiles,
            far_right,
        )),
        in_specs=[HBM] * 12,
        scratch=[
            *[pltpu.SMEM(index.shape, jnp.int32) for index in indices],
            pltpu.SMEM(contour.shape, f32),
            pltpu.VMEM(near_tiles.shape, bf16),
            pltpu.VMEM(far_right.shape, bf16),
            pltpu.VMEM((blk_dev, vec_rows, 2 * size), bf16),
            pltpu.VMEM((tile_count, vec_rows, size), f32),
            pltpu.VMEM((far_count * rank // LANES, blk_dev, vec_rows, LANES), f32),
            pltpu.VMEM((panel_devs * blk_dev, vec_rows, size), f32),
            pltpu.VMEM((panel_devs, vec_rows, LANES), f32),
            pltpu.SemaphoreType.DMA((copies,)),
        ],
    )

    if shifted:
        parts = terms[:1]
        for d in range(1, panel_devs):
            pairs = [(i, (i + d) % panel_devs) for i in range(panel_devs)]
            parts.append(lax.ppermute(terms[d], "panels", pairs))
    else:
        parts = [lax.all_to_all(terms[0], "panels", split_axis=0, concat_axis=0, tiled=True)]

    packs = [(pack, lax.ppermute(pack, "rhs", [(0, 1), (1, 0)]))]
    for s in range(1, node_devs):
        pairs = [(i, (i + s) % node_devs) for i in range(node_devs)]
        crossed = [(2 * i + c, 2 * j + 1 - c) for i, j in pairs for c in range(2)]
        packs.append((lax.ppermute(pack, "nodes", pairs), lax.ppermute(fields, ("nodes", "rhs"), crossed)))

    product = call(
        functools.partial(product_kernel, (node_devs, nodes_all)),
        struct(residual.shape),
        (*parts, far_left.transpose(0, 1, 3, 2), pack, consts),
    )
    res_hi, res_lo, ahead = call(
        ahead_kernel,
        [struct((span, rows_dev), bf16), struct((span, rows_dev), bf16), struct((4 * rhs_dev, LANES))],
        packs[0],
    )
    message, prod_hi, prod_lo = call(
        gram_kernel,
        [
            struct((4 * rhs_dev, LANES)),
            struct((span, rows_dev), bf16),
            struct((span, rows_dev), bf16),
        ],
        (product, lax.ppermute(product, "rhs", [(0, 1), (1, 0)]), res_hi, res_lo, ahead),
    )
    def last_core(pairs):
        return [p for i, j in pairs for p in ((2 * i, 2 * i), (2 * i + 1, 2 * j + 1))]

    if panel_devs & (panel_devs - 1):
        message = lax.psum(message, "panels")
    else:
        step = 1
        while step < panel_devs:
            pairs = last_core([(i, i ^ step) for i in range(panel_devs)])
            message = message + lax.ppermute(message, ("panels", "rhs"), pairs)
            step *= 2
    sums = [message]
    for s in range(1, node_devs):
        pairs = last_core([(i, (i + s) % node_devs) for i in range(node_devs)])
        sums.append(lax.ppermute(message, ("nodes", "rhs"), pairs))
    sums = [part for value in sums for part in (value, lax.ppermute(value, "rhs", [(0, 1), (1, 0)]))]
    scale_factor = 1.0 / math.sqrt(rows_dev * panel_devs)
    residual_next, moments, hankel = call(
        functools.partial(finish_kernel, (node_devs, nodes_all, scale_factor)),
        [
            struct(residual.shape),
            struct((MOM_DEV, 2, rhs_dev, rows_dev)),
            struct((MOM_DEV, 2, rhs_dev, cols)),
        ],
        (*sums, *[p for pair in packs for p in pair], prod_hi, prod_lo, res_hi, res_lo, consts),
    )
    return residual_next, moments, hankel.transpose(0, 1, 3, 2)


def solution(mesh):
    return jax.shard_map(
        per_device,
        mesh=mesh,
        in_specs=(
            P(("groups", "nodes"), None, "rhs", "panels"),
            P(("groups", "nodes"), None, "rhs", "panels"),
            P("groups", "rhs", "panels"),
            P("groups"),
            P(("groups", "panels"), None, None, None),
            P(("groups", "panels")),
            P(("groups", "panels")),
            P(("groups", "panels"), None),
            P(("groups", "panels"), None, None, None),
            P(("groups", "panels")),
            P(("groups", "panels")),
            P(("groups", "panels")),
            P(("groups", "panels"), None, None, None),
        ),
        out_specs=(
            P(("groups", "nodes"), None, "rhs", "panels"),
            P(("groups", "nodes"), None, "rhs", "panels"),
            P(("groups", "nodes"), None, None, "rhs"),
        ),
        check_vma=False,
    )
```

```python
import functools
import math

import jax
import jax.numpy as jnp
import numpy as np
from jax import lax
from jax.experimental import pallas as pl
from jax.experimental.pallas import tpu as pltpu
from jax.sharding import PartitionSpec as P

MOM_DEV = 2
LANES = 128
TILE_CHUNK = 4
MOST_SHIFTS = 8

f32 = jnp.float32
bf16 = jnp.bfloat16

PARAMS = pltpu.CompilerParams(vmem_limit_bytes=40 * 1024 * 1024)
VMEM = pl.BlockSpec(memory_space=pltpu.VMEM)
HBM = pl.BlockSpec(memory_space=pltpu.HBM)


def dot_t(left, right):
    return lax.dot_general(left, right, (((1,), (1,)), ((), ())), preferred_element_type=f32)


def dot_n(left, right):
    return lax.dot_general(left, right, (((1,), (0,)), ((), ())), preferred_element_type=f32)


def split(value):
    high = value.astype(bf16)
    return high, (value - high.astype(f32)).astype(bf16)


def dot3_t(left, right):
    (l_hi, l_lo), (r_hi, r_lo) = left, right
    rows = l_hi.shape[0]
    both = dot_t(jnp.concatenate([l_hi, l_lo], axis=0), r_hi)
    return both[:rows] + both[rows:] + dot_t(l_hi, r_lo)


def dot3_n(left, right):
    (l_hi, l_lo), (r_hi, r_lo) = left, right
    rows = l_hi.shape[0]
    both = dot_n(jnp.concatenate([l_hi, l_lo], axis=0), r_hi)
    return both[:rows] + both[rows:] + dot_n(l_hi, r_lo)


def pick(index, values):
    result = f32(values[0])
    for i in range(1, len(values)):
        result = jnp.where(index == i, f32(values[i]), result)
    return result


def node_angle(node, nodes_all):
    return np.float32(2.0 * math.pi) * (np.float32(node) + np.float32(0.5)) / np.float32(nodes_all)


def terms_kernel(dims, *refs):
    panel_devs, blk_dev, shifted = dims
    n_out = panel_devs if shifted else 1
    indices, (contour_hbm, res_hbm, iter_hbm, probe_hbm, tiles_hbm, fr_hbm) = refs[:6], refs[6:12]
    outs, refs = refs[12 : 12 + n_out], refs[12 + n_out :]
    (pack, fields, lines, consts), refs = refs[:4], refs[4:]
    held, (contour, tiles, fright, vec, terms, skel, acc, facc, sems) = refs[:6], refs[6:]
    tile_count = tiles.shape[0]
    far_count, _, rank, size = fright.shape
    res_rows, iter_rows = res_hbm.shape[0], iter_hbm.shape[0]
    node_dev = res_rows // 2
    chunk = TILE_CHUNK

    copies = []

    def start(source, target):
        copy = pltpu.make_async_copy(source, target, sems.at[len(copies)])
        copy.start()
        copies.append(copy)
        return copy

    res_copy = start(res_hbm, pack.at[pl.ds(0, res_rows)])
    small = [start(source, target) for source, target in zip(indices, held)]
    small.append(start(contour_hbm, contour))
    tile_copies = []
    for i in range(tile_count // chunk):
        part = pl.ds(i * chunk, chunk)
        tile_copies.append(start(tiles_hbm.at[part], tiles.at[part]))
    far_copy = start(fr_hbm, fright)
    rest = [
        start(iter_hbm, pack.at[pl.ds(res_rows, iter_rows)]),
        start(probe_hbm, lines.at[pl.ds(res_rows, 2)]),
    ]
    col, row, dest, fcol, frank, ftgt = held
    here = lax.axis_index("panels")

    def slot_of(owner):
        if shifted:
            owner = owner - here
            owner = jnp.where(owner < 0, owner + panel_devs, owner)
        return owner

    zero = jnp.zeros(acc.shape[1:], f32)
    for b in range(acc.shape[0]):
        acc[b] = zero
    for d in range(facc.shape[0]):
        facc[d] = zero

    res_copy.wait()
    for i in range(res_rows):
        fields[i] = pack[i]
        lines[i] = pack[i]
    for b in range(blk_dev):
        lanes = slice(b * size, (b + 1) * size)
        re = jnp.concatenate([pack[2 * k, :, lanes] for k in range(node_dev)], axis=0)
        im = jnp.concatenate([pack[2 * k + 1, :, lanes] for k in range(node_dev)], axis=0)
        upper = jnp.concatenate([re, -im], axis=1)
        lower = jnp.concatenate([im, re], axis=1)
        vec[b] = jnp.concatenate([upper, lower], axis=0).astype(bf16)

    for copy in small:
        copy.wait()
    for i in range(consts.shape[0]):
        consts[i : i + 1, :] = jnp.full((1, LANES), contour[min(i, 2)], f32)

    rows = vec.shape[1]
    for i, copy in enumerate(tile_copies):
        copy.wait()
        for t in range(i * chunk, (i + 1) * chunk):
            tile = jnp.concatenate([tiles[t, 0], tiles[t, 1]], axis=1)
            terms[t] = dot_t(vec[col[t]], tile)
    far_copy.wait()
    group = LANES // rank
    sources = vec[...].reshape(blk_dev * rows, 2 * size)
    for g in range(far_count // group):
        mats = [
            jnp.concatenate([fright[f, 0], fright[f, 1]], axis=1)
            for f in range(g * group, (g + 1) * group)
        ]
        skel[g] = dot_t(sources, jnp.concatenate(mats, axis=0)).reshape(blk_dev, rows, LANES)

    for t in range(tile_count):
        target = slot_of(dest[t]) * blk_dev + row[t]
        acc[target] = acc[target] + terms[t]
    lane = lax.broadcasted_iota(jnp.int32, (rows, LANES), 1)
    for f in range(far_count):
        target = ftgt[f]
        owner = target // blk_dev
        place = (target - owner * blk_dev) * rank
        moved = pltpu.roll(
            skel[f // group, fcol[f]], lax.rem(place - (f % group) * rank + LANES, LANES), 1
        )
        kept = (lane >= place) & (lane < place + frank[f])
        slot = slot_of(owner)
        facc[slot] = facc[slot] + jnp.where(kept, moved, 0.0)

    near_rows = blk_dev * rows
    for d in range(panel_devs):
        out = outs[d] if shifted else outs[0].at[d]
        for b in range(blk_dev):
            out[b * rows : (b + 1) * rows, :] = acc[d * blk_dev + b]
        out[near_rows:, :] = facc[d]
    for copy in rest:
        copy.wait()


def product_kernel(dims, *refs):
    node_devs, nodes_all = dims
    parts, (left, pack, contour, out) = refs[:-4], refs[-4:]
    parts = [p for part in parts for p in ([part[d] for d in range(part.shape[0])] if len(part.shape) == 3 else [part[...]])]
    node_dev, _, rhs_dev, _ = out.shape
    blk_dev, _, rank, size = left.shape
    rows = 2 * node_dev * rhs_dev
    half = rows // 2

    total = parts[0]
    for part in parts[1:]:
        total = total + part
    near = total[: blk_dev * rows]
    summed = total[blk_dev * rows :]
    re, im = summed[:half], summed[half:]
    upper = jnp.concatenate([re, -im], axis=1)
    lower = jnp.concatenate([im, re], axis=1)
    whole = jnp.concatenate([upper, lower], axis=0)
    lane = lax.broadcasted_iota(jnp.int32, whole.shape, 1)
    block = lax.rem(lane, LANES) // rank
    picked = [jnp.where(block == b, whole, 0.0) for b in range(blk_dev)]
    mats = left[...]
    stacked = jnp.concatenate(
        [mats[:, 0].reshape(blk_dev * rank, size), mats[:, 1].reshape(blk_dev * rank, size)], axis=0
    )
    applied = near + dot_n(jnp.concatenate(picked, axis=0).astype(bf16), stacked)

    here = lax.axis_index("nodes")
    for k in range(node_dev):
        cosines, sines = [], []
        for x in range(node_devs):
            angle = node_angle(x * node_dev + k, nodes_all)
            cosines.append(float(np.cos(angle)))
            sines.append(float(np.sin(angle)))
        shift_re = contour[0:1, :] + contour[2:3, :] * pick(here, cosines)
        shift_im = contour[1:2, :] + contour[2:3, :] * pick(here, sines)
        for b in range(blk_dev):
            lanes = slice(b * size, (b + 1) * size)
            top = b * rows + k * rhs_dev
            r_re, r_im = pack[2 * k, :, lanes], pack[2 * k + 1, :, lanes]
            out[k, 0, :, lanes] = applied[top : top + rhs_dev] - (shift_re * r_re - shift_im * r_im)
            top = top + half
            out[k, 1, :, lanes] = applied[top : top + rhs_dev] - (shift_re * r_im + shift_im * r_re)


def side_by_side(pair, row, count):
    return jnp.concatenate([pair[row : row + count], pair[row + count : row + 2 * count]], axis=1)


def turned(pair, row, count):
    return jnp.concatenate([-pair[row + count : row + 2 * count], pair[row : row + count]], axis=1)


def joined(own, other, row):
    first = lax.axis_index("rhs") == 0
    mine, theirs = own[row], other[row]
    top = jnp.where(first, mine, theirs)
    bottom = jnp.where(first, theirs, mine)
    return jnp.concatenate([top, bottom], axis=0)


def ahead_kernel(dims, *refs):
    node_devs, nodes_all = dims
    it = iter(refs)
    packs = [(next(it), next(it)) for _ in range(node_devs)]
    own, contour, res_hi, res_lo, mixed, message = it
    _, rhs_dev, width = own.shape
    cols = 2 * rhs_dev
    res_rows = own.shape[0] - 2
    node_dev = res_rows // 2
    span = res_rows * cols
    here = lax.axis_index("nodes")

    for s, (pack, other) in enumerate(packs):
        for i in range(res_rows):
            high, low = split(joined(pack, other, i))
            top = s * span + i * cols
            res_hi[top : top + cols, :] = high
            res_lo[top : top + cols, :] = low

    scale = jnp.concatenate([contour[2:3, :] / nodes_all] * (width // LANES), axis=1)
    for p in range(MOM_DEV):
        sum_re = jnp.zeros((rhs_dev, width), f32)
        sum_im = jnp.zeros((rhs_dev, width), f32)
        for s, (pack, _) in enumerate(packs):
            for k in range(node_dev):
                w_re, w_im = node_weight(here, scale, node_devs, node_dev, nodes_all, p, s, k)
                i_re, i_im = pack[res_rows + 2 * k], pack[res_rows + 2 * k + 1]
                sum_re = sum_re + (w_re * i_re - w_im * i_im)
                sum_im = sum_im + (w_re * i_im + w_im * i_re)
        mixed[p, 0] = sum_re
        mixed[p, 1] = sum_im

    probe = [joined(own, packs[0][1], res_rows + c) for c in range(2)]
    probe = split(jnp.concatenate(probe, axis=1))
    pair = []
    for held in (res_hi[:span, :], res_lo[:span, :]):
        rows = []
        for k in range(node_dev):
            rows.append(side_by_side(held, k * 2 * cols, cols))
            rows.append(-turned(held, k * 2 * cols, cols))
        pair.append(jnp.concatenate(rows, axis=0))
    probe_res = dot3_t(probe, tuple(pair))
    rows = []
    for p in range(MOM_DEV):
        rows.append(jnp.concatenate([mixed[p, 0], mixed[p, 1]], axis=1))
        rows.append(jnp.concatenate([mixed[p, 1], -mixed[p, 0]], axis=1))
    probe_mix = dot3_t(split(jnp.concatenate(rows, axis=0)), probe)

    message[:rhs_dev, :] = jnp.zeros((rhs_dev, LANES), f32)
    pieces = [jnp.zeros((rhs_dev, LANES // 2), f32)]
    pieces.extend(probe_mix[q * rhs_dev : (q + 1) * rhs_dev] for q in range(2 * MOM_DEV))
    message[rhs_dev:cols, :] = jnp.concatenate(pieces, axis=1)
    message[cols:, :] = jnp.concatenate([probe_res[:rhs_dev], probe_res[rhs_dev:]], axis=1)


def node_weight(here, scale, node_devs, node_dev, nodes_all, p, s, k):
    cosines, sines = [], []
    for x in range(node_devs):
        node = (x - s) % node_devs * node_dev + k
        power = x * MOM_DEV + p
        angle = np.float32(power + 1) * node_angle(node, nodes_all)
        cosines.append(float(np.cos(angle)))
        sines.append(float(np.sin(angle)))
    return scale * pick(here, cosines), scale * pick(here, sines)


def gram_kernel(own, other, res_hi, res_lo, ahead, message, prod_hi, prod_lo):
    node_dev, _, rhs_dev, _ = own.shape
    cols = 2 * rhs_dev
    for k in range(node_dev):
        for c in range(2):
            high, low = split(joined(own, other, (k, c)))
            top = (k * 2 + c) * cols
            prod_hi[top : top + cols, :] = high
            prod_lo[top : top + cols, :] = low
    sums = []
    for k in range(node_dev):
        top = k * 2 * cols
        left, right = [], []
        for p_ref, r_ref in ((prod_hi, res_hi), (prod_lo, res_lo)):
            product, source = p_ref[...], r_ref[: node_dev * 2 * cols, :]
            plain = side_by_side(product, top, cols)
            left.append(jnp.concatenate([plain, side_by_side(source, top, cols)], axis=0))
            right.append(jnp.concatenate([plain, turned(product, top, cols)], axis=0))
        sums.append(dot3_t(tuple(left), tuple(right)))
    gram = jnp.concatenate(sums, axis=1)
    half = LANES // 2
    first = lax.axis_index("rhs") == 0
    cross = jnp.where(first, gram[cols : cols + rhs_dev], gram[cols + rhs_dev :])
    message[:rhs_dev, :] = jnp.concatenate([gram[:rhs_dev], gram[rhs_dev:cols]], axis=1)
    message[rhs_dev:cols, :] = jnp.concatenate([cross, ahead[rhs_dev:cols, half:]], axis=1)
    message[cols:, :] = ahead[cols:, :]


def finish_kernel(dims, *refs):
    n_parts, node_devs, nodes_all, scale_factor = dims
    it = iter(refs)
    parts = [[next(it) for _ in range(n_parts)] for _ in range(node_devs)]
    pack, prod_hi, prod_lo, res_hi, res_lo, mixed, contour, next_out, mom_out, hankel_out = it
    node_dev, _, rhs_dev, width = next_out.shape
    cols = 2 * rhs_dev
    half = LANES // 2
    here = lax.axis_index("nodes")

    sums = [sum((part[...] for part in group[1:]), group[0][...]) for group in parts]
    if node_devs % 2:
        sums.append(sums[0])

    shape = (rhs_dev, LANES)
    lane = lax.broadcasted_iota(jnp.int32, shape, 1)
    low_half = lane < half
    base = (lane // (2 * cols)) * (2 * cols)
    spot = lax.rem(lane, cols)
    real_lane = lax.rem(lane, 2 * cols) < cols
    swapped = jnp.where(real_lane, lane + cols, lane - cols)
    sign = jnp.where(real_lane, -1.0, 1.0)

    def gathered(value, index):
        return jnp.take_along_axis(value, index, axis=1, mode="promise_in_bounds")

    solved, probe_res = [], []
    for g in range(len(sums) // 2):
        s0, s1 = sums[2 * g], sums[2 * g + 1]
        r0, r1 = pltpu.roll(s0, half, 1), pltpu.roll(s1, half, 1)
        v0, v1, v2 = [slice(i * rhs_dev, (i + 1) * rhs_dev) for i in range(3)]
        block = [
            jnp.where(low_half, s0[v0], r1[v0]),
            jnp.where(low_half, r0[v0], s1[v0]),
            jnp.where(low_half, s0[v1], r1[v1]),
        ]
        probe_res.append(
            jnp.concatenate(
                [jnp.where(low_half, s0[v2], r1[v2]), jnp.where(low_half, r0[v2], s1[v2])], axis=0
            )
        )
        inverse_diag = jnp.ones(shape, f32)
        for j in range(cols):
            at, r = divmod(j, rhs_dev)
            line = block[at][r : r + 1]
            crossed = (gathered(block[at], swapped) * sign)[r : r + 1]
            col_re = [gathered(b, base + j) for b in block[at:]]
            col_im = [gathered(b, base + cols + j) for b in block[at:]]
            inverse = 1.0 / col_re[0][r : r + 1]
            kept = (spot != j)[:1]
            scaled = jnp.where(kept, inverse, 0.0)
            f1, f2 = line * scaled, crossed * scaled
            for i in range(at, 3):
                block[i] = block[i] - (col_re[i - at] * f1 + col_im[i - at] * f2)
            inverse_diag = jnp.where(spot == j, inverse, inverse_diag)
        solved.append(block[2] * inverse_diag)

    coef = solved[0]
    cross = gathered(coef, swapped)
    plain = jnp.where(real_lane, coef, -coef)
    node_of = lane // (2 * cols)
    rows = []
    for k in range(node_dev):
        rows.append(jnp.where(node_of == k, plain, 0.0))
        rows.append(jnp.where(node_of == k, cross, 0.0))
    used = node_dev * 2 * cols
    left = split(jnp.concatenate(rows, axis=0)[:, :used])
    change = dot3_n(left, (prod_hi[...], prod_lo[...]))
    for k in range(node_dev):
        for c in range(2):
            top = (k * 2 + c) * rhs_dev
            next_out[k, c] = pack[2 * k + c] - change[top : top + rhs_dev]

    scale = contour[2:3, :] / nodes_all
    weighted = []
    for g, coef in enumerate(solved):
        cross = gathered(coef, swapped)
        rows = []
        for p in range(MOM_DEV):
            w_re = jnp.zeros(shape, f32)
            w_im = jnp.zeros(shape, f32)
            for i in range(2):
                s = 2 * g + i
                if s >= node_devs:
                    continue
                for k in range(node_dev):
                    n_re, n_im = node_weight(here, scale, node_devs, node_dev, nodes_all, p, s, k)
                    mine = node_of == i * node_dev + k
                    w_re = jnp.where(mine, n_re, w_re)
                    w_im = jnp.where(mine, n_im, w_im)
            rows.append(-sign * w_re * coef - w_im * cross)
            rows.append(-sign * w_im * coef + w_re * cross)
        weighted.append(jnp.concatenate(rows, axis=0))
    hankel = None
    total = jnp.concatenate([mixed[p, c] for p in range(MOM_DEV) for c in range(2)], axis=0)
    for g, value in enumerate(weighted):
        depth = min(LANES, node_devs * used - g * LANES)
        left = split(value)
        rows = slice(g * LANES, g * LANES + depth)
        cut = tuple(part[:, :depth] for part in left)
        total = total + dot3_n(cut, (res_hi[rows, :], res_lo[rows, :]))
        term = dot3_t(left, split(probe_res[g]))
        hankel = term if hankel is None else hankel + term
    for p in range(MOM_DEV):
        for c in range(2):
            q = 2 * p + c
            top = q * rhs_dev
            mom_out[p, c] = total[top : top + rhs_dev]
            moved = pltpu.roll(sums[0][rhs_dev:cols], half - q * cols, 1)[:, :cols]
            hankel_out[p, c] = (hankel[top : top + rhs_dev] + moved) * scale_factor


def call(kernel, out_shape, args, in_specs=None, scratch=(), cost=None):
    args = tuple(args)
    multiple = isinstance(out_shape, (list, tuple))
    return pl.pallas_call(
        kernel,
        out_shape=out_shape,
        in_specs=[VMEM] * len(args) if in_specs is None else in_specs,
        out_specs=[VMEM] * len(out_shape) if multiple else VMEM,
        scratch_shapes=list(scratch),
        compiler_params=PARAMS,
        cost_estimate=cost,
    )(*args)


def struct(shape, dtype=f32):
    return jax.ShapeDtypeStruct(shape, dtype)


def per_device(
    residual,
    iterate,
    probe,
    contour,
    near_tiles,
    near_col,
    near_row,
    near_dest,
    far_right,
    far_col,
    far_rank,
    far_target,
    far_left,
):
    node_dev, _, rhs_dev, rows_dev = residual.shape
    tile_count, _, size, _ = near_tiles.shape
    far_count, _, rank, _ = far_right.shape
    blk_dev = rows_dev // size
    panel_devs = lax.axis_size("panels")
    node_devs = lax.axis_size("nodes")
    nodes_all = node_dev * node_devs
    vec_rows = 2 * node_dev * rhs_dev
    cols = 2 * rhs_dev
    res_rows = 2 * node_dev
    span = res_rows * cols

    part_rows = blk_dev * vec_rows + vec_rows
    copies = 6 + 1 + tile_count // TILE_CHUNK + 4
    field = (rhs_dev, rows_dev)
    indices = (near_col, near_row, near_dest.reshape(tile_count), far_col, far_rank, far_target)
    shifted = panel_devs <= MOST_SHIFTS
    out_shape = [struct((part_rows, LANES))] * panel_devs if shifted else [struct((panel_devs, part_rows, LANES))]
    in_hbm = functools.partial(pltpu.with_memory_space_constraint, memory_space=pltpu.HBM)
    *terms, pack, fields, lines, consts = call(
        functools.partial(terms_kernel, (panel_devs, blk_dev, shifted)),
        [
            *out_shape,
            struct((2 * res_rows, *field)),
            struct((res_rows, *field)),
            struct((res_rows + 2, *field)),
            struct((8, LANES)),
        ],
        map(in_hbm, (
            *indices,
            contour,
            residual.reshape(res_rows, rhs_dev, rows_dev),
            iterate.reshape(res_rows, rhs_dev, rows_dev),
            probe,
            near_tiles,
            far_right,
        )),
        in_specs=[HBM] * 12,
        scratch=[
            *[pltpu.SMEM(index.shape, jnp.int32) for index in indices],
            pltpu.SMEM(contour.shape, f32),
            pltpu.VMEM(near_tiles.shape, bf16),
            pltpu.VMEM(far_right.shape, bf16),
            pltpu.VMEM((blk_dev, vec_rows, 2 * size), bf16),
            pltpu.VMEM((tile_count, vec_rows, size), f32),
            pltpu.VMEM((far_count * rank // LANES, blk_dev, vec_rows, LANES), f32),
            pltpu.VMEM((panel_devs * blk_dev, vec_rows, size), f32),
            pltpu.VMEM((panel_devs, vec_rows, LANES), f32),
            pltpu.SemaphoreType.DMA((copies,)),
        ],
    )

    if shifted:
        parts = terms[:1]
        for d in range(1, panel_devs):
            pairs = [(i, (i + d) % panel_devs) for i in range(panel_devs)]
            parts.append(lax.ppermute(terms[d], "panels", pairs))
    else:
        parts = [lax.all_to_all(terms[0], "panels", split_axis=0, concat_axis=0, tiled=True)]

    packs = [pack, lax.ppermute(lines, "rhs", [(0, 1), (1, 0)])]
    for s in range(1, node_devs):
        pairs = [(i, (i + s) % node_devs) for i in range(node_devs)]
        crossed = [(2 * i + c, 2 * j + 1 - c) for i, j in pairs for c in range(2)]
        packs.append(lax.ppermute(pack, "nodes", pairs))
        packs.append(lax.ppermute(fields, ("nodes", "rhs"), crossed))

    product = call(
        functools.partial(product_kernel, (node_devs, nodes_all)),
        struct(residual.shape),
        (*parts, far_left.transpose(0, 1, 3, 2), pack, consts),
    )
    res_hi, res_lo, mixed, ahead = call(
        functools.partial(ahead_kernel, (node_devs, nodes_all)),
        [
            struct((node_devs * span, rows_dev), bf16),
            struct((node_devs * span, rows_dev), bf16),
            struct((MOM_DEV, 2, rhs_dev, rows_dev)),
            struct((3 * rhs_dev, LANES)),
        ],
        (*packs, lines, consts),
    )
    message, prod_hi, prod_lo = call(
        gram_kernel,
        [
            struct((3 * rhs_dev, LANES)),
            struct((span, rows_dev), bf16),
            struct((span, rows_dev), bf16),
        ],
        (product, lax.ppermute(product, "rhs", [(0, 1), (1, 0)]), res_hi, res_lo, ahead),
    )
    if shifted:
        total = message
        for d in range(1, panel_devs):
            pairs = [(i, (i + d) % panel_devs) for i in range(panel_devs)]
            total = total + lax.ppermute(message, "panels", pairs)
    else:
        total = lax.psum(message, "panels")
    sums = [total]
    for s in range(1, node_devs):
        pairs = [(i, (i + s) % node_devs) for i in range(node_devs)]
        sums.append(lax.ppermute(total, "nodes", pairs))
    scale_factor = 1.0 / math.sqrt(rows_dev * panel_devs)
    residual_next, moments, hankel = call(
        functools.partial(finish_kernel, (1, node_devs, nodes_all, scale_factor)),
        [
            struct(residual.shape),
            struct((MOM_DEV, 2, rhs_dev, rows_dev)),
            struct((MOM_DEV, 2, rhs_dev, cols)),
        ],
        (*sums, pack, prod_hi, prod_lo, res_hi, res_lo, mixed, consts),
    )
    return residual_next, moments, hankel.transpose(0, 1, 3, 2)


def solution(mesh):
    return jax.shard_map(
        per_device,
        mesh=mesh,
        in_specs=(
            P(("groups", "nodes"), None, "rhs", "panels"),
            P(("groups", "nodes"), None, "rhs", "panels"),
            P("groups", "rhs", "panels"),
            P("groups"),
            P(("groups", "panels"), None, None, None),
            P(("groups", "panels")),
            P(("groups", "panels")),
            P(("groups", "panels"), None),
            P(("groups", "panels"), None, None, None),
            P(("groups", "panels")),
            P(("groups", "panels")),
            P(("groups", "panels")),
            P(("groups", "panels"), None, None, None),
        ),
        out_specs=(
            P(("groups", "nodes"), None, "rhs", "panels"),
            P(("groups", "nodes"), None, "rhs", "panels"),
            P(("groups", "nodes"), None, None, "rhs"),
        ),
        check_vma=False,
    )
```

```python
import functools
import math

import jax
import jax.numpy as jnp
import numpy as np
from jax import lax
from jax.experimental import pallas as pl
from jax.experimental.pallas import tpu as pltpu
from jax.sharding import PartitionSpec as P

MOM_DEV = 2
LANES = 128
TILE_CHUNK = 4
MOST_SHIFTS = 8

f32 = jnp.float32
bf16 = jnp.bfloat16

PARAMS = pltpu.CompilerParams(vmem_limit_bytes=40 * 1024 * 1024)
VMEM = pl.BlockSpec(memory_space=pltpu.VMEM)
HBM = pl.BlockSpec(memory_space=pltpu.HBM)


def dot_t(left, right):
    return lax.dot_general(left, right, (((1,), (1,)), ((), ())), preferred_element_type=f32)


def dot_n(left, right):
    return lax.dot_general(left, right, (((1,), (0,)), ((), ())), preferred_element_type=f32)


def split(value):
    high = value.astype(bf16)
    return high, (value - high.astype(f32)).astype(bf16)


def dot3_t(left, right):
    (l_hi, l_lo), (r_hi, r_lo) = left, right
    rows = l_hi.shape[0]
    both = dot_t(jnp.concatenate([l_hi, l_lo], axis=0), r_hi)
    return both[:rows] + both[rows:] + dot_t(l_hi, r_lo)


def dot3_n(left, right):
    (l_hi, l_lo), (r_hi, r_lo) = left, right
    rows = l_hi.shape[0]
    both = dot_n(jnp.concatenate([l_hi, l_lo], axis=0), r_hi)
    return both[:rows] + both[rows:] + dot_n(l_hi, r_lo)


def pick(index, values):
    result = f32(values[0])
    for i in range(1, len(values)):
        result = jnp.where(index == i, f32(values[i]), result)
    return result


def node_angle(node, nodes_all):
    return np.float32(2.0 * math.pi) * (np.float32(node) + np.float32(0.5)) / np.float32(nodes_all)


def terms_kernel(dims, *refs):
    panel_devs, blk_dev, shifted = dims
    n_out = panel_devs if shifted else 1
    indices, (contour_hbm, res_hbm, iter_hbm, probe_hbm, tiles_hbm, fr_hbm) = refs[:6], refs[6:12]
    outs, refs = refs[12 : 12 + n_out], refs[12 + n_out :]
    (pack, lines, consts), refs = refs[:3], refs[3:]
    held, (contour, tiles, fright, vec, terms, skel, acc, facc, sems) = refs[:6], refs[6:]
    tile_count = tiles.shape[0]
    far_count, _, rank, size = fright.shape
    res_rows, iter_rows = res_hbm.shape[0], iter_hbm.shape[0]
    node_dev = res_rows // 2
    chunk = TILE_CHUNK

    copies = []

    def start(source, target):
        copy = pltpu.make_async_copy(source, target, sems.at[len(copies)])
        copy.start()
        copies.append(copy)
        return copy

    res_copy = start(res_hbm, pack.at[pl.ds(0, res_rows)])
    small = [start(source, target) for source, target in zip(indices, held)]
    small.append(start(contour_hbm, contour))
    tile_copies = []
    for i in range(tile_count // chunk):
        part = pl.ds(i * chunk, chunk)
        tile_copies.append(start(tiles_hbm.at[part], tiles.at[part]))
    far_copy = start(fr_hbm, fright)
    rest = [
        start(iter_hbm, pack.at[pl.ds(res_rows, iter_rows)]),
        start(probe_hbm, lines.at[pl.ds(res_rows, 2)]),
    ]
    col, row, dest, fcol, frank, ftgt = held
    here = lax.axis_index("panels")

    def slot_of(owner):
        if shifted:
            owner = owner - here
            owner = jnp.where(owner < 0, owner + panel_devs, owner)
        return owner

    zero = jnp.zeros(acc.shape[1:], f32)
    for b in range(acc.shape[0]):
        acc[b] = zero
    for d in range(facc.shape[0]):
        facc[d] = zero

    res_copy.wait()
    for i in range(res_rows):
        lines[i] = pack[i]
    for b in range(blk_dev):
        lanes = slice(b * size, (b + 1) * size)
        re = jnp.concatenate([pack[2 * k, :, lanes] for k in range(node_dev)], axis=0)
        im = jnp.concatenate([pack[2 * k + 1, :, lanes] for k in range(node_dev)], axis=0)
        upper = jnp.concatenate([re, -im], axis=1)
        lower = jnp.concatenate([im, re], axis=1)
        vec[b] = jnp.concatenate([upper, lower], axis=0).astype(bf16)

    for copy in small:
        copy.wait()
    for i in range(consts.shape[0]):
        consts[i : i + 1, :] = jnp.full((1, LANES), contour[min(i, 2)], f32)

    rows = vec.shape[1]
    for i, copy in enumerate(tile_copies):
        copy.wait()
        for t in range(i * chunk, (i + 1) * chunk):
            tile = jnp.concatenate([tiles[t, 0], tiles[t, 1]], axis=1)
            terms[t] = dot_t(vec[col[t]], tile)
    far_copy.wait()
    group = LANES // rank
    sources = vec[...].reshape(blk_dev * rows, 2 * size)
    for g in range(far_count // group):
        mats = [
            jnp.concatenate([fright[f, 0], fright[f, 1]], axis=1)
            for f in range(g * group, (g + 1) * group)
        ]
        skel[g] = dot_t(sources, jnp.concatenate(mats, axis=0)).reshape(blk_dev, rows, LANES)

    for t in range(tile_count):
        target = slot_of(dest[t]) * blk_dev + row[t]
        acc[target] = acc[target] + terms[t]
    lane = lax.broadcasted_iota(jnp.int32, (rows, LANES), 1)
    for f in range(far_count):
        target = ftgt[f]
        owner = target // blk_dev
        place = (target - owner * blk_dev) * rank
        moved = pltpu.roll(
            skel[f // group, fcol[f]], lax.rem(place - (f % group) * rank + LANES, LANES), 1
        )
        kept = (lane >= place) & (lane < place + frank[f])
        slot = slot_of(owner)
        facc[slot] = facc[slot] + jnp.where(kept, moved, 0.0)

    near_rows = blk_dev * rows
    for d in range(panel_devs):
        out = outs[d] if shifted else outs[0].at[d]
        for b in range(blk_dev):
            out[b * rows : (b + 1) * rows, :] = acc[d * blk_dev + b]
        out[near_rows:, :] = facc[d]
    for copy in rest:
        copy.wait()


def product_kernel(dims, *refs):
    node_devs, nodes_all = dims
    parts, (left, pack, contour, out) = refs[:-4], refs[-4:]
    parts = [p for part in parts for p in ([part[d] for d in range(part.shape[0])] if len(part.shape) == 3 else [part[...]])]
    node_dev, _, rhs_dev, _ = out.shape
    blk_dev, _, rank, size = left.shape
    rows = 2 * node_dev * rhs_dev
    half = rows // 2

    total = parts[0]
    for part in parts[1:]:
        total = total + part
    near = total[: blk_dev * rows]
    summed = total[blk_dev * rows :]
    re, im = summed[:half], summed[half:]
    upper = jnp.concatenate([re, -im], axis=1)
    lower = jnp.concatenate([im, re], axis=1)
    whole = jnp.concatenate([upper, lower], axis=0)
    lane = lax.broadcasted_iota(jnp.int32, whole.shape, 1)
    block = lax.rem(lane, LANES) // rank
    picked = [jnp.where(block == b, whole, 0.0) for b in range(blk_dev)]
    mats = left[...]
    stacked = jnp.concatenate(
        [mats[:, 0].reshape(blk_dev * rank, size), mats[:, 1].reshape(blk_dev * rank, size)], axis=0
    )
    applied = near + dot_n(jnp.concatenate(picked, axis=0).astype(bf16), stacked)

    here = lax.axis_index("nodes")
    for k in range(node_dev):
        cosines, sines = [], []
        for x in range(node_devs):
            angle = node_angle(x * node_dev + k, nodes_all)
            cosines.append(float(np.cos(angle)))
            sines.append(float(np.sin(angle)))
        shift_re = contour[0:1, :] + contour[2:3, :] * pick(here, cosines)
        shift_im = contour[1:2, :] + contour[2:3, :] * pick(here, sines)
        for b in range(blk_dev):
            lanes = slice(b * size, (b + 1) * size)
            top = b * rows + k * rhs_dev
            r_re, r_im = pack[2 * k, :, lanes], pack[2 * k + 1, :, lanes]
            out[k, 0, :, lanes] = applied[top : top + rhs_dev] - (shift_re * r_re - shift_im * r_im)
            top = top + half
            out[k, 1, :, lanes] = applied[top : top + rhs_dev] - (shift_re * r_im + shift_im * r_re)


def side_by_side(pair, row, count):
    return jnp.concatenate([pair[row : row + count], pair[row + count : row + 2 * count]], axis=1)


def turned(pair, row, count):
    return jnp.concatenate([-pair[row + count : row + 2 * count], pair[row : row + count]], axis=1)


def joined(own, other, row):
    first = lax.axis_index("rhs") == 0
    mine, theirs = own[row], other[row]
    top = jnp.where(first, mine, theirs)
    bottom = jnp.where(first, theirs, mine)
    return jnp.concatenate([top, bottom], axis=0)


def ahead_kernel(pack, own, other, res_hi, res_lo, message):
    _, rhs_dev, _ = own.shape
    cols = 2 * rhs_dev
    res_rows = own.shape[0] - 2
    node_dev = res_rows // 2

    for i in range(res_rows):
        high, low = split(joined(own, other, i))
        res_hi[i * cols : (i + 1) * cols, :] = high
        res_lo[i * cols : (i + 1) * cols, :] = low

    probe = [joined(own, other, res_rows + c) for c in range(2)]
    probe = split(jnp.concatenate(probe, axis=1))
    pair = []
    for held in (res_hi[...], res_lo[...]):
        rows = []
        for k in range(node_dev):
            rows.append(side_by_side(held, k * 2 * cols, cols))
            rows.append(-turned(held, k * 2 * cols, cols))
        pair.append(jnp.concatenate(rows, axis=0))
    probe_res = dot3_t(probe, tuple(pair))
    rows = []
    for k in range(node_dev):
        i_re, i_im = pack[res_rows + 2 * k], pack[res_rows + 2 * k + 1]
        rows.append(jnp.concatenate([i_re, i_im], axis=1))
        rows.append(jnp.concatenate([i_im, -i_re], axis=1))
    probe_iter = dot3_t(split(jnp.concatenate(rows, axis=0)), probe)

    message[:rhs_dev, :] = jnp.zeros((rhs_dev, LANES), f32)
    pieces = [jnp.zeros((rhs_dev, LANES // 2), f32)]
    pieces.extend(probe_iter[q * rhs_dev : (q + 1) * rhs_dev] for q in range(res_rows))
    message[rhs_dev:cols, :] = jnp.concatenate(pieces, axis=1)
    message[cols:, :] = jnp.concatenate([probe_res[:rhs_dev], probe_res[rhs_dev:]], axis=1)


def node_weight(here, scale, node_devs, node_dev, nodes_all, p, s, k):
    cosines, sines = [], []
    for x in range(node_devs):
        node = (x - s) % node_devs * node_dev + k
        power = x * MOM_DEV + p
        angle = np.float32(power + 1) * node_angle(node, nodes_all)
        cosines.append(float(np.cos(angle)))
        sines.append(float(np.sin(angle)))
    return scale * pick(here, cosines), scale * pick(here, sines)


def gram_kernel(own, other, res_hi, res_lo, ahead, pack, lines, there, message, prod_hi, prod_lo, spread):
    node_dev, _, rhs_dev, _ = own.shape
    cols = 2 * rhs_dev
    for k in range(node_dev):
        for c in range(2):
            high, low = split(joined(own, other, (k, c)))
            top = (k * 2 + c) * cols
            prod_hi[top : top + cols, :] = high
            prod_lo[top : top + cols, :] = low
    sums = []
    for k in range(node_dev):
        top = k * 2 * cols
        left, right = [], []
        for p_ref, r_ref in ((prod_hi, res_hi), (prod_lo, res_lo)):
            product, source = p_ref[...], r_ref[: node_dev * 2 * cols, :]
            plain = side_by_side(product, top, cols)
            left.append(jnp.concatenate([plain, side_by_side(source, top, cols)], axis=0))
            right.append(jnp.concatenate([plain, turned(product, top, cols)], axis=0))
        sums.append(dot3_t(tuple(left), tuple(right)))
    gram = jnp.concatenate(sums, axis=1)
    half = LANES // 2
    first = lax.axis_index("rhs") == 0
    cross = jnp.where(first, gram[cols : cols + rhs_dev], gram[cols + rhs_dev :])
    message[:rhs_dev, :] = jnp.concatenate([gram[:rhs_dev], gram[rhs_dev:cols]], axis=1)
    message[rhs_dev:cols, :] = jnp.concatenate([cross, ahead[rhs_dev:cols, half:]], axis=1)
    message[cols:, :] = ahead[cols:, :]

    res_rows = 2 * node_dev
    for i in range(res_rows):
        both = joined(lines, there, i)
        spread[2 * i] = both[:rhs_dev]
        spread[2 * i + 1] = both[rhs_dev:]
        spread[2 * res_rows + i] = pack[res_rows + i]


def finish_kernel(dims, *refs):
    n_parts, node_devs, nodes_all, scale_factor = dims
    it = iter(refs)
    parts = [[next(it) for _ in range(n_parts)] for _ in range(node_devs)]
    spreads = [None] + [next(it) for _ in range(node_devs - 1)]
    pack, prod_hi, prod_lo, res_hi, res_lo, contour, next_out, mom_out, hankel_out = it
    node_dev, _, rhs_dev, width = next_out.shape
    cols = 2 * rhs_dev
    half = LANES // 2
    res_rows = 2 * node_dev
    here = lax.axis_index("nodes")

    sums = [sum((part[...] for part in group[1:]), group[0][...]) for group in parts]
    if node_devs % 2:
        sums.append(sums[0])

    shape = (rhs_dev, LANES)
    lane = lax.broadcasted_iota(jnp.int32, shape, 1)
    low_half = lane < half
    base = (lane // (2 * cols)) * (2 * cols)
    spot = lax.rem(lane, cols)
    real_lane = lax.rem(lane, 2 * cols) < cols
    swapped = jnp.where(real_lane, lane + cols, lane - cols)
    sign = jnp.where(real_lane, -1.0, 1.0)

    def gathered(value, index):
        return jnp.take_along_axis(value, index, axis=1, mode="promise_in_bounds")

    solved, probe_res = [], []
    for g in range(len(sums) // 2):
        s0, s1 = sums[2 * g], sums[2 * g + 1]
        r0, r1 = pltpu.roll(s0, half, 1), pltpu.roll(s1, half, 1)
        v0, v1, v2 = [slice(i * rhs_dev, (i + 1) * rhs_dev) for i in range(3)]
        block = [
            jnp.where(low_half, s0[v0], r1[v0]),
            jnp.where(low_half, r0[v0], s1[v0]),
            jnp.where(low_half, s0[v1], r1[v1]),
        ]
        probe_res.append(
            jnp.concatenate(
                [jnp.where(low_half, s0[v2], r1[v2]), jnp.where(low_half, r0[v2], s1[v2])], axis=0
            )
        )
        inverse_diag = jnp.ones(shape, f32)
        for j in range(cols):
            at, r = divmod(j, rhs_dev)
            line = block[at][r : r + 1]
            crossed = (gathered(block[at], swapped) * sign)[r : r + 1]
            col_re = [gathered(b, base + j) for b in block[at:]]
            col_im = [gathered(b, base + cols + j) for b in block[at:]]
            inverse = 1.0 / col_re[0][r : r + 1]
            kept = (spot != j)[:1]
            scaled = jnp.where(kept, inverse, 0.0)
            f1, f2 = line * scaled, crossed * scaled
            for i in range(at, 3):
                block[i] = block[i] - (col_re[i - at] * f1 + col_im[i - at] * f2)
            inverse_diag = jnp.where(spot == j, inverse, inverse_diag)
        solved.append(block[2] * inverse_diag)

    coef = solved[0]
    cross = gathered(coef, swapped)
    plain = jnp.where(real_lane, coef, -coef)
    node_of = lane // (2 * cols)
    rows = []
    for k in range(node_dev):
        rows.append(jnp.where(node_of == k, plain, 0.0))
        rows.append(jnp.where(node_of == k, cross, 0.0))
    used = node_dev * 2 * cols
    left = split(jnp.concatenate(rows, axis=0)[:, :used])
    change = dot3_n(left, (prod_hi[...], prod_lo[...]))
    for k in range(node_dev):
        for c in range(2):
            top = (k * 2 + c) * rhs_dev
            next_out[k, c] = pack[2 * k + c] - change[top : top + rhs_dev]

    scale = contour[2:3, :] / nodes_all
    weighted = []
    for g, coef in enumerate(solved):
        cross = gathered(coef, swapped)
        rows = []
        for p in range(MOM_DEV):
            w_re = jnp.zeros(shape, f32)
            w_im = jnp.zeros(shape, f32)
            for i in range(2):
                s = 2 * g + i
                if s >= node_devs:
                    continue
                for k in range(node_dev):
                    n_re, n_im = node_weight(here, scale, node_devs, node_dev, nodes_all, p, s, k)
                    mine = node_of == i * node_dev + k
                    w_re = jnp.where(mine, n_re, w_re)
                    w_im = jnp.where(mine, n_im, w_im)
            rows.append(-sign * w_re * coef - w_im * cross)
            rows.append(-sign * w_im * coef + w_re * cross)
        weighted.append(jnp.concatenate(rows, axis=0))
    hankel = None
    products = None
    for g, value in enumerate(weighted):
        depth = min(LANES, node_devs * used - g * LANES)
        left = split(value)
        cut = tuple(part[:, :depth] for part in left)
        highs, lows = [], []
        for i in range(depth // used):
            spread = spreads[2 * g + i]
            if spread is None:
                highs.append(res_hi[...])
                lows.append(res_lo[...])
                continue
            for q in range(res_rows):
                high, low = split(jnp.concatenate([spread[2 * q], spread[2 * q + 1]], axis=0))
                highs.append(high)
                lows.append(low)
        term = dot3_n(cut, (jnp.concatenate(highs, axis=0), jnp.concatenate(lows, axis=0)))
        products = term if products is None else products + term
        term = dot3_t(left, split(probe_res[g]))
        hankel = term if hankel is None else hankel + term

    wide = jnp.concatenate([scale] * (width // LANES), axis=1)
    for p in range(MOM_DEV):
        mom = [products[(2 * p + c) * rhs_dev : (2 * p + c + 1) * rhs_dev] for c in range(2)]
        han = [hankel[(2 * p + c) * rhs_dev : (2 * p + c + 1) * rhs_dev] for c in range(2)]
        for s in range(node_devs):
            for k in range(node_dev):
                w_re, w_im = node_weight(here, wide, node_devs, node_dev, nodes_all, p, s, k)
                held, top = (spreads[s], 2 * res_rows) if s else (pack, res_rows)
                i_re, i_im = held[top + 2 * k], held[top + 2 * k + 1]
                mom[0] = mom[0] + (w_re * i_re - w_im * i_im)
                mom[1] = mom[1] + (w_re * i_im + w_im * i_re)
                i_re, i_im = [
                    pltpu.roll(sums[s][rhs_dev:cols], half - (2 * k + c) * cols, 1)[:, :cols]
                    for c in range(2)
                ]
                w_re, w_im = w_re[:, :cols], w_im[:, :cols]
                han[0] = han[0] + (w_re * i_re - w_im * i_im)
                han[1] = han[1] + (w_re * i_im + w_im * i_re)
        for c in range(2):
            mom_out[p, c] = mom[c]
            hankel_out[p, c] = han[c] * scale_factor


def call(kernel, out_shape, args, in_specs=None, scratch=(), cost=None):
    args = tuple(args)
    multiple = isinstance(out_shape, (list, tuple))
    return pl.pallas_call(
        kernel,
        out_shape=out_shape,
        in_specs=[VMEM] * len(args) if in_specs is None else in_specs,
        out_specs=[VMEM] * len(out_shape) if multiple else VMEM,
        scratch_shapes=list(scratch),
        compiler_params=PARAMS,
        cost_estimate=cost,
    )(*args)


def struct(shape, dtype=f32):
    return jax.ShapeDtypeStruct(shape, dtype)


def per_device(
    residual,
    iterate,
    probe,
    contour,
    near_tiles,
    near_col,
    near_row,
    near_dest,
    far_right,
    far_col,
    far_rank,
    far_target,
    far_left,
):
    node_dev, _, rhs_dev, rows_dev = residual.shape
    tile_count, _, size, _ = near_tiles.shape
    far_count, _, rank, _ = far_right.shape
    blk_dev = rows_dev // size
    panel_devs = lax.axis_size("panels")
    node_devs = lax.axis_size("nodes")
    nodes_all = node_dev * node_devs
    vec_rows = 2 * node_dev * rhs_dev
    cols = 2 * rhs_dev
    res_rows = 2 * node_dev
    span = res_rows * cols

    part_rows = blk_dev * vec_rows + vec_rows
    copies = 6 + 1 + tile_count // TILE_CHUNK + 4
    field = (rhs_dev, rows_dev)
    indices = (near_col, near_row, near_dest.reshape(tile_count), far_col, far_rank, far_target)
    shifted = panel_devs <= MOST_SHIFTS
    out_shape = [struct((part_rows, LANES))] * panel_devs if shifted else [struct((panel_devs, part_rows, LANES))]
    in_hbm = functools.partial(pltpu.with_memory_space_constraint, memory_space=pltpu.HBM)
    *terms, pack, lines, consts = call(
        functools.partial(terms_kernel, (panel_devs, blk_dev, shifted)),
        [
            *out_shape,
            struct((2 * res_rows, *field)),
            struct((res_rows + 2, *field)),
            struct((8, LANES)),
        ],
        map(in_hbm, (
            *indices,
            contour,
            residual.reshape(res_rows, rhs_dev, rows_dev),
            iterate.reshape(res_rows, rhs_dev, rows_dev),
            probe,
            near_tiles,
            far_right,
        )),
        in_specs=[HBM] * 12,
        scratch=[
            *[pltpu.SMEM(index.shape, jnp.int32) for index in indices],
            pltpu.SMEM(contour.shape, f32),
            pltpu.VMEM(near_tiles.shape, bf16),
            pltpu.VMEM(far_right.shape, bf16),
            pltpu.VMEM((blk_dev, vec_rows, 2 * size), bf16),
            pltpu.VMEM((tile_count, vec_rows, size), f32),
            pltpu.VMEM((far_count * rank // LANES, blk_dev, vec_rows, LANES), f32),
            pltpu.VMEM((panel_devs * blk_dev, vec_rows, size), f32),
            pltpu.VMEM((panel_devs, vec_rows, LANES), f32),
            pltpu.SemaphoreType.DMA((copies,)),
        ],
    )

    if shifted:
        parts = terms[:1]
        for d in range(1, panel_devs):
            pairs = [(i, (i + d) % panel_devs) for i in range(panel_devs)]
            parts.append(lax.ppermute(terms[d], "panels", pairs))
    else:
        parts = [lax.all_to_all(terms[0], "panels", split_axis=0, concat_axis=0, tiled=True)]

    swap = [(0, 1), (1, 0)]
    there = lax.ppermute(lines, "rhs", swap)

    product = call(
        functools.partial(product_kernel, (node_devs, nodes_all)),
        struct(residual.shape),
        (*parts, far_left.transpose(0, 1, 3, 2), pack, consts),
    )
    res_hi, res_lo, ahead = call(
        ahead_kernel,
        [struct((span, rows_dev), bf16), struct((span, rows_dev), bf16), struct((3 * rhs_dev, LANES))],
        (pack, lines, there),
    )
    message, prod_hi, prod_lo, spread = call(
        gram_kernel,
        [
            struct((3 * rhs_dev, LANES)),
            struct((span, rows_dev), bf16),
            struct((span, rows_dev), bf16),
            struct((3 * res_rows, *field)),
        ],
        (product, lax.ppermute(product, "rhs", swap), res_hi, res_lo, ahead, pack, lines, there),
    )

    if shifted:
        total = message
        for d in range(1, panel_devs):
            pairs = [(i, (i + d) % panel_devs) for i in range(panel_devs)]
            total = total + lax.ppermute(message, "panels", pairs)
    else:
        total = lax.psum(message, "panels")
    sums, spreads = [total], []
    for s in range(1, node_devs):
        pairs = [(i, (i + s) % node_devs) for i in range(node_devs)]
        sums.append(lax.ppermute(total, "nodes", pairs))
        spreads.append(lax.ppermute(spread, "nodes", pairs))
    scale_factor = 1.0 / math.sqrt(rows_dev * panel_devs)
    residual_next, moments, hankel = call(
        functools.partial(finish_kernel, (1, node_devs, nodes_all, scale_factor)),
        [
            struct(residual.shape),
            struct((MOM_DEV, 2, rhs_dev, rows_dev)),
            struct((MOM_DEV, 2, rhs_dev, cols)),
        ],
        (*sums, *spreads, pack, prod_hi, prod_lo, res_hi, res_lo, consts),
    )
    return residual_next, moments, hankel.transpose(0, 1, 3, 2)


def solution(mesh):
    return jax.shard_map(
        per_device,
        mesh=mesh,
        in_specs=(
            P(("groups", "nodes"), None, "rhs", "panels"),
            P(("groups", "nodes"), None, "rhs", "panels"),
            P("groups", "rhs", "panels"),
            P("groups"),
            P(("groups", "panels"), None, None, None),
            P(("groups", "panels")),
            P(("groups", "panels")),
            P(("groups", "panels"), None),
            P(("groups", "panels"), None, None, None),
            P(("groups", "panels")),
            P(("groups", "panels")),
            P(("groups", "panels")),
            P(("groups", "panels"), None, None, None),
        ),
        out_specs=(
            P(("groups", "nodes"), None, "rhs", "panels"),
            P(("groups", "nodes"), None, "rhs", "panels"),
            P(("groups", "nodes"), None, None, "rhs"),
        ),
        check_vma=False,
    )
```

```python
import functools
import math

import jax
import jax.numpy as jnp
import numpy as np
from jax import lax
from jax.experimental import pallas as pl
from jax.experimental.pallas import tpu as pltpu
from jax.sharding import PartitionSpec as P

MOM_DEV = 2
LANES = 128
TILE_CHUNK = 4
MOST_SHIFTS = 8

f32 = jnp.float32
bf16 = jnp.bfloat16

PARAMS = pltpu.CompilerParams(vmem_limit_bytes=40 * 1024 * 1024)
VMEM = pl.BlockSpec(memory_space=pltpu.VMEM)
HBM = pl.BlockSpec(memory_space=pltpu.HBM)


def dot_t(left, right):
    return lax.dot_general(left, right, (((1,), (1,)), ((), ())), preferred_element_type=f32)


def dot_n(left, right):
    return lax.dot_general(left, right, (((1,), (0,)), ((), ())), preferred_element_type=f32)


def split(value):
    high = value.astype(bf16)
    return high, (value - high.astype(f32)).astype(bf16)


def dot3_t(left, right):
    (l_hi, l_lo), (r_hi, r_lo) = left, right
    rows = l_hi.shape[0]
    both = dot_t(jnp.concatenate([l_hi, l_lo], axis=0), r_hi)
    return both[:rows] + both[rows:] + dot_t(l_hi, r_lo)


def dot3_n(left, right):
    (l_hi, l_lo), (r_hi, r_lo) = left, right
    rows = l_hi.shape[0]
    both = dot_n(jnp.concatenate([l_hi, l_lo], axis=0), r_hi)
    return both[:rows] + both[rows:] + dot_n(l_hi, r_lo)


def pick(index, values):
    result = f32(values[0])
    for i in range(1, len(values)):
        result = jnp.where(index == i, f32(values[i]), result)
    return result


def node_angle(node, nodes_all):
    return np.float32(2.0 * math.pi) * (np.float32(node) + np.float32(0.5)) / np.float32(nodes_all)


def terms_kernel(dims, *refs):
    panel_devs, blk_dev, shifted = dims
    n_out = panel_devs if shifted else 1
    indices, (contour_hbm, res_hbm, iter_hbm, probe_hbm, tiles_hbm, fr_hbm) = refs[:6], refs[6:12]
    outs, refs = refs[12 : 12 + n_out], refs[12 + n_out :]
    (pack, consts), refs = refs[:2], refs[2:]
    held, (contour, tiles, fright, vec, terms, skel, acc, facc, sems) = refs[:6], refs[6:]
    tile_count = tiles.shape[0]
    far_count, _, rank, size = fright.shape
    res_rows, iter_rows = res_hbm.shape[0], iter_hbm.shape[0]
    node_dev = res_rows // 2
    chunk = TILE_CHUNK

    copies = []

    def start(source, target):
        copy = pltpu.make_async_copy(source, target, sems.at[len(copies)])
        copy.start()
        copies.append(copy)
        return copy

    res_copy = start(res_hbm, pack.at[pl.ds(0, res_rows)])
    small = [start(source, target) for source, target in zip(indices, held)]
    small.append(start(contour_hbm, contour))
    tile_copies = []
    for i in range(tile_count // chunk):
        part = pl.ds(i * chunk, chunk)
        tile_copies.append(start(tiles_hbm.at[part], tiles.at[part]))
    far_copy = start(fr_hbm, fright)
    rest = [
        start(iter_hbm, pack.at[pl.ds(res_rows, iter_rows)]),
        start(probe_hbm, pack.at[pl.ds(res_rows + iter_rows, 2)]),
    ]
    col, row, dest, fcol, frank, ftgt = held
    here = lax.axis_index("panels")

    def slot_of(owner):
        if shifted:
            owner = owner - here
            owner = jnp.where(owner < 0, owner + panel_devs, owner)
        return owner

    zero = jnp.zeros(acc.shape[1:], f32)
    for b in range(acc.shape[0]):
        acc[b] = zero
    for d in range(facc.shape[0]):
        facc[d] = zero

    res_copy.wait()
    for b in range(blk_dev):
        lanes = slice(b * size, (b + 1) * size)
        re = jnp.concatenate([pack[2 * k, :, lanes] for k in range(node_dev)], axis=0)
        im = jnp.concatenate([pack[2 * k + 1, :, lanes] for k in range(node_dev)], axis=0)
        upper = jnp.concatenate([re, -im], axis=1)
        lower = jnp.concatenate([im, re], axis=1)
        vec[b] = jnp.concatenate([upper, lower], axis=0).astype(bf16)

    for copy in small:
        copy.wait()
    for i in range(3):
        consts[i : i + 1, :] = jnp.full((1, LANES), contour[i], f32)
    core = lax.axis_index("rhs").astype(f32)
    consts[3:, :] = jnp.full((consts.shape[0] - 3, LANES), core, f32)

    rows = vec.shape[1]
    for i, copy in enumerate(tile_copies):
        copy.wait()
        for t in range(i * chunk, (i + 1) * chunk):
            tile = jnp.concatenate([tiles[t, 0], tiles[t, 1]], axis=1)
            terms[t] = dot_t(vec[col[t]], tile)
    far_copy.wait()
    group = LANES // rank
    sources = vec[...].reshape(blk_dev * rows, 2 * size)
    for g in range(far_count // group):
        mats = [
            jnp.concatenate([fright[f, 0], fright[f, 1]], axis=1)
            for f in range(g * group, (g + 1) * group)
        ]
        skel[g] = dot_t(sources, jnp.concatenate(mats, axis=0)).reshape(blk_dev, rows, LANES)

    for t in range(tile_count):
        target = slot_of(dest[t]) * blk_dev + row[t]
        acc[target] = acc[target] + terms[t]
    lane = lax.broadcasted_iota(jnp.int32, (rows, LANES), 1)
    for f in range(far_count):
        target = ftgt[f]
        owner = target // blk_dev
        place = (target - owner * blk_dev) * rank
        moved = pltpu.roll(
            skel[f // group, fcol[f]], lax.rem(place - (f % group) * rank + LANES, LANES), 1
        )
        kept = (lane >= place) & (lane < place + frank[f])
        slot = slot_of(owner)
        facc[slot] = facc[slot] + jnp.where(kept, moved, 0.0)

    near_rows = blk_dev * rows
    for d in range(panel_devs):
        out = outs[d] if shifted else outs[0].at[d]
        for b in range(blk_dev):
            out[b * rows : (b + 1) * rows, :] = acc[d * blk_dev + b]
        out[near_rows:, :] = facc[d]
    for copy in rest:
        copy.wait()


def product_kernel(dims, *refs):
    node_devs, nodes_all = dims
    parts, (left, pack, contour, out) = refs[:-4], refs[-4:]
    parts = [p for part in parts for p in ([part[d] for d in range(part.shape[0])] if len(part.shape) == 3 else [part[...]])]
    node_dev, _, rhs_dev, _ = out.shape
    blk_dev, _, rank, size = left.shape
    rows = 2 * node_dev * rhs_dev
    half = rows // 2

    total = parts[0]
    for part in parts[1:]:
        total = total + part
    near = total[: blk_dev * rows]
    summed = total[blk_dev * rows :]
    re, im = summed[:half], summed[half:]
    upper = jnp.concatenate([re, -im], axis=1)
    lower = jnp.concatenate([im, re], axis=1)
    whole = jnp.concatenate([upper, lower], axis=0)
    lane = lax.broadcasted_iota(jnp.int32, whole.shape, 1)
    block = lax.rem(lane, LANES) // rank
    picked = [jnp.where(block == b, whole, 0.0) for b in range(blk_dev)]
    mats = left[...]
    stacked = jnp.concatenate(
        [mats[:, 0].reshape(blk_dev * rank, size), mats[:, 1].reshape(blk_dev * rank, size)], axis=0
    )
    applied = near + dot_n(jnp.concatenate(picked, axis=0).astype(bf16), stacked)

    here = lax.axis_index("nodes")
    for k in range(node_dev):
        cosines, sines = [], []
        for x in range(node_devs):
            angle = node_angle(x * node_dev + k, nodes_all)
            cosines.append(float(np.cos(angle)))
            sines.append(float(np.sin(angle)))
        shift_re = contour[0:1, :] + contour[2:3, :] * pick(here, cosines)
        shift_im = contour[1:2, :] + contour[2:3, :] * pick(here, sines)
        for b in range(blk_dev):
            lanes = slice(b * size, (b + 1) * size)
            top = b * rows + k * rhs_dev
            r_re, r_im = pack[2 * k, :, lanes], pack[2 * k + 1, :, lanes]
            out[k, 0, :, lanes] = applied[top : top + rhs_dev] - (shift_re * r_re - shift_im * r_im)
            top = top + half
            out[k, 1, :, lanes] = applied[top : top + rhs_dev] - (shift_re * r_im + shift_im * r_re)


def side_by_side(pair, row, count):
    return jnp.concatenate([pair[row : row + count], pair[row + count : row + 2 * count]], axis=1)


def turned(pair, row, count):
    return jnp.concatenate([-pair[row + count : row + 2 * count], pair[row : row + count]], axis=1)


def joined(own, other, row):
    first = lax.axis_index("rhs") == 0
    mine, theirs = own[row], other[row]
    top = jnp.where(first, mine, theirs)
    bottom = jnp.where(first, theirs, mine)
    return jnp.concatenate([top, bottom], axis=0)


def ahead_kernel(own, other, res_hi, res_lo, message):
    _, rhs_dev, _ = own.shape
    cols = 2 * rhs_dev
    res_rows = res_hi.shape[0] // cols
    node_dev = res_rows // 2

    for i in range(res_rows):
        high, low = split(joined(own, other, i))
        res_hi[i * cols : (i + 1) * cols, :] = high
        res_lo[i * cols : (i + 1) * cols, :] = low

    probe = [joined(own, other, 2 * res_rows + c) for c in range(2)]
    probe = split(jnp.concatenate(probe, axis=1))
    pair = []
    for held in (res_hi[...], res_lo[...]):
        rows = []
        for k in range(node_dev):
            rows.append(side_by_side(held, k * 2 * cols, cols))
            rows.append(-turned(held, k * 2 * cols, cols))
        pair.append(jnp.concatenate(rows, axis=0))
    probe_res = dot3_t(probe, tuple(pair))
    rows = []
    for k in range(node_dev):
        i_re, i_im = [joined(own, other, res_rows + 2 * k + c) for c in range(2)]
        rows.append(jnp.concatenate([i_re, i_im], axis=1))
        rows.append(jnp.concatenate([i_im, -i_re], axis=1))
    probe_iter = dot3_t(split(jnp.concatenate(rows, axis=0)), probe)

    message[: 2 * rhs_dev, :] = jnp.zeros((2 * rhs_dev, LANES), f32)
    message[2 * rhs_dev : 3 * rhs_dev, :] = jnp.concatenate(
        [probe_res[:rhs_dev], probe_res[rhs_dev:]], axis=1
    )
    pieces = []
    for top in (0, rhs_dev):
        pieces.extend(probe_iter[q * cols + top : q * cols + top + rhs_dev] for q in range(res_rows))
    message[3 * rhs_dev :, :] = jnp.concatenate(pieces, axis=1)


def node_weight(here, scale, node_devs, node_dev, nodes_all, p, s, k):
    cosines, sines = [], []
    for x in range(node_devs):
        node = (x - s) % node_devs * node_dev + k
        power = x * MOM_DEV + p
        angle = np.float32(power + 1) * node_angle(node, nodes_all)
        cosines.append(float(np.cos(angle)))
        sines.append(float(np.sin(angle)))
    return scale * pick(here, cosines), scale * pick(here, sines)


def gram_kernel(own, other, res_hi, res_lo, ahead, pack, there, message, prod_hi, prod_lo, spread):
    node_dev, _, rhs_dev, _ = own.shape
    cols = 2 * rhs_dev
    for k in range(node_dev):
        for c in range(2):
            high, low = split(joined(own, other, (k, c)))
            top = (k * 2 + c) * cols
            prod_hi[top : top + cols, :] = high
            prod_lo[top : top + cols, :] = low
    sums = []
    for k in range(node_dev):
        top = k * 2 * cols
        left, right = [], []
        for p_ref, r_ref in ((prod_hi, res_hi), (prod_lo, res_lo)):
            product, source = p_ref[...], r_ref[: node_dev * 2 * cols, :]
            plain = side_by_side(product, top, cols)
            left.append(jnp.concatenate([plain, side_by_side(source, top, cols)], axis=0))
            right.append(jnp.concatenate([plain, turned(product, top, cols)], axis=0))
        sums.append(dot3_t(tuple(left), tuple(right)))
    gram = jnp.concatenate(sums, axis=1)
    message[:rhs_dev, :] = jnp.concatenate([gram[:rhs_dev], gram[rhs_dev:cols]], axis=1)
    message[rhs_dev:cols, :] = jnp.concatenate(
        [gram[cols : cols + rhs_dev], gram[cols + rhs_dev :]], axis=1
    )
    message[cols:, :] = ahead[cols:, :]

    res_rows = 2 * node_dev
    for i in range(res_rows):
        both = joined(pack, there, i)
        spread[2 * i] = both[:rhs_dev]
        spread[2 * i + 1] = both[rhs_dev:]
        spread[2 * res_rows + i] = pack[res_rows + i]


def finish_kernel(dims, *refs):
    paired, node_devs, nodes_all, scale_factor = dims
    it = iter(refs)
    parts = [next(it) for _ in range(node_devs)]
    spreads = [None] + [next(it) for _ in range(node_devs - 1)]
    pack, prod_hi, prod_lo, res_hi, res_lo, contour, next_out, mom_out, hankel_out = it
    node_dev, _, rhs_dev, width = next_out.shape
    cols = 2 * rhs_dev
    half = LANES // 2
    res_rows = 2 * node_dev
    here = lax.axis_index("nodes")

    first = lax.axis_index("rhs") == 0
    sums = [part[...] for part in parts]
    if paired:
        held, handed = sums
        sums = [jnp.where(first, handed, held), jnp.where(first, held, handed)]
    if node_devs % 2:
        sums.append(sums[0])

    shape = (rhs_dev, LANES)
    lane = lax.broadcasted_iota(jnp.int32, shape, 1)
    low_half = lane < half
    base = (lane // (2 * cols)) * (2 * cols)
    spot = lax.rem(lane, cols)
    real_lane = lax.rem(lane, 2 * cols) < cols
    swapped = jnp.where(real_lane, lane + cols, lane - cols)
    sign = jnp.where(real_lane, -1.0, 1.0)

    def gathered(value, index):
        return jnp.take_along_axis(value, index, axis=1, mode="promise_in_bounds")

    solved, probe_res = [], []
    for g in range(len(sums) // 2):
        s0, s1 = sums[2 * g], sums[2 * g + 1]
        r0, r1 = pltpu.roll(s0, half, 1), pltpu.roll(s1, half, 1)
        v0, v1, v2 = [slice(i * rhs_dev, (i + 1) * rhs_dev) for i in range(3)]
        block = [
            jnp.where(low_half, s0[v0], r1[v0]),
            jnp.where(low_half, r0[v0], s1[v0]),
            jnp.where(
                low_half, jnp.where(first, s0[v1], r0[v1]), jnp.where(first, r1[v1], s1[v1])
            ),
        ]
        probe_res.append(
            jnp.concatenate(
                [jnp.where(low_half, s0[v2], r1[v2]), jnp.where(low_half, r0[v2], s1[v2])], axis=0
            )
        )
        inverse_diag = jnp.ones(shape, f32)
        for j in range(cols):
            at, r = divmod(j, rhs_dev)
            line = block[at][r : r + 1]
            crossed = (gathered(block[at], swapped) * sign)[r : r + 1]
            col_re = [gathered(b, base + j) for b in block[at:]]
            col_im = [gathered(b, base + cols + j) for b in block[at:]]
            inverse = 1.0 / col_re[0][r : r + 1]
            kept = (spot != j)[:1]
            scaled = jnp.where(kept, inverse, 0.0)
            f1, f2 = line * scaled, crossed * scaled
            for i in range(at, 3):
                block[i] = block[i] - (col_re[i - at] * f1 + col_im[i - at] * f2)
            inverse_diag = jnp.where(spot == j, inverse, inverse_diag)
        solved.append(block[2] * inverse_diag)

    coef = solved[0]
    cross = gathered(coef, swapped)
    plain = jnp.where(real_lane, coef, -coef)
    node_of = lane // (2 * cols)
    rows = []
    for k in range(node_dev):
        rows.append(jnp.where(node_of == k, plain, 0.0))
        rows.append(jnp.where(node_of == k, cross, 0.0))
    used = node_dev * 2 * cols
    left = split(jnp.concatenate(rows, axis=0)[:, :used])
    change = dot3_n(left, (prod_hi[...], prod_lo[...]))
    for k in range(node_dev):
        for c in range(2):
            top = (k * 2 + c) * rhs_dev
            next_out[k, c] = pack[2 * k + c] - change[top : top + rhs_dev]

    scale = contour[2:3, :] / nodes_all
    weighted = []
    for g, coef in enumerate(solved):
        cross = gathered(coef, swapped)
        rows = []
        for p in range(MOM_DEV):
            w_re = jnp.zeros(shape, f32)
            w_im = jnp.zeros(shape, f32)
            for i in range(2):
                s = 2 * g + i
                if s >= node_devs:
                    continue
                for k in range(node_dev):
                    n_re, n_im = node_weight(here, scale, node_devs, node_dev, nodes_all, p, s, k)
                    mine = node_of == i * node_dev + k
                    w_re = jnp.where(mine, n_re, w_re)
                    w_im = jnp.where(mine, n_im, w_im)
            rows.append(-sign * w_re * coef - w_im * cross)
            rows.append(-sign * w_im * coef + w_re * cross)
        weighted.append(jnp.concatenate(rows, axis=0))
    hankel = None
    products = None
    for g, value in enumerate(weighted):
        depth = min(LANES, node_devs * used - g * LANES)
        left = split(value)
        cut = tuple(part[:, :depth] for part in left)
        highs, lows = [], []
        for i in range(depth // used):
            spread = spreads[2 * g + i]
            if spread is None:
                highs.append(res_hi[...])
                lows.append(res_lo[...])
                continue
            for q in range(res_rows):
                high, low = split(jnp.concatenate([spread[2 * q], spread[2 * q + 1]], axis=0))
                highs.append(high)
                lows.append(low)
        term = dot3_n(cut, (jnp.concatenate(highs, axis=0), jnp.concatenate(lows, axis=0)))
        products = term if products is None else products + term
        term = dot3_t(left, split(probe_res[g]))
        hankel = term if hankel is None else hankel + term

    projected = []
    for s in range(node_devs):
        value = sums[s][3 * rhs_dev :]
        projected.append(jnp.where(first, value, pltpu.roll(value, half, 1)))
    wide = jnp.concatenate([scale] * (width // LANES), axis=1)
    for p in range(MOM_DEV):
        mom = [products[(2 * p + c) * rhs_dev : (2 * p + c + 1) * rhs_dev] for c in range(2)]
        han = [hankel[(2 * p + c) * rhs_dev : (2 * p + c + 1) * rhs_dev] for c in range(2)]
        for s in range(node_devs):
            for k in range(node_dev):
                w_re, w_im = node_weight(here, wide, node_devs, node_dev, nodes_all, p, s, k)
                held, top = (spreads[s], 2 * res_rows) if s else (pack, res_rows)
                i_re, i_im = held[top + 2 * k], held[top + 2 * k + 1]
                mom[0] = mom[0] + (w_re * i_re - w_im * i_im)
                mom[1] = mom[1] + (w_re * i_im + w_im * i_re)
                i_re, i_im = [
                    pltpu.roll(projected[s], LANES - (2 * k + c) * cols, 1)[:, :cols]
                    if k + c
                    else projected[s][:, :cols]
                    for c in range(2)
                ]
                w_re, w_im = w_re[:, :cols], w_im[:, :cols]
                han[0] = han[0] + (w_re * i_re - w_im * i_im)
                han[1] = han[1] + (w_re * i_im + w_im * i_re)
        for c in range(2):
            mom_out[p, c] = mom[c]
            hankel_out[p, c] = han[c] * scale_factor


def call(kernel, out_shape, args, in_specs=None, scratch=(), cost=None):
    args = tuple(args)
    multiple = isinstance(out_shape, (list, tuple))
    return pl.pallas_call(
        kernel,
        out_shape=out_shape,
        in_specs=[VMEM] * len(args) if in_specs is None else in_specs,
        out_specs=[VMEM] * len(out_shape) if multiple else VMEM,
        scratch_shapes=list(scratch),
        compiler_params=PARAMS,
        cost_estimate=cost,
    )(*args)


def struct(shape, dtype=f32):
    return jax.ShapeDtypeStruct(shape, dtype)


def per_device(
    residual,
    iterate,
    probe,
    contour,
    near_tiles,
    near_col,
    near_row,
    near_dest,
    far_right,
    far_col,
    far_rank,
    far_target,
    far_left,
):
    node_dev, _, rhs_dev, rows_dev = residual.shape
    tile_count, _, size, _ = near_tiles.shape
    far_count, _, rank, _ = far_right.shape
    blk_dev = rows_dev // size
    panel_devs = lax.axis_size("panels")
    node_devs = lax.axis_size("nodes")
    nodes_all = node_dev * node_devs
    vec_rows = 2 * node_dev * rhs_dev
    cols = 2 * rhs_dev
    res_rows = 2 * node_dev
    span = res_rows * cols

    part_rows = blk_dev * vec_rows + vec_rows
    copies = 6 + 1 + tile_count // TILE_CHUNK + 4
    field = (rhs_dev, rows_dev)
    indices = (near_col, near_row, near_dest.reshape(tile_count), far_col, far_rank, far_target)
    shifted = panel_devs <= MOST_SHIFTS
    out_shape = [struct((part_rows, LANES))] * panel_devs if shifted else [struct((panel_devs, part_rows, LANES))]
    in_hbm = functools.partial(pltpu.with_memory_space_constraint, memory_space=pltpu.HBM)
    *terms, pack, consts = call(
        functools.partial(terms_kernel, (panel_devs, blk_dev, shifted)),
        [
            *out_shape,
            struct((2 * res_rows + 2, *field)),
            struct((8, LANES)),
        ],
        map(in_hbm, (
            *indices,
            contour,
            residual.reshape(res_rows, rhs_dev, rows_dev),
            iterate.reshape(res_rows, rhs_dev, rows_dev),
            probe,
            near_tiles,
            far_right,
        )),
        in_specs=[HBM] * 12,
        scratch=[
            *[pltpu.SMEM(index.shape, jnp.int32) for index in indices],
            pltpu.SMEM(contour.shape, f32),
            pltpu.VMEM(near_tiles.shape, bf16),
            pltpu.VMEM(far_right.shape, bf16),
            pltpu.VMEM((blk_dev, vec_rows, 2 * size), bf16),
            pltpu.VMEM((tile_count, vec_rows, size), f32),
            pltpu.VMEM((far_count * rank // LANES, blk_dev, vec_rows, LANES), f32),
            pltpu.VMEM((panel_devs * blk_dev, vec_rows, size), f32),
            pltpu.VMEM((panel_devs, vec_rows, LANES), f32),
            pltpu.SemaphoreType.DMA((copies,)),
        ],
    )

    if shifted:
        parts = terms[:1]
        for d in range(1, panel_devs):
            pairs = [(i, (i + d) % panel_devs) for i in range(panel_devs)]
            parts.append(lax.ppermute(terms[d], "panels", pairs))
    else:
        parts = [lax.all_to_all(terms[0], "panels", split_axis=0, concat_axis=0, tiled=True)]

    swap = [(0, 1), (1, 0)]
    there = lax.ppermute(pack, "rhs", swap)

    product = call(
        functools.partial(product_kernel, (node_devs, nodes_all)),
        struct(residual.shape),
        (*parts, far_left.transpose(0, 1, 3, 2), pack, consts),
    )
    res_hi, res_lo, ahead = call(
        ahead_kernel,
        [struct((span, rows_dev), bf16), struct((span, rows_dev), bf16), struct((4 * rhs_dev, LANES))],
        (pack, there),
    )
    message, prod_hi, prod_lo, spread = call(
        gram_kernel,
        [
            struct((4 * rhs_dev, LANES)),
            struct((span, rows_dev), bf16),
            struct((span, rows_dev), bf16),
            struct((3 * res_rows, *field)),
        ],
        (product, lax.ppermute(product, "rhs", swap), res_hi, res_lo, ahead, pack, there),
    )

    node_pairs = [[(i, (i + s) % node_devs) for i in range(node_devs)] for s in range(node_devs)]
    spreads = [lax.ppermute(spread, "nodes", pairs) for pairs in node_pairs[1:]]
    paired = shifted and panel_devs > 1 and node_devs == 2
    if paired:
        arrived = []
        for d in range(panel_devs):
            pairs = []
            for z, x, c in np.ndindex(panel_devs, 2, 2):
                to_z = (z + (d or c)) % panel_devs
                to_x = x if c else 1 - x
                pairs.append(((z * 2 + x) * 2 + c, (to_z * 2 + to_x) * 2 + c))
            arrived.append(lax.ppermute(message, ("panels", "nodes", "rhs"), pairs))
        held = jnp.where(consts[3:4, :] > 0.5, message, arrived[0])
        for value in arrived[1:]:
            held = held + value
        sums = [held, lax.ppermute(held, "rhs", swap)]
    else:
        total = lax.psum(message, "panels")
        sums = [total] + [lax.ppermute(total, "nodes", pairs) for pairs in node_pairs[1:]]
    scale_factor = 1.0 / math.sqrt(rows_dev * panel_devs)
    residual_next, moments, hankel = call(
        functools.partial(finish_kernel, (paired, node_devs, nodes_all, scale_factor)),
        [
            struct(residual.shape),
            struct((MOM_DEV, 2, rhs_dev, rows_dev)),
            struct((MOM_DEV, 2, rhs_dev, cols)),
        ],
        (*sums, *spreads, pack, prod_hi, prod_lo, res_hi, res_lo, consts),
    )
    return residual_next, moments, hankel.transpose(0, 1, 3, 2)


def solution(mesh):
    return jax.shard_map(
        per_device,
        mesh=mesh,
        in_specs=(
            P(("groups", "nodes"), None, "rhs", "panels"),
            P(("groups", "nodes"), None, "rhs", "panels"),
            P("groups", "rhs", "panels"),
            P("groups"),
            P(("groups", "panels"), None, None, None),
            P(("groups", "panels")),
            P(("groups", "panels")),
            P(("groups", "panels"), None),
            P(("groups", "panels"), None, None, None),
            P(("groups", "panels")),
            P(("groups", "panels")),
            P(("groups", "panels")),
            P(("groups", "panels"), None, None, None),
        ),
        out_specs=(
            P(("groups", "nodes"), None, "rhs", "panels"),
            P(("groups", "nodes"), None, "rhs", "panels"),
            P(("groups", "nodes"), None, None, "rhs"),
        ),
        check_vma=False,
    )
```

```python
import functools
import math

import jax
import jax.numpy as jnp
import numpy as np
from jax import lax
from jax.experimental import pallas as pl
from jax.experimental.pallas import tpu as pltpu
from jax.sharding import PartitionSpec as P

MOM_DEV = 2
LANES = 128
TILE_CHUNK = 4
MOST_SHIFTS = 8

f32 = jnp.float32
bf16 = jnp.bfloat16

PARAMS = pltpu.CompilerParams(vmem_limit_bytes=40 * 1024 * 1024)
VMEM = pl.BlockSpec(memory_space=pltpu.VMEM)
HBM = pl.BlockSpec(memory_space=pltpu.HBM)


def dot_t(left, right):
    return lax.dot_general(left, right, (((1,), (1,)), ((), ())), preferred_element_type=f32)


def dot_n(left, right):
    return lax.dot_general(left, right, (((1,), (0,)), ((), ())), preferred_element_type=f32)


def split(value):
    high = value.astype(bf16)
    return high, (value - high.astype(f32)).astype(bf16)


def dot3_t(left, right):
    (l_hi, l_lo), (r_hi, r_lo) = left, right
    rows = l_hi.shape[0]
    both = dot_t(jnp.concatenate([l_hi, l_lo], axis=0), r_hi)
    return both[:rows] + both[rows:] + dot_t(l_hi, r_lo)


def dot3_n(left, right):
    (l_hi, l_lo), (r_hi, r_lo) = left, right
    rows = l_hi.shape[0]
    both = dot_n(jnp.concatenate([l_hi, l_lo], axis=0), r_hi)
    return both[:rows] + both[rows:] + dot_n(l_hi, r_lo)


def pick(index, values):
    result = f32(values[0])
    for i in range(1, len(values)):
        result = jnp.where(index == i, f32(values[i]), result)
    return result


def node_angle(node, nodes_all):
    return np.float32(2.0 * math.pi) * (np.float32(node) + np.float32(0.5)) / np.float32(nodes_all)


def terms_kernel(dims, *refs):
    panel_devs, blk_dev, shifted = dims
    n_out = panel_devs if shifted else 1
    indices, (contour_hbm, res_hbm, iter_hbm, probe_hbm, tiles_hbm, fr_hbm) = refs[:6], refs[6:12]
    outs, refs = refs[12 : 12 + n_out], refs[12 + n_out :]
    (pack, lines, consts), refs = refs[:3], refs[3:]
    held, (contour, tiles, fright, vec, terms, skel, acc, facc, sems) = refs[:6], refs[6:]
    tile_count = tiles.shape[0]
    far_count, _, rank, size = fright.shape
    res_rows, iter_rows = res_hbm.shape[0], iter_hbm.shape[0]
    node_dev = res_rows // 2
    chunk = TILE_CHUNK

    copies = []

    def start(source, target):
        copy = pltpu.make_async_copy(source, target, sems.at[len(copies)])
        copy.start()
        copies.append(copy)
        return copy

    res_copy = start(res_hbm, pack.at[pl.ds(0, res_rows)])
    small = [start(source, target) for source, target in zip(indices, held)]
    small.append(start(contour_hbm, contour))
    tile_copies = []
    for i in range(tile_count // chunk):
        part = pl.ds(i * chunk, chunk)
        tile_copies.append(start(tiles_hbm.at[part], tiles.at[part]))
    far_copy = start(fr_hbm, fright)
    rest = [
        start(iter_hbm, pack.at[pl.ds(res_rows, iter_rows)]),
        start(probe_hbm, lines.at[pl.ds(res_rows, 2)]),
    ]
    col, row, dest, fcol, frank, ftgt = held
    here = lax.axis_index("panels")

    def slot_of(owner):
        if shifted:
            owner = owner - here
            owner = jnp.where(owner < 0, owner + panel_devs, owner)
        return owner

    zero = jnp.zeros(acc.shape[1:], f32)
    for b in range(acc.shape[0]):
        acc[b] = zero
    for d in range(facc.shape[0]):
        facc[d] = zero

    res_copy.wait()
    for i in range(res_rows):
        lines[i] = pack[i]
    for b in range(blk_dev):
        lanes = slice(b * size, (b + 1) * size)
        re = jnp.concatenate([pack[2 * k, :, lanes] for k in range(node_dev)], axis=0)
        im = jnp.concatenate([pack[2 * k + 1, :, lanes] for k in range(node_dev)], axis=0)
        upper = jnp.concatenate([re, -im], axis=1)
        lower = jnp.concatenate([im, re], axis=1)
        vec[b] = jnp.concatenate([upper, lower], axis=0).astype(bf16)

    for copy in small:
        copy.wait()
    for i in range(consts.shape[0]):
        consts[i : i + 1, :] = jnp.full((1, LANES), contour[min(i, 2)], f32)

    rows = vec.shape[1]
    for i, copy in enumerate(tile_copies):
        copy.wait()
        for t in range(i * chunk, (i + 1) * chunk):
            tile = jnp.concatenate([tiles[t, 0], tiles[t, 1]], axis=1)
            terms[t] = dot_t(vec[col[t]], tile)
    far_copy.wait()
    group = LANES // rank
    sources = vec[...].reshape(blk_dev * rows, 2 * size)
    for g in range(far_count // group):
        mats = [
            jnp.concatenate([fright[f, 0], fright[f, 1]], axis=1)
            for f in range(g * group, (g + 1) * group)
        ]
        skel[g] = dot_t(sources, jnp.concatenate(mats, axis=0)).reshape(blk_dev, rows, LANES)

    for t in range(tile_count):
        target = slot_of(dest[t]) * blk_dev + row[t]
        acc[target] = acc[target] + terms[t]
    lane = lax.broadcasted_iota(jnp.int32, (rows, LANES), 1)
    for f in range(far_count):
        target = ftgt[f]
        owner = target // blk_dev
        place = (target - owner * blk_dev) * rank
        moved = pltpu.roll(
            skel[f // group, fcol[f]], lax.rem(place - (f % group) * rank + LANES, LANES), 1
        )
        kept = (lane >= place) & (lane < place + frank[f])
        slot = slot_of(owner)
        facc[slot] = facc[slot] + jnp.where(kept, moved, 0.0)

    near_rows = blk_dev * rows
    for d in range(panel_devs):
        out = outs[d] if shifted else outs[0].at[d]
        for b in range(blk_dev):
            out[b * rows : (b + 1) * rows, :] = acc[d * blk_dev + b]
        out[near_rows:, :] = facc[d]
    for copy in rest:
        copy.wait()


def product_kernel(dims, *refs):
    node_devs, nodes_all = dims
    parts, (left, pack, contour, out) = refs[:-4], refs[-4:]
    parts = [p for part in parts for p in ([part[d] for d in range(part.shape[0])] if len(part.shape) == 3 else [part[...]])]
    node_dev, _, rhs_dev, _ = out.shape
    blk_dev, _, rank, size = left.shape
    rows = 2 * node_dev * rhs_dev
    half = rows // 2

    total = parts[0]
    for part in parts[1:]:
        total = total + part
    near = total[: blk_dev * rows]
    summed = total[blk_dev * rows :]
    re, im = summed[:half], summed[half:]
    upper = jnp.concatenate([re, -im], axis=1)
    lower = jnp.concatenate([im, re], axis=1)
    whole = jnp.concatenate([upper, lower], axis=0)
    lane = lax.broadcasted_iota(jnp.int32, whole.shape, 1)
    block = lax.rem(lane, LANES) // rank
    picked = [jnp.where(block == b, whole, 0.0) for b in range(blk_dev)]
    mats = left[...]
    stacked = jnp.concatenate(
        [mats[:, 0].reshape(blk_dev * rank, size), mats[:, 1].reshape(blk_dev * rank, size)], axis=0
    )
    applied = near + dot_n(jnp.concatenate(picked, axis=0).astype(bf16), stacked)

    here = lax.axis_index("nodes")
    for k in range(node_dev):
        cosines, sines = [], []
        for x in range(node_devs):
            angle = node_angle(x * node_dev + k, nodes_all)
            cosines.append(float(np.cos(angle)))
            sines.append(float(np.sin(angle)))
        shift_re = contour[0:1, :] + contour[2:3, :] * pick(here, cosines)
        shift_im = contour[1:2, :] + contour[2:3, :] * pick(here, sines)
        for b in range(blk_dev):
            lanes = slice(b * size, (b + 1) * size)
            top = b * rows + k * rhs_dev
            r_re, r_im = pack[2 * k, :, lanes], pack[2 * k + 1, :, lanes]
            out[k, 0, :, lanes] = applied[top : top + rhs_dev] - (shift_re * r_re - shift_im * r_im)
            top = top + half
            out[k, 1, :, lanes] = applied[top : top + rhs_dev] - (shift_re * r_im + shift_im * r_re)


def side_by_side(pair, row, count):
    return jnp.concatenate([pair[row : row + count], pair[row + count : row + 2 * count]], axis=1)


def turned(pair, row, count):
    return jnp.concatenate([-pair[row + count : row + 2 * count], pair[row : row + count]], axis=1)


def joined(own, other, row):
    first = lax.axis_index("rhs") == 0
    mine, theirs = own[row], other[row]
    top = jnp.where(first, mine, theirs)
    bottom = jnp.where(first, theirs, mine)
    return jnp.concatenate([top, bottom], axis=0)


def ahead_kernel(node_devs, *refs):
    theirs, refs = refs[: node_devs - 1], refs[node_devs - 1 :]
    pack, own, other, res_hi, res_lo, message, *onward = refs
    _, rhs_dev, _ = own.shape
    cols = 2 * rhs_dev
    res_rows = own.shape[0] - 2
    node_dev = res_rows // 2

    for i in range(res_rows):
        high, low = split(joined(own, other, i))
        res_hi[i * cols : (i + 1) * cols, :] = high
        res_lo[i * cols : (i + 1) * cols, :] = low

    for there, out in zip(theirs, onward):
        for i in range(res_rows):
            out[i] = there[i]

    probe = [joined(own, other, res_rows + c) for c in range(2)]
    probe = split(jnp.concatenate(probe, axis=1))
    pair = []
    for held in (res_hi[...], res_lo[...]):
        rows = []
        for k in range(node_dev):
            rows.append(side_by_side(held, k * 2 * cols, cols))
            rows.append(-turned(held, k * 2 * cols, cols))
        pair.append(jnp.concatenate(rows, axis=0))
    probe_res = dot3_t(probe, tuple(pair))
    rows = []
    for k in range(node_dev):
        i_re, i_im = pack[res_rows + 2 * k], pack[res_rows + 2 * k + 1]
        rows.append(jnp.concatenate([i_re, i_im], axis=1))
        rows.append(jnp.concatenate([i_im, -i_re], axis=1))
    probe_iter = dot3_t(split(jnp.concatenate(rows, axis=0)), probe)

    message[:rhs_dev, :] = jnp.zeros((rhs_dev, LANES), f32)
    pieces = [jnp.zeros((rhs_dev, LANES // 2), f32)]
    pieces.extend(probe_iter[q * rhs_dev : (q + 1) * rhs_dev] for q in range(res_rows))
    message[rhs_dev:cols, :] = jnp.concatenate(pieces, axis=1)
    message[cols:, :] = jnp.concatenate([probe_res[:rhs_dev], probe_res[rhs_dev:]], axis=1)


def node_weight(here, scale, node_devs, node_dev, nodes_all, p, s, k):
    cosines, sines = [], []
    for x in range(node_devs):
        node = (x - s) % node_devs * node_dev + k
        power = x * MOM_DEV + p
        angle = np.float32(power + 1) * node_angle(node, nodes_all)
        cosines.append(float(np.cos(angle)))
        sines.append(float(np.sin(angle)))
    return scale * pick(here, cosines), scale * pick(here, sines)


def gram_kernel(own, other, res_hi, res_lo, ahead, message, prod_hi, prod_lo):
    node_dev, _, rhs_dev, _ = own.shape
    cols = 2 * rhs_dev
    for k in range(node_dev):
        for c in range(2):
            high, low = split(joined(own, other, (k, c)))
            top = (k * 2 + c) * cols
            prod_hi[top : top + cols, :] = high
            prod_lo[top : top + cols, :] = low
    sums = []
    for k in range(node_dev):
        top = k * 2 * cols
        left, right = [], []
        for p_ref, r_ref in ((prod_hi, res_hi), (prod_lo, res_lo)):
            product, source = p_ref[...], r_ref[: node_dev * 2 * cols, :]
            plain = side_by_side(product, top, cols)
            left.append(jnp.concatenate([plain, side_by_side(source, top, cols)], axis=0))
            right.append(jnp.concatenate([plain, turned(product, top, cols)], axis=0))
        sums.append(dot3_t(tuple(left), tuple(right)))
    gram = jnp.concatenate(sums, axis=1)
    half = LANES // 2
    first = lax.axis_index("rhs") == 0
    cross = jnp.where(first, gram[cols : cols + rhs_dev], gram[cols + rhs_dev :])
    message[:rhs_dev, :] = jnp.concatenate([gram[:rhs_dev], gram[rhs_dev:cols]], axis=1)
    message[rhs_dev:cols, :] = jnp.concatenate([cross, ahead[rhs_dev:cols, half:]], axis=1)
    message[cols:, :] = ahead[cols:, :]


def finish_kernel(dims, *refs):
    n_parts, node_devs, nodes_all, scale_factor = dims
    it = iter(refs)
    parts = [[next(it) for _ in range(n_parts)] for _ in range(node_devs)]
    packs = [next(it) for _ in range(node_devs)]
    others = [None] + [next(it) for _ in range(node_devs - 1)]
    prod_hi, prod_lo, res_hi, res_lo, contour, next_out, mom_out, hankel_out = it
    node_dev, _, rhs_dev, width = next_out.shape
    cols = 2 * rhs_dev
    half = LANES // 2
    res_rows = 2 * node_dev
    here = lax.axis_index("nodes")

    sums = [sum((part[...] for part in group[1:]), group[0][...]) for group in parts]
    if node_devs % 2:
        sums.append(sums[0])

    shape = (rhs_dev, LANES)
    lane = lax.broadcasted_iota(jnp.int32, shape, 1)
    low_half = lane < half
    base = (lane // (2 * cols)) * (2 * cols)
    spot = lax.rem(lane, cols)
    real_lane = lax.rem(lane, 2 * cols) < cols
    swapped = jnp.where(real_lane, lane + cols, lane - cols)
    sign = jnp.where(real_lane, -1.0, 1.0)

    def gathered(value, index):
        return jnp.take_along_axis(value, index, axis=1, mode="promise_in_bounds")

    solved, probe_res = [], []
    for g in range(len(sums) // 2):
        s0, s1 = sums[2 * g], sums[2 * g + 1]
        r0, r1 = pltpu.roll(s0, half, 1), pltpu.roll(s1, half, 1)
        v0, v1, v2 = [slice(i * rhs_dev, (i + 1) * rhs_dev) for i in range(3)]
        block = [
            jnp.where(low_half, s0[v0], r1[v0]),
            jnp.where(low_half, r0[v0], s1[v0]),
            jnp.where(low_half, s0[v1], r1[v1]),
        ]
        probe_res.append(
            jnp.concatenate(
                [jnp.where(low_half, s0[v2], r1[v2]), jnp.where(low_half, r0[v2], s1[v2])], axis=0
            )
        )
        inverse_diag = jnp.ones(shape, f32)
        for j in range(cols):
            at, r = divmod(j, rhs_dev)
            line = block[at][r : r + 1]
            crossed = (gathered(block[at], swapped) * sign)[r : r + 1]
            col_re = [gathered(b, base + j) for b in block[at:]]
            col_im = [gathered(b, base + cols + j) for b in block[at:]]
            inverse = 1.0 / col_re[0][r : r + 1]
            kept = (spot != j)[:1]
            scaled = jnp.where(kept, inverse, 0.0)
            f1, f2 = line * scaled, crossed * scaled
            for i in range(at, 3):
                block[i] = block[i] - (col_re[i - at] * f1 + col_im[i - at] * f2)
            inverse_diag = jnp.where(spot == j, inverse, inverse_diag)
        solved.append(block[2] * inverse_diag)

    coef = solved[0]
    cross = gathered(coef, swapped)
    plain = jnp.where(real_lane, coef, -coef)
    node_of = lane // (2 * cols)
    rows = []
    for k in range(node_dev):
        rows.append(jnp.where(node_of == k, plain, 0.0))
        rows.append(jnp.where(node_of == k, cross, 0.0))
    used = node_dev * 2 * cols
    left = split(jnp.concatenate(rows, axis=0)[:, :used])
    change = dot3_n(left, (prod_hi[...], prod_lo[...]))
    for k in range(node_dev):
        for c in range(2):
            top = (k * 2 + c) * rhs_dev
            next_out[k, c] = packs[0][2 * k + c] - change[top : top + rhs_dev]

    scale = contour[2:3, :] / nodes_all
    weighted = []
    for g, coef in enumerate(solved):
        cross = gathered(coef, swapped)
        rows = []
        for p in range(MOM_DEV):
            w_re = jnp.zeros(shape, f32)
            w_im = jnp.zeros(shape, f32)
            for i in range(2):
                s = 2 * g + i
                if s >= node_devs:
                    continue
                for k in range(node_dev):
                    n_re, n_im = node_weight(here, scale, node_devs, node_dev, nodes_all, p, s, k)
                    mine = node_of == i * node_dev + k
                    w_re = jnp.where(mine, n_re, w_re)
                    w_im = jnp.where(mine, n_im, w_im)
            rows.append(-sign * w_re * coef - w_im * cross)
            rows.append(-sign * w_im * coef + w_re * cross)
        weighted.append(jnp.concatenate(rows, axis=0))
    hankel = None
    products = None
    for g, value in enumerate(weighted):
        depth = min(LANES, node_devs * used - g * LANES)
        left = split(value)
        cut = tuple(part[:, :depth] for part in left)
        highs, lows = [], []
        for i in range(depth // used):
            s = 2 * g + i
            if s == 0:
                highs.append(res_hi[...])
                lows.append(res_lo[...])
                continue
            for q in range(res_rows):
                high, low = split(joined(packs[s], others[s], q))
                highs.append(high)
                lows.append(low)
        term = dot3_n(cut, (jnp.concatenate(highs, axis=0), jnp.concatenate(lows, axis=0)))
        products = term if products is None else products + term
        term = dot3_t(left, split(probe_res[g]))
        hankel = term if hankel is None else hankel + term

    wide = jnp.concatenate([scale] * (width // LANES), axis=1)
    for p in range(MOM_DEV):
        mom = [products[(2 * p + c) * rhs_dev : (2 * p + c + 1) * rhs_dev] for c in range(2)]
        han = [hankel[(2 * p + c) * rhs_dev : (2 * p + c + 1) * rhs_dev] for c in range(2)]
        for s in range(node_devs):
            for k in range(node_dev):
                w_re, w_im = node_weight(here, wide, node_devs, node_dev, nodes_all, p, s, k)
                i_re, i_im = packs[s][res_rows + 2 * k], packs[s][res_rows + 2 * k + 1]
                mom[0] = mom[0] + (w_re * i_re - w_im * i_im)
                mom[1] = mom[1] + (w_re * i_im + w_im * i_re)
                i_re, i_im = [
                    pltpu.roll(sums[s][rhs_dev:cols], half - (2 * k + c) * cols, 1)[:, :cols]
                    for c in range(2)
                ]
                w_re, w_im = w_re[:, :cols], w_im[:, :cols]
                han[0] = han[0] + (w_re * i_re - w_im * i_im)
                han[1] = han[1] + (w_re * i_im + w_im * i_re)
        for c in range(2):
            mom_out[p, c] = mom[c]
            hankel_out[p, c] = han[c] * scale_factor


def call(kernel, out_shape, args, in_specs=None, scratch=(), cost=None):
    args = tuple(args)
    multiple = isinstance(out_shape, (list, tuple))
    return pl.pallas_call(
        kernel,
        out_shape=out_shape,
        in_specs=[VMEM] * len(args) if in_specs is None else in_specs,
        out_specs=[VMEM] * len(out_shape) if multiple else VMEM,
        scratch_shapes=list(scratch),
        compiler_params=PARAMS,
        cost_estimate=cost,
    )(*args)


def struct(shape, dtype=f32):
    return jax.ShapeDtypeStruct(shape, dtype)


def per_device(
    residual,
    iterate,
    probe,
    contour,
    near_tiles,
    near_col,
    near_row,
    near_dest,
    far_right,
    far_col,
    far_rank,
    far_target,
    far_left,
):
    node_dev, _, rhs_dev, rows_dev = residual.shape
    tile_count, _, size, _ = near_tiles.shape
    far_count, _, rank, _ = far_right.shape
    blk_dev = rows_dev // size
    panel_devs = lax.axis_size("panels")
    node_devs = lax.axis_size("nodes")
    nodes_all = node_dev * node_devs
    vec_rows = 2 * node_dev * rhs_dev
    cols = 2 * rhs_dev
    res_rows = 2 * node_dev
    span = res_rows * cols

    part_rows = blk_dev * vec_rows + vec_rows
    copies = 6 + 1 + tile_count // TILE_CHUNK + 4
    field = (rhs_dev, rows_dev)
    indices = (near_col, near_row, near_dest.reshape(tile_count), far_col, far_rank, far_target)
    shifted = panel_devs <= MOST_SHIFTS
    out_shape = [struct((part_rows, LANES))] * panel_devs if shifted else [struct((panel_devs, part_rows, LANES))]
    in_hbm = functools.partial(pltpu.with_memory_space_constraint, memory_space=pltpu.HBM)
    *terms, pack, lines, consts = call(
        functools.partial(terms_kernel, (panel_devs, blk_dev, shifted)),
        [
            *out_shape,
            struct((2 * res_rows, *field)),
            struct((res_rows + 2, *field)),
            struct((8, LANES)),
        ],
        map(in_hbm, (
            *indices,
            contour,
            residual.reshape(res_rows, rhs_dev, rows_dev),
            iterate.reshape(res_rows, rhs_dev, rows_dev),
            probe,
            near_tiles,
            far_right,
        )),
        in_specs=[HBM] * 12,
        scratch=[
            *[pltpu.SMEM(index.shape, jnp.int32) for index in indices],
            pltpu.SMEM(contour.shape, f32),
            pltpu.VMEM(near_tiles.shape, bf16),
            pltpu.VMEM(far_right.shape, bf16),
            pltpu.VMEM((blk_dev, vec_rows, 2 * size), bf16),
            pltpu.VMEM((tile_count, vec_rows, size), f32),
            pltpu.VMEM((far_count * rank // LANES, blk_dev, vec_rows, LANES), f32),
            pltpu.VMEM((panel_devs * blk_dev, vec_rows, size), f32),
            pltpu.VMEM((panel_devs, vec_rows, LANES), f32),
            pltpu.SemaphoreType.DMA((copies,)),
        ],
    )

    if shifted:
        parts = terms[:1]
        for d in range(1, panel_devs):
            pairs = [(i, (i + d) % panel_devs) for i in range(panel_devs)]
            parts.append(lax.ppermute(terms[d], "panels", pairs))
    else:
        parts = [lax.all_to_all(terms[0], "panels", split_axis=0, concat_axis=0, tiled=True)]

    swap = [(0, 1), (1, 0)]
    there = lax.ppermute(lines, "rhs", swap)
    node_pairs = [[(i, (i + s) % node_devs) for i in range(node_devs)] for s in range(node_devs)]
    packs = [pack] + [lax.ppermute(pack, "nodes", pairs) for pairs in node_pairs[1:]]

    product = call(
        functools.partial(product_kernel, (node_devs, nodes_all)),
        struct(residual.shape),
        (*parts, far_left.transpose(0, 1, 3, 2), pack, consts),
    )
    res_hi, res_lo, ahead, *onward = call(
        functools.partial(ahead_kernel, node_devs),
        [struct((span, rows_dev), bf16), struct((span, rows_dev), bf16), struct((3 * rhs_dev, LANES))]
        + [struct((res_rows, *field))] * (node_devs - 1),
        (*packs[1:], pack, lines, there),
    )
    others = [lax.ppermute(value, "rhs", swap) for value in onward]
    message, prod_hi, prod_lo = call(
        gram_kernel,
        [
            struct((3 * rhs_dev, LANES)),
            struct((span, rows_dev), bf16),
            struct((span, rows_dev), bf16),
        ],
        (product, lax.ppermute(product, "rhs", swap), res_hi, res_lo, ahead),
    )

    if shifted:
        total = message
        for d in range(1, panel_devs):
            pairs = [(i, (i + d) % panel_devs) for i in range(panel_devs)]
            total = total + lax.ppermute(message, "panels", pairs)
    else:
        total = lax.psum(message, "panels")
    sums = [total] + [lax.ppermute(total, "nodes", pairs) for pairs in node_pairs[1:]]
    scale_factor = 1.0 / math.sqrt(rows_dev * panel_devs)
    residual_next, moments, hankel = call(
        functools.partial(finish_kernel, (1, node_devs, nodes_all, scale_factor)),
        [
            struct(residual.shape),
            struct((MOM_DEV, 2, rhs_dev, rows_dev)),
            struct((MOM_DEV, 2, rhs_dev, cols)),
        ],
        (*sums, *packs, *others, prod_hi, prod_lo, res_hi, res_lo, consts),
    )
    return residual_next, moments, hankel.transpose(0, 1, 3, 2)


def solution(mesh):
    return jax.shard_map(
        per_device,
        mesh=mesh,
        in_specs=(
            P(("groups", "nodes"), None, "rhs", "panels"),
            P(("groups", "nodes"), None, "rhs", "panels"),
            P("groups", "rhs", "panels"),
            P("groups"),
            P(("groups", "panels"), None, None, None),
            P(("groups", "panels")),
            P(("groups", "panels")),
            P(("groups", "panels"), None),
            P(("groups", "panels"), None, None, None),
            P(("groups", "panels")),
            P(("groups", "panels")),
            P(("groups", "panels")),
            P(("groups", "panels"), None, None, None),
        ),
        out_specs=(
            P(("groups", "nodes"), None, "rhs", "panels"),
            P(("groups", "nodes"), None, "rhs", "panels"),
            P(("groups", "nodes"), None, None, "rhs"),
        ),
        check_vma=False,
    )
```

```python
import functools
import math

import jax
import jax.numpy as jnp
import numpy as np
from jax import lax
from jax.experimental import pallas as pl
from jax.experimental.pallas import tpu as pltpu
from jax.sharding import PartitionSpec as P

MOM_DEV = 2
LANES = 128
TILE_CHUNK = 4
MOST_SHIFTS = 8

f32 = jnp.float32
bf16 = jnp.bfloat16

PARAMS = pltpu.CompilerParams(vmem_limit_bytes=40 * 1024 * 1024)
VMEM = pl.BlockSpec(memory_space=pltpu.VMEM)
HBM = pl.BlockSpec(memory_space=pltpu.HBM)


def dot_t(left, right):
    return lax.dot_general(left, right, (((1,), (1,)), ((), ())), preferred_element_type=f32)


def dot_n(left, right):
    return lax.dot_general(left, right, (((1,), (0,)), ((), ())), preferred_element_type=f32)


def split(value):
    high = value.astype(bf16)
    return high, (value - high.astype(f32)).astype(bf16)


def dot3_t(left, right):
    (l_hi, l_lo), (r_hi, r_lo) = left, right
    rows = l_hi.shape[0]
    both = dot_t(jnp.concatenate([l_hi, l_lo], axis=0), r_hi)
    return both[:rows] + both[rows:] + dot_t(l_hi, r_lo)


def dot3_n(left, right):
    (l_hi, l_lo), (r_hi, r_lo) = left, right
    rows = l_hi.shape[0]
    both = dot_n(jnp.concatenate([l_hi, l_lo], axis=0), r_hi)
    return both[:rows] + both[rows:] + dot_n(l_hi, r_lo)


def pick(index, values):
    result = f32(values[0])
    for i in range(1, len(values)):
        result = jnp.where(index == i, f32(values[i]), result)
    return result


def node_angle(node, nodes_all):
    return np.float32(2.0 * math.pi) * (np.float32(node) + np.float32(0.5)) / np.float32(nodes_all)


def terms_kernel(dims, *refs):
    panel_devs, blk_dev, shifted = dims
    n_out = panel_devs if shifted else 1
    indices, (contour_hbm, res_hbm, iter_hbm, probe_hbm, tiles_hbm, fr_hbm) = refs[:6], refs[6:12]
    outs, refs = refs[12 : 12 + n_out], refs[12 + n_out :]
    (pack, lines, consts), refs = refs[:3], refs[3:]
    held, (contour, tiles, fright, vec, terms, skel, acc, facc, sems) = refs[:6], refs[6:]
    tile_count = tiles.shape[0]
    far_count, _, rank, size = fright.shape
    res_rows, iter_rows = res_hbm.shape[0], iter_hbm.shape[0]
    node_dev = res_rows // 2
    chunk = TILE_CHUNK

    copies = []

    def start(source, target):
        copy = pltpu.make_async_copy(source, target, sems.at[len(copies)])
        copy.start()
        copies.append(copy)
        return copy

    res_copy = start(res_hbm, pack.at[pl.ds(0, res_rows)])
    small = [start(source, target) for source, target in zip(indices, held)]
    small.append(start(contour_hbm, contour))
    tile_copies = []
    for i in range(tile_count // chunk):
        part = pl.ds(i * chunk, chunk)
        tile_copies.append(start(tiles_hbm.at[part], tiles.at[part]))
    far_copy = start(fr_hbm, fright)
    rest = [
        start(iter_hbm, pack.at[pl.ds(res_rows, iter_rows)]),
        start(probe_hbm, lines.at[pl.ds(res_rows, 2)]),
    ]
    col, row, dest, fcol, frank, ftgt = held
    here = lax.axis_index("panels")

    def slot_of(owner):
        if shifted:
            owner = owner - here
            owner = jnp.where(owner < 0, owner + panel_devs, owner)
        return owner

    zero = jnp.zeros(acc.shape[1:], f32)
    for b in range(acc.shape[0]):
        acc[b] = zero
    for d in range(facc.shape[0]):
        facc[d] = zero

    res_copy.wait()
    for i in range(res_rows):
        lines[i] = pack[i]
    for b in range(blk_dev):
        lanes = slice(b * size, (b + 1) * size)
        re = jnp.concatenate([pack[2 * k, :, lanes] for k in range(node_dev)], axis=0)
        im = jnp.concatenate([pack[2 * k + 1, :, lanes] for k in range(node_dev)], axis=0)
        upper = jnp.concatenate([re, -im], axis=1)
        lower = jnp.concatenate([im, re], axis=1)
        vec[b] = jnp.concatenate([upper, lower], axis=0).astype(bf16)

    for copy in small:
        copy.wait()
    for i in range(consts.shape[0]):
        consts[i : i + 1, :] = jnp.full((1, LANES), contour[min(i, 2)], f32)

    rows = vec.shape[1]
    for i, copy in enumerate(tile_copies):
        copy.wait()
        for t in range(i * chunk, (i + 1) * chunk):
            tile = jnp.concatenate([tiles[t, 0], tiles[t, 1]], axis=1)
            terms[t] = dot_t(vec[col[t]], tile)
    far_copy.wait()
    group = LANES // rank
    sources = vec[...].reshape(blk_dev * rows, 2 * size)
    for g in range(far_count // group):
        mats = [
            jnp.concatenate([fright[f, 0], fright[f, 1]], axis=1)
            for f in range(g * group, (g + 1) * group)
        ]
        skel[g] = dot_t(sources, jnp.concatenate(mats, axis=0)).reshape(blk_dev, rows, LANES)

    for t in range(tile_count):
        target = slot_of(dest[t]) * blk_dev + row[t]
        acc[target] = acc[target] + terms[t]
    lane = lax.broadcasted_iota(jnp.int32, (rows, LANES), 1)
    for f in range(far_count):
        target = ftgt[f]
        owner = target // blk_dev
        place = (target - owner * blk_dev) * rank
        moved = pltpu.roll(
            skel[f // group, fcol[f]], lax.rem(place - (f % group) * rank + LANES, LANES), 1
        )
        kept = (lane >= place) & (lane < place + frank[f])
        slot = slot_of(owner)
        facc[slot] = facc[slot] + jnp.where(kept, moved, 0.0)

    near_rows = blk_dev * rows
    for d in range(panel_devs):
        out = outs[d] if shifted else outs[0].at[d]
        for b in range(blk_dev):
            out[b * rows : (b + 1) * rows, :] = acc[d * blk_dev + b]
        out[near_rows:, :] = facc[d]
    for copy in rest:
        copy.wait()


def product_kernel(dims, *refs):
    node_devs, nodes_all = dims
    parts, (left, pack, contour, out) = refs[:-4], refs[-4:]
    parts = [p for part in parts for p in ([part[d] for d in range(part.shape[0])] if len(part.shape) == 3 else [part[...]])]
    node_dev, _, rhs_dev, _ = out.shape
    blk_dev, _, rank, size = left.shape
    rows = 2 * node_dev * rhs_dev
    half = rows // 2

    total = parts[0]
    for part in parts[1:]:
        total = total + part
    near = total[: blk_dev * rows]
    summed = total[blk_dev * rows :]
    re, im = summed[:half], summed[half:]
    upper = jnp.concatenate([re, -im], axis=1)
    lower = jnp.concatenate([im, re], axis=1)
    whole = jnp.concatenate([upper, lower], axis=0)
    lane = lax.broadcasted_iota(jnp.int32, whole.shape, 1)
    block = lax.rem(lane, LANES) // rank
    picked = [jnp.where(block == b, whole, 0.0) for b in range(blk_dev)]
    mats = left[...]
    stacked = jnp.concatenate(
        [mats[:, 0].reshape(blk_dev * rank, size), mats[:, 1].reshape(blk_dev * rank, size)], axis=0
    )
    applied = near + dot_n(jnp.concatenate(picked, axis=0).astype(bf16), stacked)

    here = lax.axis_index("nodes")
    for k in range(node_dev):
        cosines, sines = [], []
        for x in range(node_devs):
            angle = node_angle(x * node_dev + k, nodes_all)
            cosines.append(float(np.cos(angle)))
            sines.append(float(np.sin(angle)))
        shift_re = contour[0:1, :] + contour[2:3, :] * pick(here, cosines)
        shift_im = contour[1:2, :] + contour[2:3, :] * pick(here, sines)
        for b in range(blk_dev):
            lanes = slice(b * size, (b + 1) * size)
            top = b * rows + k * rhs_dev
            r_re, r_im = pack[2 * k, :, lanes], pack[2 * k + 1, :, lanes]
            out[k, 0, :, lanes] = applied[top : top + rhs_dev] - (shift_re * r_re - shift_im * r_im)
            top = top + half
            out[k, 1, :, lanes] = applied[top : top + rhs_dev] - (shift_re * r_im + shift_im * r_re)


def side_by_side(pair, row, count):
    return jnp.concatenate([pair[row : row + count], pair[row + count : row + 2 * count]], axis=1)


def turned(pair, row, count):
    return jnp.concatenate([-pair[row + count : row + 2 * count], pair[row : row + count]], axis=1)


def joined(own, other, row):
    first = lax.axis_index("rhs") == 0
    mine, theirs = own[row], other[row]
    top = jnp.where(first, mine, theirs)
    bottom = jnp.where(first, theirs, mine)
    return jnp.concatenate([top, bottom], axis=0)


def ahead_kernel(node_devs, *refs):
    theirs, refs = refs[: node_devs - 1], refs[node_devs - 1 :]
    pack, own, other, res_hi, res_lo, message, *onward = refs
    _, rhs_dev, _ = own.shape
    cols = 2 * rhs_dev
    res_rows = own.shape[0] - 2
    node_dev = res_rows // 2

    for i in range(res_rows):
        high, low = split(joined(own, other, i))
        res_hi[i * cols : (i + 1) * cols, :] = high
        res_lo[i * cols : (i + 1) * cols, :] = low

    for there, out in zip(theirs, onward):
        for i in range(res_rows):
            out[i] = there[i]

    probe = [joined(own, other, res_rows + c) for c in range(2)]
    probe = split(jnp.concatenate(probe, axis=1))
    pair = []
    for held in (res_hi[...], res_lo[...]):
        rows = []
        for k in range(node_dev):
            rows.append(side_by_side(held, k * 2 * cols, cols))
            rows.append(-turned(held, k * 2 * cols, cols))
        pair.append(jnp.concatenate(rows, axis=0))
    probe_res = dot3_t(probe, tuple(pair))
    rows = []
    for k in range(node_dev):
        i_re, i_im = pack[res_rows + 2 * k], pack[res_rows + 2 * k + 1]
        rows.append(jnp.concatenate([i_re, i_im], axis=1))
        rows.append(jnp.concatenate([i_im, -i_re], axis=1))
    probe_iter = dot3_t(split(jnp.concatenate(rows, axis=0)), probe)

    message[:rhs_dev, :] = jnp.zeros((rhs_dev, LANES), f32)
    pieces = [jnp.zeros((rhs_dev, LANES // 2), f32)]
    pieces.extend(probe_iter[q * rhs_dev : (q + 1) * rhs_dev] for q in range(res_rows))
    message[rhs_dev:cols, :] = jnp.concatenate(pieces, axis=1)
    message[cols:, :] = jnp.concatenate([probe_res[:rhs_dev], probe_res[rhs_dev:]], axis=1)


def node_weight(here, scale, node_devs, node_dev, nodes_all, p, s, k):
    cosines, sines = [], []
    for x in range(node_devs):
        node = (x - s) % node_devs * node_dev + k
        power = x * MOM_DEV + p
        angle = np.float32(power + 1) * node_angle(node, nodes_all)
        cosines.append(float(np.cos(angle)))
        sines.append(float(np.sin(angle)))
    return scale * pick(here, cosines), scale * pick(here, sines)


def gram_kernel(own, other, res_hi, res_lo, ahead, message, prod_hi, prod_lo):
    node_dev, _, rhs_dev, _ = own.shape
    cols = 2 * rhs_dev
    for k in range(node_dev):
        for c in range(2):
            high, low = split(joined(own, other, (k, c)))
            top = (k * 2 + c) * cols
            prod_hi[top : top + cols, :] = high
            prod_lo[top : top + cols, :] = low
    sums = []
    for k in range(node_dev):
        top = k * 2 * cols
        left, right = [], []
        for p_ref, r_ref in ((prod_hi, res_hi), (prod_lo, res_lo)):
            product, source = p_ref[...], r_ref[: node_dev * 2 * cols, :]
            plain = side_by_side(product, top, cols)
            left.append(jnp.concatenate([plain, side_by_side(source, top, cols)], axis=0))
            right.append(jnp.concatenate([plain, turned(product, top, cols)], axis=0))
        sums.append(dot3_t(tuple(left), tuple(right)))
    gram = jnp.concatenate(sums, axis=1)
    half = LANES // 2
    first = lax.axis_index("rhs") == 0
    cross = jnp.where(first, gram[cols : cols + rhs_dev], gram[cols + rhs_dev :])
    message[:rhs_dev, :] = jnp.concatenate([gram[:rhs_dev], gram[rhs_dev:cols]], axis=1)
    message[rhs_dev:cols, :] = jnp.concatenate([cross, ahead[rhs_dev:cols, half:]], axis=1)
    message[cols:, :] = ahead[cols:, :]


def finish_kernel(dims, *refs):
    n_parts, node_devs, nodes_all, scale_factor = dims
    it = iter(refs)
    parts = [[next(it) for _ in range(n_parts)] for _ in range(node_devs)]
    packs = [next(it) for _ in range(node_devs)]
    others = [None] + [next(it) for _ in range(node_devs - 1)]
    prod_hi, prod_lo, res_hi, res_lo, contour, next_out, mom_out, hankel_out = it
    node_dev, _, rhs_dev, width = next_out.shape
    cols = 2 * rhs_dev
    half = LANES // 2
    res_rows = 2 * node_dev
    here = lax.axis_index("nodes")

    sums = [sum((part[...] for part in group[1:]), group[0][...]) for group in parts]
    if node_devs % 2:
        sums.append(sums[0])

    shape = (rhs_dev, LANES)
    lane = lax.broadcasted_iota(jnp.int32, shape, 1)
    low_half = lane < half
    base = (lane // (2 * cols)) * (2 * cols)
    spot = lax.rem(lane, cols)
    real_lane = lax.rem(lane, 2 * cols) < cols
    swapped = jnp.where(real_lane, lane + cols, lane - cols)
    sign = jnp.where(real_lane, -1.0, 1.0)

    def gathered(value, index):
        return jnp.take_along_axis(value, index, axis=1, mode="promise_in_bounds")

    solved, probe_res = [], []
    for g in range(len(sums) // 2):
        s0, s1 = sums[2 * g], sums[2 * g + 1]
        r0, r1 = pltpu.roll(s0, half, 1), pltpu.roll(s1, half, 1)
        v0, v1, v2 = [slice(i * rhs_dev, (i + 1) * rhs_dev) for i in range(3)]
        block = [
            jnp.where(low_half, s0[v0], r1[v0]),
            jnp.where(low_half, r0[v0], s1[v0]),
            jnp.where(low_half, s0[v1], r1[v1]),
        ]
        probe_res.append(
            jnp.concatenate(
                [jnp.where(low_half, s0[v2], r1[v2]), jnp.where(low_half, r0[v2], s1[v2])], axis=0
            )
        )
        for j in range(0, cols, 2):
            at, r = divmod(j, rhs_dev)
            line = block[at]
            crossed = gathered(line, swapped) * sign
            columns = [
                [gathered(value, base + spot_at) for value in block[at:]]
                for spot_at in (j, cols + j, j + 1, cols + j + 1)
            ]
            pivot = (spot == j) | (spot == j + 1)
            g, crossed_g = [], []
            for i in range(2):
                one = spot == j + i
                row = jnp.where(pivot[:1], 0.0, line[r + i : r + i + 1])
                g.append(jnp.where((one & real_lane)[:1], -1.0, row))
                row = jnp.where(pivot[:1], 0.0, crossed[r + i : r + i + 1])
                crossed_g.append(jnp.where((one & ~real_lane)[:1], -1.0, row))
            inverse_p = 1.0 / columns[0][0][r : r + 1]
            b_re, b_im = columns[0][0][r + 1 : r + 2], columns[1][0][r + 1 : r + 2]
            t_re, t_im = b_re * inverse_p, b_im * inverse_p
            inverse_s = 1.0 / (columns[2][0][r + 1 : r + 2] - (t_re * b_re + t_im * b_im))
            h = (g[1] - (g[0] * t_re + crossed_g[0] * t_im)) * inverse_s
            crossed_h = (crossed_g[1] - (crossed_g[0] * t_re - g[0] * t_im)) * inverse_s
            f = g[0] * inverse_p - (h * t_re - crossed_h * t_im)
            crossed_f = crossed_g[0] * inverse_p - (crossed_h * t_re + h * t_im)
            for i in range(at, 3):
                c0_re, c0_im, c1_re, c1_im = [value[i - at] for value in columns]
                change = (c0_re * f + c0_im * crossed_f) + (c1_re * h + c1_im * crossed_h)
                block[i] = jnp.where(pivot, 0.0, block[i]) - change
        solved.append(block[2])

    coef = solved[0]
    cross = gathered(coef, swapped)
    plain = jnp.where(real_lane, coef, -coef)
    node_of = lane // (2 * cols)
    rows = []
    for k in range(node_dev):
        rows.append(jnp.where(node_of == k, plain, 0.0))
        rows.append(jnp.where(node_of == k, cross, 0.0))
    used = node_dev * 2 * cols
    left = split(jnp.concatenate(rows, axis=0)[:, :used])
    change = dot3_n(left, (prod_hi[...], prod_lo[...]))
    for k in range(node_dev):
        for c in range(2):
            top = (k * 2 + c) * rhs_dev
            next_out[k, c] = packs[0][2 * k + c] - change[top : top + rhs_dev]

    scale = contour[2:3, :] / nodes_all
    weighted = []
    for g, coef in enumerate(solved):
        cross = gathered(coef, swapped)
        rows = []
        for p in range(MOM_DEV):
            w_re = jnp.zeros(shape, f32)
            w_im = jnp.zeros(shape, f32)
            for i in range(2):
                s = 2 * g + i
                if s >= node_devs:
                    continue
                for k in range(node_dev):
                    n_re, n_im = node_weight(here, scale, node_devs, node_dev, nodes_all, p, s, k)
                    mine = node_of == i * node_dev + k
                    w_re = jnp.where(mine, n_re, w_re)
                    w_im = jnp.where(mine, n_im, w_im)
            rows.append(-sign * w_re * coef - w_im * cross)
            rows.append(-sign * w_im * coef + w_re * cross)
        weighted.append(jnp.concatenate(rows, axis=0))
    hankel = None
    products = None
    for g, value in enumerate(weighted):
        depth = min(LANES, node_devs * used - g * LANES)
        left = split(value)
        cut = tuple(part[:, :depth] for part in left)
        highs, lows = [], []
        for i in range(depth // used):
            s = 2 * g + i
            if s == 0:
                highs.append(res_hi[...])
                lows.append(res_lo[...])
                continue
            for q in range(res_rows):
                high, low = split(joined(packs[s], others[s], q))
                highs.append(high)
                lows.append(low)
        term = dot3_n(cut, (jnp.concatenate(highs, axis=0), jnp.concatenate(lows, axis=0)))
        products = term if products is None else products + term
        term = dot3_t(left, split(probe_res[g]))
        hankel = term if hankel is None else hankel + term

    wide = jnp.concatenate([scale] * (width // LANES), axis=1)
    for p in range(MOM_DEV):
        mom = [products[(2 * p + c) * rhs_dev : (2 * p + c + 1) * rhs_dev] for c in range(2)]
        han = [hankel[(2 * p + c) * rhs_dev : (2 * p + c + 1) * rhs_dev] for c in range(2)]
        for s in range(node_devs):
            for k in range(node_dev):
                w_re, w_im = node_weight(here, wide, node_devs, node_dev, nodes_all, p, s, k)
                i_re, i_im = packs[s][res_rows + 2 * k], packs[s][res_rows + 2 * k + 1]
                mom[0] = mom[0] + (w_re * i_re - w_im * i_im)
                mom[1] = mom[1] + (w_re * i_im + w_im * i_re)
                i_re, i_im = [
                    pltpu.roll(sums[s][rhs_dev:cols], half - (2 * k + c) * cols, 1)[:, :cols]
                    for c in range(2)
                ]
                w_re, w_im = w_re[:, :cols], w_im[:, :cols]
                han[0] = han[0] + (w_re * i_re - w_im * i_im)
                han[1] = han[1] + (w_re * i_im + w_im * i_re)
        for c in range(2):
            mom_out[p, c] = mom[c]
            hankel_out[p, c] = han[c] * scale_factor


def call(kernel, out_shape, args, in_specs=None, scratch=(), cost=None):
    args = tuple(args)
    multiple = isinstance(out_shape, (list, tuple))
    return pl.pallas_call(
        kernel,
        out_shape=out_shape,
        in_specs=[VMEM] * len(args) if in_specs is None else in_specs,
        out_specs=[VMEM] * len(out_shape) if multiple else VMEM,
        scratch_shapes=list(scratch),
        compiler_params=PARAMS,
        cost_estimate=cost,
    )(*args)


def struct(shape, dtype=f32):
    return jax.ShapeDtypeStruct(shape, dtype)


def per_device(
    residual,
    iterate,
    probe,
    contour,
    near_tiles,
    near_col,
    near_row,
    near_dest,
    far_right,
    far_col,
    far_rank,
    far_target,
    far_left,
):
    node_dev, _, rhs_dev, rows_dev = residual.shape
    tile_count, _, size, _ = near_tiles.shape
    far_count, _, rank, _ = far_right.shape
    blk_dev = rows_dev // size
    panel_devs = lax.axis_size("panels")
    node_devs = lax.axis_size("nodes")
    nodes_all = node_dev * node_devs
    vec_rows = 2 * node_dev * rhs_dev
    cols = 2 * rhs_dev
    res_rows = 2 * node_dev
    span = res_rows * cols

    part_rows = blk_dev * vec_rows + vec_rows
    copies = 6 + 1 + tile_count // TILE_CHUNK + 4
    field = (rhs_dev, rows_dev)
    indices = (near_col, near_row, near_dest.reshape(tile_count), far_col, far_rank, far_target)
    shifted = panel_devs <= MOST_SHIFTS
    out_shape = [struct((part_rows, LANES))] * panel_devs if shifted else [struct((panel_devs, part_rows, LANES))]
    in_hbm = functools.partial(pltpu.with_memory_space_constraint, memory_space=pltpu.HBM)
    *terms, pack, lines, consts = call(
        functools.partial(terms_kernel, (panel_devs, blk_dev, shifted)),
        [
            *out_shape,
            struct((2 * res_rows, *field)),
            struct((res_rows + 2, *field)),
            struct((8, LANES)),
        ],
        map(in_hbm, (
            *indices,
            contour,
            residual.reshape(res_rows, rhs_dev, rows_dev),
            iterate.reshape(res_rows, rhs_dev, rows_dev),
            probe,
            near_tiles,
            far_right,
        )),
        in_specs=[HBM] * 12,
        scratch=[
            *[pltpu.SMEM(index.shape, jnp.int32) for index in indices],
            pltpu.SMEM(contour.shape, f32),
            pltpu.VMEM(near_tiles.shape, bf16),
            pltpu.VMEM(far_right.shape, bf16),
            pltpu.VMEM((blk_dev, vec_rows, 2 * size), bf16),
            pltpu.VMEM((tile_count, vec_rows, size), f32),
            pltpu.VMEM((far_count * rank // LANES, blk_dev, vec_rows, LANES), f32),
            pltpu.VMEM((panel_devs * blk_dev, vec_rows, size), f32),
            pltpu.VMEM((panel_devs, vec_rows, LANES), f32),
            pltpu.SemaphoreType.DMA((copies,)),
        ],
    )

    if shifted:
        parts = terms[:1]
        for d in range(1, panel_devs):
            pairs = [(i, (i + d) % panel_devs) for i in range(panel_devs)]
            parts.append(lax.ppermute(terms[d], "panels", pairs))
    else:
        parts = [lax.all_to_all(terms[0], "panels", split_axis=0, concat_axis=0, tiled=True)]

    swap = [(0, 1), (1, 0)]
    there = lax.ppermute(lines, "rhs", swap)
    node_pairs = [[(i, (i + s) % node_devs) for i in range(node_devs)] for s in range(node_devs)]
    packs = [pack] + [lax.ppermute(pack, "nodes", pairs) for pairs in node_pairs[1:]]

    product = call(
        functools.partial(product_kernel, (node_devs, nodes_all)),
        struct(residual.shape),
        (*parts, far_left.transpose(0, 1, 3, 2), pack, consts),
    )
    res_hi, res_lo, ahead, *onward = call(
        functools.partial(ahead_kernel, node_devs),
        [struct((span, rows_dev), bf16), struct((span, rows_dev), bf16), struct((3 * rhs_dev, LANES))]
        + [struct((res_rows, *field))] * (node_devs - 1),
        (*packs[1:], pack, lines, there),
    )
    others = [lax.ppermute(value, "rhs", swap) for value in onward]
    message, prod_hi, prod_lo = call(
        gram_kernel,
        [
            struct((3 * rhs_dev, LANES)),
            struct((span, rows_dev), bf16),
            struct((span, rows_dev), bf16),
        ],
        (product, lax.ppermute(product, "rhs", swap), res_hi, res_lo, ahead),
    )

    if shifted:
        total = message
        for d in range(panel_devs - 1, 0, -1):
            pairs = [(i, (i + d) % panel_devs) for i in range(panel_devs)]
            total = total + lax.ppermute(message, "panels", pairs)
    else:
        total = lax.psum(message, "panels")
    sums = [total] + [lax.ppermute(total, "nodes", pairs) for pairs in node_pairs[1:]]
    scale_factor = 1.0 / math.sqrt(rows_dev * panel_devs)
    residual_next, moments, hankel = call(
        functools.partial(finish_kernel, (1, node_devs, nodes_all, scale_factor)),
        [
            struct(residual.shape),
            struct((MOM_DEV, 2, rhs_dev, rows_dev)),
            struct((MOM_DEV, 2, rhs_dev, cols)),
        ],
        (*sums, *packs, *others, prod_hi, prod_lo, res_hi, res_lo, consts),
    )
    return residual_next, moments, hankel.transpose(0, 1, 3, 2)


def solution(mesh):
    return jax.shard_map(
        per_device,
        mesh=mesh,
        in_specs=(
            P(("groups", "nodes"), None, "rhs", "panels"),
            P(("groups", "nodes"), None, "rhs", "panels"),
            P("groups", "rhs", "panels"),
            P("groups"),
            P(("groups", "panels"), None, None, None),
            P(("groups", "panels")),
            P(("groups", "panels")),
            P(("groups", "panels"), None),
            P(("groups", "panels"), None, None, None),
            P(("groups", "panels")),
            P(("groups", "panels")),
            P(("groups", "panels")),
            P(("groups", "panels"), None, None, None),
        ),
        out_specs=(
            P(("groups", "nodes"), None, "rhs", "panels"),
            P(("groups", "nodes"), None, "rhs", "panels"),
            P(("groups", "nodes"), None, None, "rhs"),
        ),
        check_vma=False,
    )
```

```python
import functools
import math

import jax
import jax.numpy as jnp
import numpy as np
from jax import lax
from jax.experimental import pallas as pl
from jax.experimental.pallas import tpu as pltpu
from jax.sharding import PartitionSpec as P

MOM_DEV = 2
LANES = 128
TILE_CHUNK = 4
MOST_SHIFTS = 8

f32 = jnp.float32
bf16 = jnp.bfloat16

PARAMS = pltpu.CompilerParams(vmem_limit_bytes=40 * 1024 * 1024)
VMEM = pl.BlockSpec(memory_space=pltpu.VMEM)
HBM = pl.BlockSpec(memory_space=pltpu.HBM)


def dot_t(left, right):
    return lax.dot_general(left, right, (((1,), (1,)), ((), ())), preferred_element_type=f32)


def dot_n(left, right):
    return lax.dot_general(left, right, (((1,), (0,)), ((), ())), preferred_element_type=f32)


def split(value):
    high = value.astype(bf16)
    return high, (value - high.astype(f32)).astype(bf16)


def dot3_t(left, right):
    (l_hi, l_lo), (r_hi, r_lo) = left, right
    rows = l_hi.shape[0]
    both = dot_t(jnp.concatenate([l_hi, l_lo], axis=0), r_hi)
    return both[:rows] + both[rows:] + dot_t(l_hi, r_lo)


def dot3_n(left, right):
    (l_hi, l_lo), (r_hi, r_lo) = left, right
    rows = l_hi.shape[0]
    both = dot_n(jnp.concatenate([l_hi, l_lo], axis=0), r_hi)
    return both[:rows] + both[rows:] + dot_n(l_hi, r_lo)


def pick(index, values):
    result = f32(values[0])
    for i in range(1, len(values)):
        result = jnp.where(index == i, f32(values[i]), result)
    return result


def node_angle(node, nodes_all):
    return np.float32(2.0 * math.pi) * (np.float32(node) + np.float32(0.5)) / np.float32(nodes_all)


def terms_kernel(dims, *refs):
    panel_devs, blk_dev, shifted = dims
    n_out = panel_devs if shifted else 1
    indices, (contour_hbm, res_hbm, iter_hbm, probe_hbm, tiles_hbm, fr_hbm) = refs[:6], refs[6:12]
    outs, refs = refs[12 : 12 + n_out], refs[12 + n_out :]
    (pack, lines, consts), refs = refs[:3], refs[3:]
    held, (contour, tiles, fright, vec, terms, skel, acc, facc, sems) = refs[:6], refs[6:]
    tile_count = tiles.shape[0]
    far_count, _, rank, size = fright.shape
    res_rows, iter_rows = res_hbm.shape[0], iter_hbm.shape[0]
    node_dev = res_rows // 2
    chunk = TILE_CHUNK

    copies = []

    def start(source, target):
        copy = pltpu.make_async_copy(source, target, sems.at[len(copies)])
        copy.start()
        copies.append(copy)
        return copy

    res_copy = start(res_hbm, pack.at[pl.ds(0, res_rows)])
    small = [start(source, target) for source, target in zip(indices, held)]
    small.append(start(contour_hbm, contour))
    far_copy = start(fr_hbm, fright)
    tile_copies = []
    for i in range(tile_count // chunk):
        part = pl.ds(i * chunk, chunk)
        tile_copies.append(start(tiles_hbm.at[part], tiles.at[part]))
    rest = [
        start(iter_hbm, pack.at[pl.ds(res_rows, iter_rows)]),
        start(probe_hbm, lines.at[pl.ds(res_rows, 2)]),
    ]
    col, row, dest, fcol, frank, ftgt = held
    here = lax.axis_index("panels")

    def slot_of(owner):
        if shifted:
            owner = owner - here
            owner = jnp.where(owner < 0, owner + panel_devs, owner)
        return owner

    zero = jnp.zeros(acc.shape[1:], f32)
    for b in range(acc.shape[0]):
        acc[b] = zero
    for d in range(facc.shape[0]):
        facc[d] = zero

    res_copy.wait()
    for i in range(res_rows):
        lines[i] = pack[i]
    for b in range(blk_dev):
        lanes = slice(b * size, (b + 1) * size)
        re = jnp.concatenate([pack[2 * k, :, lanes] for k in range(node_dev)], axis=0)
        im = jnp.concatenate([pack[2 * k + 1, :, lanes] for k in range(node_dev)], axis=0)
        upper = jnp.concatenate([re, -im], axis=1)
        lower = jnp.concatenate([im, re], axis=1)
        vec[b] = jnp.concatenate([upper, lower], axis=0).astype(bf16)

    for copy in small:
        copy.wait()
    for i in range(consts.shape[0]):
        consts[i : i + 1, :] = jnp.full((1, LANES), contour[min(i, 2)], f32)

    rows = vec.shape[1]
    far_copy.wait()
    group = LANES // rank
    sources = vec[...].reshape(blk_dev * rows, 2 * size)
    for g in range(far_count // group):
        mats = [
            jnp.concatenate([fright[f, 0], fright[f, 1]], axis=1)
            for f in range(g * group, (g + 1) * group)
        ]
        skel[g] = dot_t(sources, jnp.concatenate(mats, axis=0)).reshape(blk_dev, rows, LANES)
    lane = lax.broadcasted_iota(jnp.int32, (rows, LANES), 1)

    def add_far(f):
        target = ftgt[f]
        owner = target // blk_dev
        place = (target - owner * blk_dev) * rank
        moved = pltpu.roll(
            skel[f // group, fcol[f]], lax.rem(place - (f % group) * rank + LANES, LANES), 1
        )
        kept = (lane >= place) & (lane < place + frank[f])
        slot = slot_of(owner)
        facc[slot] = facc[slot] + jnp.where(kept, moved, 0.0)

    def add_near(t):
        target = slot_of(dest[t]) * blk_dev + row[t]
        acc[target] = acc[target] + terms[t]

    chunks = len(tile_copies)
    for i in range(chunks + 1):
        if i < chunks:
            tile_copies[i].wait()
            for t in range(i * chunk, (i + 1) * chunk):
                tile = jnp.concatenate([tiles[t, 0], tiles[t, 1]], axis=1)
                terms[t] = dot_t(vec[col[t]], tile)
            for f in range(i * far_count // chunks, (i + 1) * far_count // chunks):
                add_far(f)
        if i:
            for t in range((i - 1) * chunk, i * chunk):
                add_near(t)

    near_rows = blk_dev * rows
    for d in range(panel_devs):
        out = outs[d] if shifted else outs[0].at[d]
        for b in range(blk_dev):
            out[b * rows : (b + 1) * rows, :] = acc[d * blk_dev + b]
        out[near_rows:, :] = facc[d]
    for copy in rest:
        copy.wait()


def product_kernel(dims, *refs):
    node_devs, nodes_all = dims
    parts, (left, pack, contour, out) = refs[:-4], refs[-4:]
    parts = [p for part in parts for p in ([part[d] for d in range(part.shape[0])] if len(part.shape) == 3 else [part[...]])]
    node_dev, _, rhs_dev, _ = out.shape
    blk_dev, _, rank, size = left.shape
    rows = 2 * node_dev * rhs_dev
    half = rows // 2

    total = parts[0]
    for part in parts[1:]:
        total = total + part
    near = total[: blk_dev * rows]
    summed = total[blk_dev * rows :]
    re, im = summed[:half], summed[half:]
    upper = jnp.concatenate([re, -im], axis=1)
    lower = jnp.concatenate([im, re], axis=1)
    whole = jnp.concatenate([upper, lower], axis=0)
    lane = lax.broadcasted_iota(jnp.int32, whole.shape, 1)
    block = lax.rem(lane, LANES) // rank
    picked = [jnp.where(block == b, whole, 0.0) for b in range(blk_dev)]
    mats = left[...]
    stacked = jnp.concatenate(
        [mats[:, 0].reshape(blk_dev * rank, size), mats[:, 1].reshape(blk_dev * rank, size)], axis=0
    )
    applied = near + dot_n(jnp.concatenate(picked, axis=0).astype(bf16), stacked)

    here = lax.axis_index("nodes")
    for k in range(node_dev):
        cosines, sines = [], []
        for x in range(node_devs):
            angle = node_angle(x * node_dev + k, nodes_all)
            cosines.append(float(np.cos(angle)))
            sines.append(float(np.sin(angle)))
        shift_re = contour[0:1, :] + contour[2:3, :] * pick(here, cosines)
        shift_im = contour[1:2, :] + contour[2:3, :] * pick(here, sines)
        for b in range(blk_dev):
            lanes = slice(b * size, (b + 1) * size)
            top = b * rows + k * rhs_dev
            r_re, r_im = pack[2 * k, :, lanes], pack[2 * k + 1, :, lanes]
            out[k, 0, :, lanes] = applied[top : top + rhs_dev] - (shift_re * r_re - shift_im * r_im)
            top = top + half
            out[k, 1, :, lanes] = applied[top : top + rhs_dev] - (shift_re * r_im + shift_im * r_re)


def side_by_side(pair, row, count):
    return jnp.concatenate([pair[row : row + count], pair[row + count : row + 2 * count]], axis=1)


def turned(pair, row, count):
    return jnp.concatenate([-pair[row + count : row + 2 * count], pair[row : row + count]], axis=1)


def joined(own, other, row):
    first = lax.axis_index("rhs") == 0
    mine, theirs = own[row], other[row]
    top = jnp.where(first, mine, theirs)
    bottom = jnp.where(first, theirs, mine)
    return jnp.concatenate([top, bottom], axis=0)


def ahead_kernel(node_devs, *refs):
    theirs, refs = refs[: node_devs - 1], refs[node_devs - 1 :]
    pack, own, other, res_hi, res_lo, message, *onward = refs
    _, rhs_dev, _ = own.shape
    cols = 2 * rhs_dev
    res_rows = own.shape[0] - 2
    node_dev = res_rows // 2

    for i in range(res_rows):
        high, low = split(joined(own, other, i))
        res_hi[i * cols : (i + 1) * cols, :] = high
        res_lo[i * cols : (i + 1) * cols, :] = low

    for there, out in zip(theirs, onward):
        for i in range(res_rows):
            out[i] = there[i]

    probe = [joined(own, other, res_rows + c) for c in range(2)]
    probe = split(jnp.concatenate(probe, axis=1))
    pair = []
    for held in (res_hi[...], res_lo[...]):
        rows = []
        for k in range(node_dev):
            rows.append(side_by_side(held, k * 2 * cols, cols))
            rows.append(-turned(held, k * 2 * cols, cols))
        pair.append(jnp.concatenate(rows, axis=0))
    probe_res = dot3_t(probe, tuple(pair))
    rows = []
    for k in range(node_dev):
        i_re, i_im = pack[res_rows + 2 * k], pack[res_rows + 2 * k + 1]
        rows.append(jnp.concatenate([i_re, i_im], axis=1))
        rows.append(jnp.concatenate([i_im, -i_re], axis=1))
    probe_iter = dot3_t(split(jnp.concatenate(rows, axis=0)), probe)

    message[:rhs_dev, :] = jnp.zeros((rhs_dev, LANES), f32)
    pieces = [jnp.zeros((rhs_dev, LANES // 2), f32)]
    pieces.extend(probe_iter[q * rhs_dev : (q + 1) * rhs_dev] for q in range(res_rows))
    message[rhs_dev:cols, :] = jnp.concatenate(pieces, axis=1)
    message[cols:, :] = jnp.concatenate([probe_res[:rhs_dev], probe_res[rhs_dev:]], axis=1)


def node_weight(here, scale, node_devs, node_dev, nodes_all, p, s, k):
    cosines, sines = [], []
    for x in range(node_devs):
        node = (x - s) % node_devs * node_dev + k
        power = x * MOM_DEV + p
        angle = np.float32(power + 1) * node_angle(node, nodes_all)
        cosines.append(float(np.cos(angle)))
        sines.append(float(np.sin(angle)))
    return scale * pick(here, cosines), scale * pick(here, sines)


def gram_kernel(own, other, res_hi, res_lo, ahead, message, prod_hi, prod_lo):
    node_dev, _, rhs_dev, _ = own.shape
    cols = 2 * rhs_dev
    for k in range(node_dev):
        for c in range(2):
            high, low = split(joined(own, other, (k, c)))
            top = (k * 2 + c) * cols
            prod_hi[top : top + cols, :] = high
            prod_lo[top : top + cols, :] = low
    sums = []
    for k in range(node_dev):
        top = k * 2 * cols
        left, right = [], []
        for p_ref, r_ref in ((prod_hi, res_hi), (prod_lo, res_lo)):
            product, source = p_ref[...], r_ref[: node_dev * 2 * cols, :]
            plain = side_by_side(product, top, cols)
            left.append(jnp.concatenate([plain, side_by_side(source, top, cols)], axis=0))
            right.append(jnp.concatenate([plain, turned(product, top, cols)], axis=0))
        sums.append(dot3_t(tuple(left), tuple(right)))
    gram = jnp.concatenate(sums, axis=1)
    half = LANES // 2
    first = lax.axis_index("rhs") == 0
    cross = jnp.where(first, gram[cols : cols + rhs_dev], gram[cols + rhs_dev :])
    message[:rhs_dev, :] = jnp.concatenate([gram[:rhs_dev], gram[rhs_dev:cols]], axis=1)
    message[rhs_dev:cols, :] = jnp.concatenate([cross, ahead[rhs_dev:cols, half:]], axis=1)
    message[cols:, :] = ahead[cols:, :]


def finish_kernel(dims, *refs):
    n_parts, node_devs, nodes_all, scale_factor = dims
    it = iter(refs)
    parts = [[next(it) for _ in range(n_parts)] for _ in range(node_devs)]
    packs = [next(it) for _ in range(node_devs)]
    others = [None] + [next(it) for _ in range(node_devs - 1)]
    prod_hi, prod_lo, res_hi, res_lo, contour, next_out, mom_out, hankel_out = it
    node_dev, _, rhs_dev, width = next_out.shape
    cols = 2 * rhs_dev
    half = LANES // 2
    res_rows = 2 * node_dev
    here = lax.axis_index("nodes")

    sums = [sum((part[...] for part in group[1:]), group[0][...]) for group in parts]
    if node_devs % 2:
        sums.append(sums[0])

    shape = (rhs_dev, LANES)
    lane = lax.broadcasted_iota(jnp.int32, shape, 1)
    low_half = lane < half
    base = (lane // (2 * cols)) * (2 * cols)
    spot = lax.rem(lane, cols)
    real_lane = lax.rem(lane, 2 * cols) < cols
    swapped = jnp.where(real_lane, lane + cols, lane - cols)
    sign = jnp.where(real_lane, -1.0, 1.0)

    def gathered(value, index):
        return jnp.take_along_axis(value, index, axis=1, mode="promise_in_bounds")

    solved, probe_res = [], []
    for g in range(len(sums) // 2):
        s0, s1 = sums[2 * g], sums[2 * g + 1]
        r0, r1 = pltpu.roll(s0, half, 1), pltpu.roll(s1, half, 1)
        v0, v1, v2 = [slice(i * rhs_dev, (i + 1) * rhs_dev) for i in range(3)]
        block = [
            jnp.where(low_half, s0[v0], r1[v0]),
            jnp.where(low_half, r0[v0], s1[v0]),
            jnp.where(low_half, s0[v1], r1[v1]),
        ]
        probe_res.append(
            jnp.concatenate(
                [jnp.where(low_half, s0[v2], r1[v2]), jnp.where(low_half, r0[v2], s1[v2])], axis=0
            )
        )
        for j in range(0, cols, 2):
            at, r = divmod(j, rhs_dev)
            line = block[at]
            crossed = gathered(line, swapped) * sign
            columns = [
                [gathered(value, base + spot_at) for value in block[at:]]
                for spot_at in (j, cols + j, j + 1, cols + j + 1)
            ]
            pivot = (spot == j) | (spot == j + 1)
            g, crossed_g = [], []
            for i in range(2):
                one = spot == j + i
                row = jnp.where(pivot[:1], 0.0, line[r + i : r + i + 1])
                g.append(jnp.where((one & real_lane)[:1], -1.0, row))
                row = jnp.where(pivot[:1], 0.0, crossed[r + i : r + i + 1])
                crossed_g.append(jnp.where((one & ~real_lane)[:1], -1.0, row))
            inverse_p = 1.0 / columns[0][0][r : r + 1]
            b_re, b_im = columns[0][0][r + 1 : r + 2], columns[1][0][r + 1 : r + 2]
            t_re, t_im = b_re * inverse_p, b_im * inverse_p
            inverse_s = 1.0 / (columns[2][0][r + 1 : r + 2] - (t_re * b_re + t_im * b_im))
            h = (g[1] - (g[0] * t_re + crossed_g[0] * t_im)) * inverse_s
            crossed_h = (crossed_g[1] - (crossed_g[0] * t_re - g[0] * t_im)) * inverse_s
            f = g[0] * inverse_p - (h * t_re - crossed_h * t_im)
            crossed_f = crossed_g[0] * inverse_p - (crossed_h * t_re + h * t_im)
            for i in range(at, 3):
                c0_re, c0_im, c1_re, c1_im = [value[i - at] for value in columns]
                change = (c0_re * f + c0_im * crossed_f) + (c1_re * h + c1_im * crossed_h)
                block[i] = jnp.where(pivot, 0.0, block[i]) - change
        solved.append(block[2])

    coef = solved[0]
    cross = gathered(coef, swapped)
    plain = jnp.where(real_lane, coef, -coef)
    node_of = lane // (2 * cols)
    rows = []
    for k in range(node_dev):
        rows.append(jnp.where(node_of == k, plain, 0.0))
        rows.append(jnp.where(node_of == k, cross, 0.0))
    used = node_dev * 2 * cols
    left = split(jnp.concatenate(rows, axis=0)[:, :used])
    change = dot3_n(left, (prod_hi[...], prod_lo[...]))
    for k in range(node_dev):
        for c in range(2):
            top = (k * 2 + c) * rhs_dev
            next_out[k, c] = packs[0][2 * k + c] - change[top : top + rhs_dev]

    scale = contour[2:3, :] / nodes_all
    weighted = []
    for g, coef in enumerate(solved):
        cross = gathered(coef, swapped)
        rows = []
        for p in range(MOM_DEV):
            w_re = jnp.zeros(shape, f32)
            w_im = jnp.zeros(shape, f32)
            for i in range(2):
                s = 2 * g + i
                if s >= node_devs:
                    continue
                for k in range(node_dev):
                    n_re, n_im = node_weight(here, scale, node_devs, node_dev, nodes_all, p, s, k)
                    mine = node_of == i * node_dev + k
                    w_re = jnp.where(mine, n_re, w_re)
                    w_im = jnp.where(mine, n_im, w_im)
            rows.append(-sign * w_re * coef - w_im * cross)
            rows.append(-sign * w_im * coef + w_re * cross)
        weighted.append(jnp.concatenate(rows, axis=0))
    hankel = None
    products = None
    for g, value in enumerate(weighted):
        depth = min(LANES, node_devs * used - g * LANES)
        left = split(value)
        cut = tuple(part[:, :depth] for part in left)
        highs, lows = [], []
        for i in range(depth // used):
            s = 2 * g + i
            if s == 0:
                highs.append(res_hi[...])
                lows.append(res_lo[...])
                continue
            for q in range(res_rows):
                high, low = split(joined(packs[s], others[s], q))
                highs.append(high)
                lows.append(low)
        term = dot3_n(cut, (jnp.concatenate(highs, axis=0), jnp.concatenate(lows, axis=0)))
        products = term if products is None else products + term
        term = dot3_t(left, split(probe_res[g]))
        hankel = term if hankel is None else hankel + term

    wide = jnp.concatenate([scale] * (width // LANES), axis=1)
    for p in range(MOM_DEV):
        mom = [products[(2 * p + c) * rhs_dev : (2 * p + c + 1) * rhs_dev] for c in range(2)]
        han = [hankel[(2 * p + c) * rhs_dev : (2 * p + c + 1) * rhs_dev] for c in range(2)]
        for s in range(node_devs):
            for k in range(node_dev):
                w_re, w_im = node_weight(here, wide, node_devs, node_dev, nodes_all, p, s, k)
                i_re, i_im = packs[s][res_rows + 2 * k], packs[s][res_rows + 2 * k + 1]
                mom[0] = mom[0] + (w_re * i_re - w_im * i_im)
                mom[1] = mom[1] + (w_re * i_im + w_im * i_re)
                i_re, i_im = [
                    pltpu.roll(sums[s][rhs_dev:cols], half - (2 * k + c) * cols, 1)[:, :cols]
                    for c in range(2)
                ]
                w_re, w_im = w_re[:, :cols], w_im[:, :cols]
                han[0] = han[0] + (w_re * i_re - w_im * i_im)
                han[1] = han[1] + (w_re * i_im + w_im * i_re)
        for c in range(2):
            mom_out[p, c] = mom[c]
            hankel_out[p, c] = han[c] * scale_factor


def call(kernel, out_shape, args, in_specs=None, scratch=(), cost=None):
    args = tuple(args)
    multiple = isinstance(out_shape, (list, tuple))
    return pl.pallas_call(
        kernel,
        out_shape=out_shape,
        in_specs=[VMEM] * len(args) if in_specs is None else in_specs,
        out_specs=[VMEM] * len(out_shape) if multiple else VMEM,
        scratch_shapes=list(scratch),
        compiler_params=PARAMS,
        cost_estimate=cost,
    )(*args)


def struct(shape, dtype=f32):
    return jax.ShapeDtypeStruct(shape, dtype)


def per_device(
    residual,
    iterate,
    probe,
    contour,
    near_tiles,
    near_col,
    near_row,
    near_dest,
    far_right,
    far_col,
    far_rank,
    far_target,
    far_left,
):
    node_dev, _, rhs_dev, rows_dev = residual.shape
    tile_count, _, size, _ = near_tiles.shape
    far_count, _, rank, _ = far_right.shape
    blk_dev = rows_dev // size
    panel_devs = lax.axis_size("panels")
    node_devs = lax.axis_size("nodes")
    nodes_all = node_dev * node_devs
    vec_rows = 2 * node_dev * rhs_dev
    cols = 2 * rhs_dev
    res_rows = 2 * node_dev
    span = res_rows * cols

    part_rows = blk_dev * vec_rows + vec_rows
    copies = 6 + 1 + tile_count // TILE_CHUNK + 4
    field = (rhs_dev, rows_dev)
    indices = (near_col, near_row, near_dest.reshape(tile_count), far_col, far_rank, far_target)
    shifted = panel_devs <= MOST_SHIFTS
    out_shape = [struct((part_rows, LANES))] * panel_devs if shifted else [struct((panel_devs, part_rows, LANES))]
    in_hbm = functools.partial(pltpu.with_memory_space_constraint, memory_space=pltpu.HBM)
    *terms, pack, lines, consts = call(
        functools.partial(terms_kernel, (panel_devs, blk_dev, shifted)),
        [
            *out_shape,
            struct((2 * res_rows, *field)),
            struct((res_rows + 2, *field)),
            struct((8, LANES)),
        ],
        map(in_hbm, (
            *indices,
            contour,
            residual.reshape(res_rows, rhs_dev, rows_dev),
            iterate.reshape(res_rows, rhs_dev, rows_dev),
            probe,
            near_tiles,
            far_right,
        )),
        in_specs=[HBM] * 12,
        scratch=[
            *[pltpu.SMEM(index.shape, jnp.int32) for index in indices],
            pltpu.SMEM(contour.shape, f32),
            pltpu.VMEM(near_tiles.shape, bf16),
            pltpu.VMEM(far_right.shape, bf16),
            pltpu.VMEM((blk_dev, vec_rows, 2 * size), bf16),
            pltpu.VMEM((tile_count, vec_rows, size), f32),
            pltpu.VMEM((far_count * rank // LANES, blk_dev, vec_rows, LANES), f32),
            pltpu.VMEM((panel_devs * blk_dev, vec_rows, size), f32),
            pltpu.VMEM((panel_devs, vec_rows, LANES), f32),
            pltpu.SemaphoreType.DMA((copies,)),
        ],
    )

    if shifted:
        parts = terms[:1]
        for d in range(1, panel_devs):
            pairs = [(i, (i + d) % panel_devs) for i in range(panel_devs)]
            parts.append(lax.ppermute(terms[d], "panels", pairs))
    else:
        parts = [lax.all_to_all(terms[0], "panels", split_axis=0, concat_axis=0, tiled=True)]

    swap = [(0, 1), (1, 0)]
    there = lax.ppermute(lines, "rhs", swap)
    node_pairs = [[(i, (i + s) % node_devs) for i in range(node_devs)] for s in range(node_devs)]
    packs = [pack] + [lax.ppermute(pack, "nodes", pairs) for pairs in node_pairs[1:]]

    product = call(
        functools.partial(product_kernel, (node_devs, nodes_all)),
        struct(residual.shape),
        (*parts, far_left.transpose(0, 1, 3, 2), pack, consts),
    )
    res_hi, res_lo, ahead, *onward = call(
        functools.partial(ahead_kernel, node_devs),
        [struct((span, rows_dev), bf16), struct((span, rows_dev), bf16), struct((3 * rhs_dev, LANES))]
        + [struct((res_rows, *field))] * (node_devs - 1),
        (*packs[1:], pack, lines, there),
    )
    others = [lax.ppermute(value, "rhs", swap) for value in onward]
    message, prod_hi, prod_lo = call(
        gram_kernel,
        [
            struct((3 * rhs_dev, LANES)),
            struct((span, rows_dev), bf16),
            struct((span, rows_dev), bf16),
        ],
        (product, lax.ppermute(product, "rhs", swap), res_hi, res_lo, ahead),
    )

    if shifted:
        total = message
        for d in range(panel_devs - 1, 0, -1):
            pairs = [(i, (i + d) % panel_devs) for i in range(panel_devs)]
            total = total + lax.ppermute(message, "panels", pairs)
    else:
        total = lax.psum(message, "panels")
    sums = [total] + [lax.ppermute(total, "nodes", pairs) for pairs in node_pairs[1:]]
    scale_factor = 1.0 / math.sqrt(rows_dev * panel_devs)
    residual_next, moments, hankel = call(
        functools.partial(finish_kernel, (1, node_devs, nodes_all, scale_factor)),
        [
            struct(residual.shape),
            struct((MOM_DEV, 2, rhs_dev, rows_dev)),
            struct((MOM_DEV, 2, rhs_dev, cols)),
        ],
        (*sums, *packs, *others, prod_hi, prod_lo, res_hi, res_lo, consts),
    )
    return residual_next, moments, hankel.transpose(0, 1, 3, 2)


def solution(mesh):
    return jax.shard_map(
        per_device,
        mesh=mesh,
        in_specs=(
            P(("groups", "nodes"), None, "rhs", "panels"),
            P(("groups", "nodes"), None, "rhs", "panels"),
            P("groups", "rhs", "panels"),
            P("groups"),
            P(("groups", "panels"), None, None, None),
            P(("groups", "panels")),
            P(("groups", "panels")),
            P(("groups", "panels"), None),
            P(("groups", "panels"), None, None, None),
            P(("groups", "panels")),
            P(("groups", "panels")),
            P(("groups", "panels")),
            P(("groups", "panels"), None, None, None),
        ),
        out_specs=(
            P(("groups", "nodes"), None, "rhs", "panels"),
            P(("groups", "nodes"), None, "rhs", "panels"),
            P(("groups", "nodes"), None, None, "rhs"),
        ),
        check_vma=False,
    )
```

```python
import functools
import math

import jax
import jax.numpy as jnp
import numpy as np
from jax import lax
from jax.experimental import pallas as pl
from jax.experimental.pallas import tpu as pltpu
from jax.sharding import PartitionSpec as P

MOM_DEV = 2
LANES = 128
TILE_CHUNK = 4
MOST_SHIFTS = 8

f32 = jnp.float32
bf16 = jnp.bfloat16

PARAMS = pltpu.CompilerParams(vmem_limit_bytes=40 * 1024 * 1024)
VMEM = pl.BlockSpec(memory_space=pltpu.VMEM)
HBM = pl.BlockSpec(memory_space=pltpu.HBM)


def dot_t(left, right):
    return lax.dot_general(left, right, (((1,), (1,)), ((), ())), preferred_element_type=f32)


def dot_n(left, right):
    return lax.dot_general(left, right, (((1,), (0,)), ((), ())), preferred_element_type=f32)


def split(value):
    high = value.astype(bf16)
    return high, (value - high.astype(f32)).astype(bf16)


def dot3_t(left, right):
    (l_hi, l_lo), (r_hi, r_lo) = left, right
    rows = l_hi.shape[0]
    both = dot_t(jnp.concatenate([l_hi, l_lo], axis=0), r_hi)
    return both[:rows] + both[rows:] + dot_t(l_hi, r_lo)


def dot3_n(left, right):
    (l_hi, l_lo), (r_hi, r_lo) = left, right
    rows = l_hi.shape[0]
    both = dot_n(jnp.concatenate([l_hi, l_lo], axis=0), r_hi)
    return both[:rows] + both[rows:] + dot_n(l_hi, r_lo)


def pick(index, values):
    result = f32(values[0])
    for i in range(1, len(values)):
        result = jnp.where(index == i, f32(values[i]), result)
    return result


def node_angle(node, nodes_all):
    return np.float32(2.0 * math.pi) * (np.float32(node) + np.float32(0.5)) / np.float32(nodes_all)


def terms_kernel(dims, *refs):
    panel_devs, blk_dev, shifted = dims
    n_out = panel_devs if shifted else 1
    indices, (contour_hbm, res_hbm, iter_hbm, probe_hbm, tiles_hbm, fr_hbm) = refs[:6], refs[6:12]
    outs, refs = refs[12 : 12 + n_out], refs[12 + n_out :]
    (pack, lines, consts), refs = refs[:3], refs[3:]
    held, (contour, tiles, fright, vec, terms, skel, acc, facc, sems) = refs[:6], refs[6:]
    tile_count = tiles.shape[0]
    far_count, _, rank, size = fright.shape
    res_rows, iter_rows = res_hbm.shape[0], iter_hbm.shape[0]
    node_dev = res_rows // 2
    chunk = TILE_CHUNK

    copies = []

    def start(source, target):
        copy = pltpu.make_async_copy(source, target, sems.at[len(copies)])
        copy.start()
        copies.append(copy)
        return copy

    res_copy = start(res_hbm, pack.at[pl.ds(0, res_rows)])
    small = [start(source, target) for source, target in zip(indices, held)]
    small.append(start(contour_hbm, contour))
    far_copy = start(fr_hbm, fright)
    tile_copies = []
    for i in range(tile_count // chunk):
        part = pl.ds(i * chunk, chunk)
        tile_copies.append(start(tiles_hbm.at[part], tiles.at[part]))
    rest = [
        start(iter_hbm, pack.at[pl.ds(res_rows, iter_rows)]),
        start(probe_hbm, lines.at[pl.ds(res_rows, 2)]),
    ]
    col, row, dest, fcol, frank, ftgt = held
    here = lax.axis_index("panels")

    def slot_of(owner):
        if shifted:
            owner = owner - here
            owner = jnp.where(owner < 0, owner + panel_devs, owner)
        return owner

    zero = jnp.zeros(acc.shape[1:], f32)
    for b in range(acc.shape[0]):
        acc[b] = zero
    for d in range(facc.shape[0]):
        facc[d] = zero

    res_copy.wait()
    for i in range(res_rows):
        lines[i] = pack[i]
    for b in range(blk_dev):
        lanes = slice(b * size, (b + 1) * size)
        re = jnp.concatenate([pack[2 * k, :, lanes] for k in range(node_dev)], axis=0)
        im = jnp.concatenate([pack[2 * k + 1, :, lanes] for k in range(node_dev)], axis=0)
        upper = jnp.concatenate([re, -im], axis=1)
        lower = jnp.concatenate([im, re], axis=1)
        vec[b] = jnp.concatenate([upper, lower], axis=0).astype(bf16)

    for copy in small:
        copy.wait()
    for i in range(consts.shape[0]):
        consts[i : i + 1, :] = jnp.full((1, LANES), contour[min(i, 2)], f32)

    rows = vec.shape[1]
    far_copy.wait()
    group = LANES // rank
    sources = vec[...].reshape(blk_dev * rows, 2 * size)
    for g in range(far_count // group):
        mats = [
            jnp.concatenate([fright[f, 0], fright[f, 1]], axis=1)
            for f in range(g * group, (g + 1) * group)
        ]
        skel[g] = dot_t(sources, jnp.concatenate(mats, axis=0)).reshape(blk_dev, rows, LANES)
    lane = lax.broadcasted_iota(jnp.int32, (rows, LANES), 1)

    def add_far(f):
        target = ftgt[f]
        owner = target // blk_dev
        place = (target - owner * blk_dev) * rank
        moved = pltpu.roll(
            skel[f // group, fcol[f]], lax.rem(place - (f % group) * rank + LANES, LANES), 1
        )
        kept = (lane >= place) & (lane < place + frank[f])
        slot = slot_of(owner)
        facc[slot] = facc[slot] + jnp.where(kept, moved, 0.0)

    def add_near(t):
        target = slot_of(dest[t]) * blk_dev + row[t]
        acc[target] = acc[target] + terms[t]

    chunks = len(tile_copies)
    for i in range(chunks + 1):
        if i < chunks:
            tile_copies[i].wait()
            for t in range(i * chunk, (i + 1) * chunk, 2):
                pair = [jnp.concatenate([tiles[u, 0], tiles[u, 1]], axis=1) for u in (t, t + 1)]
                left = jnp.concatenate([vec[col[t]], vec[col[t + 1]]], axis=0)
                both = dot_t(left, jnp.concatenate(pair, axis=0))
                terms[t] = both[:rows, :size]
                terms[t + 1] = both[rows:, size:]
            for f in range(i * far_count // chunks, (i + 1) * far_count // chunks):
                add_far(f)
        if i:
            for t in range((i - 1) * chunk, i * chunk):
                add_near(t)

    near_rows = blk_dev * rows
    for d in range(panel_devs):
        out = outs[d] if shifted else outs[0].at[d]
        for b in range(blk_dev):
            out[b * rows : (b + 1) * rows, :] = acc[d * blk_dev + b]
        out[near_rows:, :] = facc[d]
    for copy in rest:
        copy.wait()


def product_kernel(dims, *refs):
    node_devs, nodes_all = dims
    parts, (left, pack, contour, out) = refs[:-4], refs[-4:]
    parts = [p for part in parts for p in ([part[d] for d in range(part.shape[0])] if len(part.shape) == 3 else [part[...]])]
    node_dev, _, rhs_dev, _ = out.shape
    blk_dev, _, rank, size = left.shape
    rows = 2 * node_dev * rhs_dev
    half = rows // 2

    total = parts[0]
    for part in parts[1:]:
        total = total + part
    near = total[: blk_dev * rows]
    summed = total[blk_dev * rows :]
    re, im = summed[:half], summed[half:]
    upper = jnp.concatenate([re, -im], axis=1)
    lower = jnp.concatenate([im, re], axis=1)
    whole = jnp.concatenate([upper, lower], axis=0)
    lane = lax.broadcasted_iota(jnp.int32, whole.shape, 1)
    block = lax.rem(lane, LANES) // rank
    picked = [jnp.where(block == b, whole, 0.0) for b in range(blk_dev)]
    mats = left[...]
    stacked = jnp.concatenate(
        [mats[:, 0].reshape(blk_dev * rank, size), mats[:, 1].reshape(blk_dev * rank, size)], axis=0
    )
    applied = near + dot_n(jnp.concatenate(picked, axis=0).astype(bf16), stacked)

    here = lax.axis_index("nodes")
    for k in range(node_dev):
        cosines, sines = [], []
        for x in range(node_devs):
            angle = node_angle(x * node_dev + k, nodes_all)
            cosines.append(float(np.cos(angle)))
            sines.append(float(np.sin(angle)))
        shift_re = contour[0:1, :] + contour[2:3, :] * pick(here, cosines)
        shift_im = contour[1:2, :] + contour[2:3, :] * pick(here, sines)
        for b in range(blk_dev):
            lanes = slice(b * size, (b + 1) * size)
            top = b * rows + k * rhs_dev
            r_re, r_im = pack[2 * k, :, lanes], pack[2 * k + 1, :, lanes]
            out[k, 0, :, lanes] = applied[top : top + rhs_dev] - (shift_re * r_re - shift_im * r_im)
            top = top + half
            out[k, 1, :, lanes] = applied[top : top + rhs_dev] - (shift_re * r_im + shift_im * r_re)


def side_by_side(pair, row, count):
    return jnp.concatenate([pair[row : row + count], pair[row + count : row + 2 * count]], axis=1)


def turned(pair, row, count):
    return jnp.concatenate([-pair[row + count : row + 2 * count], pair[row : row + count]], axis=1)


def joined(own, other, row):
    first = lax.axis_index("rhs") == 0
    mine, theirs = own[row], other[row]
    top = jnp.where(first, mine, theirs)
    bottom = jnp.where(first, theirs, mine)
    return jnp.concatenate([top, bottom], axis=0)


def ahead_kernel(node_devs, *refs):
    theirs, refs = refs[: node_devs - 1], refs[node_devs - 1 :]
    pack, own, other, res_hi, res_lo, message, *onward = refs
    _, rhs_dev, _ = own.shape
    cols = 2 * rhs_dev
    res_rows = own.shape[0] - 2
    node_dev = res_rows // 2

    for i in range(res_rows):
        high, low = split(joined(own, other, i))
        res_hi[i * cols : (i + 1) * cols, :] = high
        res_lo[i * cols : (i + 1) * cols, :] = low

    for there, out in zip(theirs, onward):
        for i in range(res_rows):
            out[i] = there[i]

    probe = [joined(own, other, res_rows + c) for c in range(2)]
    probe = split(jnp.concatenate(probe, axis=1))
    pair = []
    for held in (res_hi[...], res_lo[...]):
        rows = []
        for k in range(node_dev):
            rows.append(side_by_side(held, k * 2 * cols, cols))
            rows.append(-turned(held, k * 2 * cols, cols))
        pair.append(jnp.concatenate(rows, axis=0))
    probe_res = dot3_t(probe, tuple(pair))
    rows = []
    for k in range(node_dev):
        i_re, i_im = pack[res_rows + 2 * k], pack[res_rows + 2 * k + 1]
        rows.append(jnp.concatenate([i_re, i_im], axis=1))
        rows.append(jnp.concatenate([i_im, -i_re], axis=1))
    probe_iter = dot3_t(split(jnp.concatenate(rows, axis=0)), probe)

    message[:rhs_dev, :] = jnp.zeros((rhs_dev, LANES), f32)
    pieces = [jnp.zeros((rhs_dev, LANES // 2), f32)]
    pieces.extend(probe_iter[q * rhs_dev : (q + 1) * rhs_dev] for q in range(res_rows))
    message[rhs_dev:cols, :] = jnp.concatenate(pieces, axis=1)
    message[cols:, :] = jnp.concatenate([probe_res[:rhs_dev], probe_res[rhs_dev:]], axis=1)


def node_weight(here, scale, node_devs, node_dev, nodes_all, p, s, k):
    cosines, sines = [], []
    for x in range(node_devs):
        node = (x - s) % node_devs * node_dev + k
        power = x * MOM_DEV + p
        angle = np.float32(power + 1) * node_angle(node, nodes_all)
        cosines.append(float(np.cos(angle)))
        sines.append(float(np.sin(angle)))
    return scale * pick(here, cosines), scale * pick(here, sines)


def gram_kernel(own, other, res_hi, res_lo, ahead, message, prod_hi, prod_lo):
    node_dev, _, rhs_dev, _ = own.shape
    cols = 2 * rhs_dev
    for k in range(node_dev):
        for c in range(2):
            high, low = split(joined(own, other, (k, c)))
            top = (k * 2 + c) * cols
            prod_hi[top : top + cols, :] = high
            prod_lo[top : top + cols, :] = low
    sums = []
    for k in range(node_dev):
        top = k * 2 * cols
        left, right = [], []
        for p_ref, r_ref in ((prod_hi, res_hi), (prod_lo, res_lo)):
            product, source = p_ref[...], r_ref[: node_dev * 2 * cols, :]
            plain = side_by_side(product, top, cols)
            left.append(jnp.concatenate([plain, side_by_side(source, top, cols)], axis=0))
            right.append(jnp.concatenate([plain, turned(product, top, cols)], axis=0))
        sums.append(dot3_t(tuple(left), tuple(right)))
    gram = jnp.concatenate(sums, axis=1)
    half = LANES // 2
    first = lax.axis_index("rhs") == 0
    cross = jnp.where(first, gram[cols : cols + rhs_dev], gram[cols + rhs_dev :])
    message[:rhs_dev, :] = jnp.concatenate([gram[:rhs_dev], gram[rhs_dev:cols]], axis=1)
    message[rhs_dev:cols, :] = jnp.concatenate([cross, ahead[rhs_dev:cols, half:]], axis=1)
    message[cols:, :] = ahead[cols:, :]


def finish_kernel(dims, *refs):
    n_parts, node_devs, nodes_all, scale_factor = dims
    it = iter(refs)
    parts = [next(it) for _ in range(n_parts)]
    packs = [next(it) for _ in range(node_devs)]
    others = [None] + [next(it) for _ in range(node_devs - 1)]
    prod_hi, prod_lo, res_hi, res_lo, contour, next_out, mom_out, hankel_out = it
    node_dev, _, rhs_dev, width = next_out.shape
    cols = 2 * rhs_dev
    half = LANES // 2
    res_rows = 2 * node_dev
    here = lax.axis_index("nodes")

    tall = 3 * rhs_dev
    sums = [part[i : i + tall, :] for part in parts for i in range(0, part.shape[0], tall)]
    if node_devs % 2:
        sums.append(sums[0])

    shape = (rhs_dev, LANES)
    lane = lax.broadcasted_iota(jnp.int32, shape, 1)
    low_half = lane < half
    base = (lane // (2 * cols)) * (2 * cols)
    spot = lax.rem(lane, cols)
    real_lane = lax.rem(lane, 2 * cols) < cols
    swapped = jnp.where(real_lane, lane + cols, lane - cols)
    sign = jnp.where(real_lane, -1.0, 1.0)

    def gathered(value, index):
        return jnp.take_along_axis(value, index, axis=1, mode="promise_in_bounds")

    solved, probe_res = [], []
    for g in range(len(sums) // 2):
        s0, s1 = sums[2 * g], sums[2 * g + 1]
        r0, r1 = pltpu.roll(s0, half, 1), pltpu.roll(s1, half, 1)
        v0, v1, v2 = [slice(i * rhs_dev, (i + 1) * rhs_dev) for i in range(3)]
        block = [
            jnp.where(low_half, s0[v0], r1[v0]),
            jnp.where(low_half, r0[v0], s1[v0]),
            jnp.where(low_half, s0[v1], r1[v1]),
        ]
        probe_res.append(
            jnp.concatenate(
                [jnp.where(low_half, s0[v2], r1[v2]), jnp.where(low_half, r0[v2], s1[v2])], axis=0
            )
        )
        for j in range(0, cols, 2):
            at, r = divmod(j, rhs_dev)
            line = block[at]
            crossed = gathered(line, swapped) * sign
            columns = [
                [gathered(value, base + spot_at) for value in block[at:]]
                for spot_at in (j, cols + j, j + 1, cols + j + 1)
            ]
            pivot = (spot == j) | (spot == j + 1)
            g, crossed_g = [], []
            for i in range(2):
                one = spot == j + i
                row = jnp.where(pivot[:1], 0.0, line[r + i : r + i + 1])
                g.append(jnp.where((one & real_lane)[:1], -1.0, row))
                row = jnp.where(pivot[:1], 0.0, crossed[r + i : r + i + 1])
                crossed_g.append(jnp.where((one & ~real_lane)[:1], -1.0, row))
            inverse_p = 1.0 / columns[0][0][r : r + 1]
            b_re, b_im = columns[0][0][r + 1 : r + 2], columns[1][0][r + 1 : r + 2]
            t_re, t_im = b_re * inverse_p, b_im * inverse_p
            inverse_s = 1.0 / (columns[2][0][r + 1 : r + 2] - (t_re * b_re + t_im * b_im))
            h = (g[1] - (g[0] * t_re + crossed_g[0] * t_im)) * inverse_s
            crossed_h = (crossed_g[1] - (crossed_g[0] * t_re - g[0] * t_im)) * inverse_s
            f = g[0] * inverse_p - (h * t_re - crossed_h * t_im)
            crossed_f = crossed_g[0] * inverse_p - (crossed_h * t_re + h * t_im)
            for i in range(at, 3):
                c0_re, c0_im, c1_re, c1_im = [value[i - at] for value in columns]
                change = (c0_re * f + c0_im * crossed_f) + (c1_re * h + c1_im * crossed_h)
                block[i] = jnp.where(pivot, 0.0, block[i]) - change
        solved.append(block[2])

    coef = solved[0]
    cross = gathered(coef, swapped)
    plain = jnp.where(real_lane, coef, -coef)
    node_of = lane // (2 * cols)
    rows = []
    for k in range(node_dev):
        rows.append(jnp.where(node_of == k, plain, 0.0))
        rows.append(jnp.where(node_of == k, cross, 0.0))
    used = node_dev * 2 * cols
    left = split(jnp.concatenate(rows, axis=0)[:, :used])
    change = dot3_n(left, (prod_hi[...], prod_lo[...]))
    for k in range(node_dev):
        for c in range(2):
            top = (k * 2 + c) * rhs_dev
            next_out[k, c] = packs[0][2 * k + c] - change[top : top + rhs_dev]

    scale = contour[2:3, :] / nodes_all
    weighted = []
    for g, coef in enumerate(solved):
        cross = gathered(coef, swapped)
        rows = []
        for p in range(MOM_DEV):
            w_re = jnp.zeros(shape, f32)
            w_im = jnp.zeros(shape, f32)
            for i in range(2):
                s = 2 * g + i
                if s >= node_devs:
                    continue
                for k in range(node_dev):
                    n_re, n_im = node_weight(here, scale, node_devs, node_dev, nodes_all, p, s, k)
                    mine = node_of == i * node_dev + k
                    w_re = jnp.where(mine, n_re, w_re)
                    w_im = jnp.where(mine, n_im, w_im)
            rows.append(-sign * w_re * coef - w_im * cross)
            rows.append(-sign * w_im * coef + w_re * cross)
        weighted.append(jnp.concatenate(rows, axis=0))
    hankel = None
    products = None
    for g, value in enumerate(weighted):
        depth = min(LANES, node_devs * used - g * LANES)
        left = split(value)
        cut = tuple(part[:, :depth] for part in left)
        highs, lows = [], []
        for i in range(depth // used):
            s = 2 * g + i
            if s == 0:
                highs.append(res_hi[...])
                lows.append(res_lo[...])
                continue
            for q in range(res_rows):
                high, low = split(joined(packs[s], others[s], q))
                highs.append(high)
                lows.append(low)
        term = dot3_n(cut, (jnp.concatenate(highs, axis=0), jnp.concatenate(lows, axis=0)))
        products = term if products is None else products + term
        term = dot3_t(left, split(probe_res[g]))
        hankel = term if hankel is None else hankel + term

    wide = jnp.concatenate([scale] * (width // LANES), axis=1)
    for p in range(MOM_DEV):
        mom = [products[(2 * p + c) * rhs_dev : (2 * p + c + 1) * rhs_dev] for c in range(2)]
        han = [hankel[(2 * p + c) * rhs_dev : (2 * p + c + 1) * rhs_dev] for c in range(2)]
        for s in range(node_devs):
            for k in range(node_dev):
                w_re, w_im = node_weight(here, wide, node_devs, node_dev, nodes_all, p, s, k)
                i_re, i_im = packs[s][res_rows + 2 * k], packs[s][res_rows + 2 * k + 1]
                mom[0] = mom[0] + (w_re * i_re - w_im * i_im)
                mom[1] = mom[1] + (w_re * i_im + w_im * i_re)
                i_re, i_im = [
                    pltpu.roll(sums[s][rhs_dev:cols], half - (2 * k + c) * cols, 1)[:, :cols]
                    for c in range(2)
                ]
                w_re, w_im = w_re[:, :cols], w_im[:, :cols]
                han[0] = han[0] + (w_re * i_re - w_im * i_im)
                han[1] = han[1] + (w_re * i_im + w_im * i_re)
        for c in range(2):
            mom_out[p, c] = mom[c]
            hankel_out[p, c] = han[c] * scale_factor


def call(kernel, out_shape, args, in_specs=None, scratch=(), cost=None):
    args = tuple(args)
    multiple = isinstance(out_shape, (list, tuple))
    return pl.pallas_call(
        kernel,
        out_shape=out_shape,
        in_specs=[VMEM] * len(args) if in_specs is None else in_specs,
        out_specs=[VMEM] * len(out_shape) if multiple else VMEM,
        scratch_shapes=list(scratch),
        compiler_params=PARAMS,
        cost_estimate=cost,
    )(*args)


def struct(shape, dtype=f32):
    return jax.ShapeDtypeStruct(shape, dtype)


def per_device(
    residual,
    iterate,
    probe,
    contour,
    near_tiles,
    near_col,
    near_row,
    near_dest,
    far_right,
    far_col,
    far_rank,
    far_target,
    far_left,
):
    node_dev, _, rhs_dev, rows_dev = residual.shape
    tile_count, _, size, _ = near_tiles.shape
    far_count, _, rank, _ = far_right.shape
    blk_dev = rows_dev // size
    panel_devs = lax.axis_size("panels")
    node_devs = lax.axis_size("nodes")
    nodes_all = node_dev * node_devs
    vec_rows = 2 * node_dev * rhs_dev
    cols = 2 * rhs_dev
    res_rows = 2 * node_dev
    span = res_rows * cols

    part_rows = blk_dev * vec_rows + vec_rows
    copies = 6 + 1 + tile_count // TILE_CHUNK + 4
    field = (rhs_dev, rows_dev)
    indices = (near_col, near_row, near_dest.reshape(tile_count), far_col, far_rank, far_target)
    shifted = panel_devs <= MOST_SHIFTS
    out_shape = [struct((part_rows, LANES))] * panel_devs if shifted else [struct((panel_devs, part_rows, LANES))]
    in_hbm = functools.partial(pltpu.with_memory_space_constraint, memory_space=pltpu.HBM)
    *terms, pack, lines, consts = call(
        functools.partial(terms_kernel, (panel_devs, blk_dev, shifted)),
        [
            *out_shape,
            struct((2 * res_rows, *field)),
            struct((res_rows + 2, *field)),
            struct((8, LANES)),
        ],
        map(in_hbm, (
            *indices,
            contour,
            residual.reshape(res_rows, rhs_dev, rows_dev),
            iterate.reshape(res_rows, rhs_dev, rows_dev),
            probe,
            near_tiles,
            far_right,
        )),
        in_specs=[HBM] * 12,
        scratch=[
            *[pltpu.SMEM(index.shape, jnp.int32) for index in indices],
            pltpu.SMEM(contour.shape, f32),
            pltpu.VMEM(near_tiles.shape, bf16),
            pltpu.VMEM(far_right.shape, bf16),
            pltpu.VMEM((blk_dev, vec_rows, 2 * size), bf16),
            pltpu.VMEM((tile_count, vec_rows, size), f32),
            pltpu.VMEM((far_count * rank // LANES, blk_dev, vec_rows, LANES), f32),
            pltpu.VMEM((panel_devs * blk_dev, vec_rows, size), f32),
            pltpu.VMEM((panel_devs, vec_rows, LANES), f32),
            pltpu.SemaphoreType.DMA((copies,)),
        ],
    )

    if shifted:
        parts = terms[:1]
        for d in range(1, panel_devs):
            pairs = [(i, (i + d) % panel_devs) for i in range(panel_devs)]
            parts.append(lax.ppermute(terms[d], "panels", pairs))
    else:
        parts = [lax.all_to_all(terms[0], "panels", split_axis=0, concat_axis=0, tiled=True)]

    swap = [(0, 1), (1, 0)]
    there = lax.ppermute(lines, "rhs", swap)
    node_pairs = [[(i, (i + s) % node_devs) for i in range(node_devs)] for s in range(node_devs)]
    packs = [pack] + [lax.ppermute(pack, "nodes", pairs) for pairs in node_pairs[1:]]

    product = call(
        functools.partial(product_kernel, (node_devs, nodes_all)),
        struct(residual.shape),
        (*parts, far_left.transpose(0, 1, 3, 2), pack, consts),
    )
    res_hi, res_lo, ahead, *onward = call(
        functools.partial(ahead_kernel, node_devs),
        [struct((span, rows_dev), bf16), struct((span, rows_dev), bf16), struct((3 * rhs_dev, LANES))]
        + [struct((res_rows, *field))] * (node_devs - 1),
        (*packs[1:], pack, lines, there),
    )
    others = [lax.ppermute(value, "rhs", swap) for value in onward]
    message, prod_hi, prod_lo = call(
        gram_kernel,
        [
            struct((3 * rhs_dev, LANES)),
            struct((span, rows_dev), bf16),
            struct((span, rows_dev), bf16),
        ],
        (product, lax.ppermute(product, "rhs", swap), res_hi, res_lo, ahead),
    )

    if shifted and node_devs == 2 and panel_devs > 1 and not panel_devs & (panel_devs - 1):
        near = [(i, i ^ 1) for i in range(panel_devs)]
        far = [(2 * i + x, 2 * (i ^ 1) + 1 - x) for i in range(panel_devs) for x in range(2)]
        across = lax.ppermute(message, ("panels", "nodes"), far)
        aside = lax.ppermute(message, "nodes", node_pairs[1])
        along = lax.ppermute(message, "panels", near)
        both = jnp.concatenate([message + along, aside + across], axis=0)
        step = 2
        while step < panel_devs:
            both = both + lax.ppermute(both, "panels", [(i, i ^ step) for i in range(panel_devs)])
            step *= 2
        sums = [both]
    else:
        total = lax.psum(message, "panels")
        sums = [total] + [lax.ppermute(total, "nodes", pairs) for pairs in node_pairs[1:]]
    scale_factor = 1.0 / math.sqrt(rows_dev * panel_devs)
    residual_next, moments, hankel = call(
        functools.partial(finish_kernel, (len(sums), node_devs, nodes_all, scale_factor)),
        [
            struct(residual.shape),
            struct((MOM_DEV, 2, rhs_dev, rows_dev)),
            struct((MOM_DEV, 2, rhs_dev, cols)),
        ],
        (*sums, *packs, *others, prod_hi, prod_lo, res_hi, res_lo, consts),
    )
    return residual_next, moments, hankel.transpose(0, 1, 3, 2)


def solution(mesh):
    return jax.shard_map(
        per_device,
        mesh=mesh,
        in_specs=(
            P(("groups", "nodes"), None, "rhs", "panels"),
            P(("groups", "nodes"), None, "rhs", "panels"),
            P("groups", "rhs", "panels"),
            P("groups"),
            P(("groups", "panels"), None, None, None),
            P(("groups", "panels")),
            P(("groups", "panels")),
            P(("groups", "panels"), None),
            P(("groups", "panels"), None, None, None),
            P(("groups", "panels")),
            P(("groups", "panels")),
            P(("groups", "panels")),
            P(("groups", "panels"), None, None, None),
        ),
        out_specs=(
            P(("groups", "nodes"), None, "rhs", "panels"),
            P(("groups", "nodes"), None, "rhs", "panels"),
            P(("groups", "nodes"), None, None, "rhs"),
        ),
        check_vma=False,
    )
```

```python
import functools
import math

import jax
import jax.numpy as jnp
import numpy as np
from jax import lax
from jax.experimental import pallas as pl
from jax.experimental.pallas import tpu as pltpu
from jax.sharding import PartitionSpec as P

MOM_DEV = 2
LANES = 128
TILE_CHUNK = 8
MOST_SHIFTS = 8

f32 = jnp.float32
bf16 = jnp.bfloat16

PARAMS = pltpu.CompilerParams(vmem_limit_bytes=40 * 1024 * 1024)
VMEM = pl.BlockSpec(memory_space=pltpu.VMEM)
HBM = pl.BlockSpec(memory_space=pltpu.HBM)


def dot_t(left, right):
    return lax.dot_general(left, right, (((1,), (1,)), ((), ())), preferred_element_type=f32)


def dot_n(left, right):
    return lax.dot_general(left, right, (((1,), (0,)), ((), ())), preferred_element_type=f32)


def split(value):
    high = value.astype(bf16)
    return high, (value - high.astype(f32)).astype(bf16)


def dot3_t(left, right):
    (l_hi, l_lo), (r_hi, r_lo) = left, right
    rows = l_hi.shape[0]
    both = dot_t(jnp.concatenate([l_hi, l_lo], axis=0), r_hi)
    return both[:rows] + both[rows:] + dot_t(l_hi, r_lo)


def dot3_n(left, right):
    (l_hi, l_lo), (r_hi, r_lo) = left, right
    rows = l_hi.shape[0]
    both = dot_n(jnp.concatenate([l_hi, l_lo], axis=0), r_hi)
    return both[:rows] + both[rows:] + dot_n(l_hi, r_lo)


def pick(index, values):
    result = f32(values[0])
    for i in range(1, len(values)):
        result = jnp.where(index == i, f32(values[i]), result)
    return result


def node_angle(node, nodes_all):
    return np.float32(2.0 * math.pi) * (np.float32(node) + np.float32(0.5)) / np.float32(nodes_all)


def terms_kernel(dims, *refs):
    panel_devs, blk_dev, shifted = dims
    n_out = panel_devs if shifted else 1
    indices, (contour_hbm, res_hbm, iter_hbm, probe_hbm, tiles_hbm, fr_hbm) = refs[:6], refs[6:12]
    outs, refs = refs[12 : 12 + n_out], refs[12 + n_out :]
    (pack, lines, consts), refs = refs[:3], refs[3:]
    held, (contour, tiles, fright, vec, terms, skel, acc, facc, sems) = refs[:6], refs[6:]
    tile_count = tiles.shape[0]
    far_count, _, rank, size = fright.shape
    res_rows, iter_rows = res_hbm.shape[0], iter_hbm.shape[0]
    node_dev = res_rows // 2
    chunk = TILE_CHUNK

    copies = []

    def start(source, target):
        copy = pltpu.make_async_copy(source, target, sems.at[len(copies)])
        copy.start()
        copies.append(copy)
        return copy

    res_copy = start(res_hbm, pack.at[pl.ds(0, res_rows)])
    small = [start(source, target) for source, target in zip(indices, held)]
    small.append(start(contour_hbm, contour))
    far_copy = start(fr_hbm, fright)
    tile_copies = []
    for i in range(tile_count // chunk):
        part = pl.ds(i * chunk, chunk)
        tile_copies.append(start(tiles_hbm.at[part], tiles.at[part]))
    rest = [
        start(iter_hbm, pack.at[pl.ds(res_rows, iter_rows)]),
        start(probe_hbm, lines.at[pl.ds(res_rows, 2)]),
    ]
    col, row, dest, fcol, frank, ftgt = held
    here = lax.axis_index("panels")

    def slot_of(owner):
        if shifted:
            owner = owner - here
            owner = jnp.where(owner < 0, owner + panel_devs, owner)
        return owner

    zero = jnp.zeros(acc.shape[1:], f32)
    for b in range(acc.shape[0]):
        acc[b] = zero
    for d in range(facc.shape[0]):
        facc[d] = zero

    res_copy.wait()
    for i in range(res_rows):
        lines[i] = pack[i]
    for b in range(blk_dev):
        lanes = slice(b * size, (b + 1) * size)
        re = jnp.concatenate([pack[2 * k, :, lanes] for k in range(node_dev)], axis=0)
        im = jnp.concatenate([pack[2 * k + 1, :, lanes] for k in range(node_dev)], axis=0)
        upper = jnp.concatenate([re, -im], axis=1)
        lower = jnp.concatenate([im, re], axis=1)
        vec[b] = jnp.concatenate([upper, lower], axis=0).astype(bf16)

    for copy in small:
        copy.wait()
    for i in range(consts.shape[0]):
        consts[i : i + 1, :] = jnp.full((1, LANES), contour[min(i, 2)], f32)

    rows = vec.shape[1]
    far_copy.wait()
    group = LANES // rank
    sources = vec[...].reshape(blk_dev * rows, 2 * size)
    for g in range(far_count // group):
        mats = [
            jnp.concatenate([fright[f, 0], fright[f, 1]], axis=1)
            for f in range(g * group, (g + 1) * group)
        ]
        skel[g] = dot_t(sources, jnp.concatenate(mats, axis=0)).reshape(blk_dev, rows, LANES)
    lane = lax.broadcasted_iota(jnp.int32, (rows, LANES), 1)

    def add_far(f):
        target = ftgt[f]
        owner = target // blk_dev
        place = (target - owner * blk_dev) * rank
        moved = pltpu.roll(
            skel[f // group, fcol[f]], lax.rem(place - (f % group) * rank + LANES, LANES), 1
        )
        kept = (lane >= place) & (lane < place + frank[f])
        slot = slot_of(owner)
        facc[slot] = facc[slot] + jnp.where(kept, moved, 0.0)

    def add_near(t):
        target = slot_of(dest[t]) * blk_dev + row[t]
        acc[target] = acc[target] + terms[t]

    chunks = len(tile_copies)
    for i in range(chunks + 1):
        if i < chunks:
            tile_copies[i].wait()
            for t in range(i * chunk, (i + 1) * chunk):
                tile = jnp.concatenate([tiles[t, 0], tiles[t, 1]], axis=1)
                terms[t] = dot_t(vec[col[t]], tile)
            for f in range(i * far_count // chunks, (i + 1) * far_count // chunks):
                add_far(f)
        if i:
            for t in range((i - 1) * chunk, i * chunk):
                add_near(t)

    near_rows = blk_dev * rows
    for d in range(panel_devs):
        out = outs[d] if shifted else outs[0].at[d]
        for b in range(blk_dev):
            out[b * rows : (b + 1) * rows, :] = acc[d * blk_dev + b]
        out[near_rows:, :] = facc[d]
    for copy in rest:
        copy.wait()


def product_kernel(dims, *refs):
    node_devs, nodes_all = dims
    parts, (left, pack, contour, out) = refs[:-4], refs[-4:]
    parts = [p for part in parts for p in ([part[d] for d in range(part.shape[0])] if len(part.shape) == 3 else [part[...]])]
    node_dev, _, rhs_dev, _ = out.shape
    blk_dev, _, rank, size = left.shape
    rows = 2 * node_dev * rhs_dev
    half = rows // 2

    total = parts[0]
    for part in parts[1:]:
        total = total + part
    near = total[: blk_dev * rows]
    summed = total[blk_dev * rows :]
    re, im = summed[:half], summed[half:]
    upper = jnp.concatenate([re, -im], axis=1)
    lower = jnp.concatenate([im, re], axis=1)
    whole = jnp.concatenate([upper, lower], axis=0)
    lane = lax.broadcasted_iota(jnp.int32, whole.shape, 1)
    block = lax.rem(lane, LANES) // rank
    picked = [jnp.where(block == b, whole, 0.0) for b in range(blk_dev)]
    mats = left[...]
    stacked = jnp.concatenate(
        [mats[:, 0].reshape(blk_dev * rank, size), mats[:, 1].reshape(blk_dev * rank, size)], axis=0
    )
    applied = near + dot_n(jnp.concatenate(picked, axis=0).astype(bf16), stacked)

    here = lax.axis_index("nodes")
    for k in range(node_dev):
        cosines, sines = [], []
        for x in range(node_devs):
            angle = node_angle(x * node_dev + k, nodes_all)
            cosines.append(float(np.cos(angle)))
            sines.append(float(np.sin(angle)))
        shift_re = contour[0:1, :] + contour[2:3, :] * pick(here, cosines)
        shift_im = contour[1:2, :] + contour[2:3, :] * pick(here, sines)
        for b in range(blk_dev):
            lanes = slice(b * size, (b + 1) * size)
            top = b * rows + k * rhs_dev
            r_re, r_im = pack[2 * k, :, lanes], pack[2 * k + 1, :, lanes]
            out[k, 0, :, lanes] = applied[top : top + rhs_dev] - (shift_re * r_re - shift_im * r_im)
            top = top + half
            out[k, 1, :, lanes] = applied[top : top + rhs_dev] - (shift_re * r_im + shift_im * r_re)


def side_by_side(pair, row, count):
    return jnp.concatenate([pair[row : row + count], pair[row + count : row + 2 * count]], axis=1)


def turned(pair, row, count):
    return jnp.concatenate([-pair[row + count : row + 2 * count], pair[row : row + count]], axis=1)


def joined(own, other, row):
    first = lax.axis_index("rhs") == 0
    mine, theirs = own[row], other[row]
    top = jnp.where(first, mine, theirs)
    bottom = jnp.where(first, theirs, mine)
    return jnp.concatenate([top, bottom], axis=0)


def ahead_kernel(node_devs, *refs):
    theirs, refs = refs[: node_devs - 1], refs[node_devs - 1 :]
    pack, own, other, res_hi, res_lo, message, *onward = refs
    _, rhs_dev, _ = own.shape
    cols = 2 * rhs_dev
    res_rows = own.shape[0] - 2
    node_dev = res_rows // 2

    for i in range(res_rows):
        high, low = split(joined(own, other, i))
        res_hi[i * cols : (i + 1) * cols, :] = high
        res_lo[i * cols : (i + 1) * cols, :] = low

    for there, out in zip(theirs, onward):
        for i in range(res_rows):
            out[i] = there[i]

    probe = [joined(own, other, res_rows + c) for c in range(2)]
    probe = split(jnp.concatenate(probe, axis=1))
    pair = []
    for held in (res_hi[...], res_lo[...]):
        rows = []
        for k in range(node_dev):
            rows.append(side_by_side(held, k * 2 * cols, cols))
            rows.append(-turned(held, k * 2 * cols, cols))
        pair.append(jnp.concatenate(rows, axis=0))
    probe_res = dot3_t(probe, tuple(pair))
    rows = []
    for k in range(node_dev):
        i_re, i_im = pack[res_rows + 2 * k], pack[res_rows + 2 * k + 1]
        rows.append(jnp.concatenate([i_re, i_im], axis=1))
        rows.append(jnp.concatenate([i_im, -i_re], axis=1))
    probe_iter = dot3_t(split(jnp.concatenate(rows, axis=0)), probe)

    message[:rhs_dev, :] = jnp.zeros((rhs_dev, LANES), f32)
    pieces = [jnp.zeros((rhs_dev, LANES // 2), f32)]
    pieces.extend(probe_iter[q * rhs_dev : (q + 1) * rhs_dev] for q in range(res_rows))
    message[rhs_dev:cols, :] = jnp.concatenate(pieces, axis=1)
    message[cols:, :] = jnp.concatenate([probe_res[:rhs_dev], probe_res[rhs_dev:]], axis=1)


def node_weight(here, scale, node_devs, node_dev, nodes_all, p, s, k):
    cosines, sines = [], []
    for x in range(node_devs):
        node = (x - s) % node_devs * node_dev + k
        power = x * MOM_DEV + p
        angle = np.float32(power + 1) * node_angle(node, nodes_all)
        cosines.append(float(np.cos(angle)))
        sines.append(float(np.sin(angle)))
    return scale * pick(here, cosines), scale * pick(here, sines)


def gram_kernel(own, other, res_hi, res_lo, ahead, message, prod_hi, prod_lo):
    node_dev, _, rhs_dev, _ = own.shape
    cols = 2 * rhs_dev
    for k in range(node_dev):
        for c in range(2):
            high, low = split(joined(own, other, (k, c)))
            top = (k * 2 + c) * cols
            prod_hi[top : top + cols, :] = high
            prod_lo[top : top + cols, :] = low
    sums = []
    for k in range(node_dev):
        top = k * 2 * cols
        left, right = [], []
        for p_ref, r_ref in ((prod_hi, res_hi), (prod_lo, res_lo)):
            product, source = p_ref[...], r_ref[: node_dev * 2 * cols, :]
            plain = side_by_side(product, top, cols)
            left.append(jnp.concatenate([plain, side_by_side(source, top, cols)], axis=0))
            right.append(jnp.concatenate([plain, turned(product, top, cols)], axis=0))
        sums.append(dot3_t(tuple(left), tuple(right)))
    gram = jnp.concatenate(sums, axis=1)
    half = LANES // 2
    first = lax.axis_index("rhs") == 0
    cross = jnp.where(first, gram[cols : cols + rhs_dev], gram[cols + rhs_dev :])
    message[:rhs_dev, :] = jnp.concatenate([gram[:rhs_dev], gram[rhs_dev:cols]], axis=1)
    message[rhs_dev:cols, :] = jnp.concatenate([cross, ahead[rhs_dev:cols, half:]], axis=1)
    message[cols:, :] = ahead[cols:, :]


def finish_kernel(dims, *refs):
    n_parts, node_devs, nodes_all, scale_factor = dims
    it = iter(refs)
    parts = [[next(it) for _ in range(n_parts)] for _ in range(node_devs)]
    packs = [next(it) for _ in range(node_devs)]
    others = [None] + [next(it) for _ in range(node_devs - 1)]
    prod_hi, prod_lo, res_hi, res_lo, contour, next_out, mom_out, hankel_out = it
    node_dev, _, rhs_dev, width = next_out.shape
    cols = 2 * rhs_dev
    half = LANES // 2
    res_rows = 2 * node_dev
    here = lax.axis_index("nodes")

    sums = [sum((part[...] for part in group[1:]), group[0][...]) for group in parts]
    if node_devs % 2:
        sums.append(sums[0])

    shape = (rhs_dev, LANES)
    lane = lax.broadcasted_iota(jnp.int32, shape, 1)
    low_half = lane < half
    base = (lane // (2 * cols)) * (2 * cols)
    spot = lax.rem(lane, cols)
    real_lane = lax.rem(lane, 2 * cols) < cols
    swapped = jnp.where(real_lane, lane + cols, lane - cols)
    sign = jnp.where(real_lane, -1.0, 1.0)

    def gathered(value, index):
        return jnp.take_along_axis(value, index, axis=1, mode="promise_in_bounds")

    solved, probe_res = [], []
    for g in range(len(sums) // 2):
        s0, s1 = sums[2 * g], sums[2 * g + 1]
        r0, r1 = pltpu.roll(s0, half, 1), pltpu.roll(s1, half, 1)
        v0, v1, v2 = [slice(i * rhs_dev, (i + 1) * rhs_dev) for i in range(3)]
        block = [
            jnp.where(low_half, s0[v0], r1[v0]),
            jnp.where(low_half, r0[v0], s1[v0]),
            jnp.where(low_half, s0[v1], r1[v1]),
        ]
        probe_res.append(
            jnp.concatenate(
                [jnp.where(low_half, s0[v2], r1[v2]), jnp.where(low_half, r0[v2], s1[v2])], axis=0
            )
        )
        for j in range(0, cols, 2):
            at, r = divmod(j, rhs_dev)
            line = block[at]
            crossed = gathered(line, swapped) * sign
            columns = [
                [gathered(value, base + spot_at) for value in block[at:]]
                for spot_at in (j, cols + j, j + 1, cols + j + 1)
            ]
            pivot = (spot == j) | (spot == j + 1)
            g, crossed_g = [], []
            for i in range(2):
                one = spot == j + i
                row = jnp.where(pivot[:1], 0.0, line[r + i : r + i + 1])
                g.append(jnp.where((one & real_lane)[:1], -1.0, row))
                row = jnp.where(pivot[:1], 0.0, crossed[r + i : r + i + 1])
                crossed_g.append(jnp.where((one & ~real_lane)[:1], -1.0, row))
            inverse_p = 1.0 / columns[0][0][r : r + 1]
            b_re, b_im = columns[0][0][r + 1 : r + 2], columns[1][0][r + 1 : r + 2]
            t_re, t_im = b_re * inverse_p, b_im * inverse_p
            inverse_s = 1.0 / (columns[2][0][r + 1 : r + 2] - (t_re * b_re + t_im * b_im))
            h = (g[1] - (g[0] * t_re + crossed_g[0] * t_im)) * inverse_s
            crossed_h = (crossed_g[1] - (crossed_g[0] * t_re - g[0] * t_im)) * inverse_s
            f = g[0] * inverse_p - (h * t_re - crossed_h * t_im)
            crossed_f = crossed_g[0] * inverse_p - (crossed_h * t_re + h * t_im)
            for i in range(at, 3):
                c0_re, c0_im, c1_re, c1_im = [value[i - at] for value in columns]
                change = (c0_re * f + c0_im * crossed_f) + (c1_re * h + c1_im * crossed_h)
                block[i] = jnp.where(pivot, 0.0, block[i]) - change
        solved.append(block[2])

    coef = solved[0]
    cross = gathered(coef, swapped)
    plain = jnp.where(real_lane, coef, -coef)
    node_of = lane // (2 * cols)
    rows = []
    for k in range(node_dev):
        rows.append(jnp.where(node_of == k, plain, 0.0))
        rows.append(jnp.where(node_of == k, cross, 0.0))
    used = node_dev * 2 * cols
    left = split(jnp.concatenate(rows, axis=0)[:, :used])
    change = dot3_n(left, (prod_hi[...], prod_lo[...]))
    for k in range(node_dev):
        for c in range(2):
            top = (k * 2 + c) * rhs_dev
            next_out[k, c] = packs[0][2 * k + c] - change[top : top + rhs_dev]

    scale = contour[2:3, :] / nodes_all
    weighted = []
    for g, coef in enumerate(solved):
        cross = gathered(coef, swapped)
        rows = []
        for p in range(MOM_DEV):
            w_re = jnp.zeros(shape, f32)
            w_im = jnp.zeros(shape, f32)
            for i in range(2):
                s = 2 * g + i
                if s >= node_devs:
                    continue
                for k in range(node_dev):
                    n_re, n_im = node_weight(here, scale, node_devs, node_dev, nodes_all, p, s, k)
                    mine = node_of == i * node_dev + k
                    w_re = jnp.where(mine, n_re, w_re)
                    w_im = jnp.where(mine, n_im, w_im)
            rows.append(-sign * w_re * coef - w_im * cross)
            rows.append(-sign * w_im * coef + w_re * cross)
        weighted.append(jnp.concatenate(rows, axis=0))
    hankel = None
    products = None
    for g, value in enumerate(weighted):
        depth = min(LANES, node_devs * used - g * LANES)
        left = split(value)
        cut = tuple(part[:, :depth] for part in left)
        highs, lows = [], []
        for i in range(depth // used):
            s = 2 * g + i
            if s == 0:
                highs.append(res_hi[...])
                lows.append(res_lo[...])
                continue
            for q in range(res_rows):
                high, low = split(joined(packs[s], others[s], q))
                highs.append(high)
                lows.append(low)
        term = dot3_n(cut, (jnp.concatenate(highs, axis=0), jnp.concatenate(lows, axis=0)))
        products = term if products is None else products + term
        term = dot3_t(left, split(probe_res[g]))
        hankel = term if hankel is None else hankel + term

    wide = jnp.concatenate([scale] * (width // LANES), axis=1)
    for p in range(MOM_DEV):
        mom = [products[(2 * p + c) * rhs_dev : (2 * p + c + 1) * rhs_dev] for c in range(2)]
        han = [hankel[(2 * p + c) * rhs_dev : (2 * p + c + 1) * rhs_dev] for c in range(2)]
        for s in range(node_devs):
            for k in range(node_dev):
                w_re, w_im = node_weight(here, wide, node_devs, node_dev, nodes_all, p, s, k)
                i_re, i_im = packs[s][res_rows + 2 * k], packs[s][res_rows + 2 * k + 1]
                mom[0] = mom[0] + (w_re * i_re - w_im * i_im)
                mom[1] = mom[1] + (w_re * i_im + w_im * i_re)
                i_re, i_im = [
                    pltpu.roll(sums[s][rhs_dev:cols], half - (2 * k + c) * cols, 1)[:, :cols]
                    for c in range(2)
                ]
                w_re, w_im = w_re[:, :cols], w_im[:, :cols]
                han[0] = han[0] + (w_re * i_re - w_im * i_im)
                han[1] = han[1] + (w_re * i_im + w_im * i_re)
        for c in range(2):
            mom_out[p, c] = mom[c]
            hankel_out[p, c] = han[c] * scale_factor


def call(kernel, out_shape, args, in_specs=None, scratch=(), cost=None):
    args = tuple(args)
    multiple = isinstance(out_shape, (list, tuple))
    return pl.pallas_call(
        kernel,
        out_shape=out_shape,
        in_specs=[VMEM] * len(args) if in_specs is None else in_specs,
        out_specs=[VMEM] * len(out_shape) if multiple else VMEM,
        scratch_shapes=list(scratch),
        compiler_params=PARAMS,
        cost_estimate=cost,
    )(*args)


def struct(shape, dtype=f32):
    return jax.ShapeDtypeStruct(shape, dtype)


def per_device(
    residual,
    iterate,
    probe,
    contour,
    near_tiles,
    near_col,
    near_row,
    near_dest,
    far_right,
    far_col,
    far_rank,
    far_target,
    far_left,
):
    node_dev, _, rhs_dev, rows_dev = residual.shape
    tile_count, _, size, _ = near_tiles.shape
    far_count, _, rank, _ = far_right.shape
    blk_dev = rows_dev // size
    panel_devs = lax.axis_size("panels")
    node_devs = lax.axis_size("nodes")
    nodes_all = node_dev * node_devs
    vec_rows = 2 * node_dev * rhs_dev
    cols = 2 * rhs_dev
    res_rows = 2 * node_dev
    span = res_rows * cols

    part_rows = blk_dev * vec_rows + vec_rows
    copies = 6 + 1 + tile_count // TILE_CHUNK + 4
    field = (rhs_dev, rows_dev)
    indices = (near_col, near_row, near_dest.reshape(tile_count), far_col, far_rank, far_target)
    shifted = panel_devs <= MOST_SHIFTS
    out_shape = [struct((part_rows, LANES))] * panel_devs if shifted else [struct((panel_devs, part_rows, LANES))]
    in_hbm = functools.partial(pltpu.with_memory_space_constraint, memory_space=pltpu.HBM)
    *terms, pack, lines, consts = call(
        functools.partial(terms_kernel, (panel_devs, blk_dev, shifted)),
        [
            *out_shape,
            struct((2 * res_rows, *field)),
            struct((res_rows + 2, *field)),
            struct((8, LANES)),
        ],
        map(in_hbm, (
            *indices,
            contour,
            residual.reshape(res_rows, rhs_dev, rows_dev),
            iterate.reshape(res_rows, rhs_dev, rows_dev),
            probe,
            near_tiles,
            far_right,
        )),
        in_specs=[HBM] * 12,
        scratch=[
            *[pltpu.SMEM(index.shape, jnp.int32) for index in indices],
            pltpu.SMEM(contour.shape, f32),
            pltpu.VMEM(near_tiles.shape, bf16),
            pltpu.VMEM(far_right.shape, bf16),
            pltpu.VMEM((blk_dev, vec_rows, 2 * size), bf16),
            pltpu.VMEM((tile_count, vec_rows, size), f32),
            pltpu.VMEM((far_count * rank // LANES, blk_dev, vec_rows, LANES), f32),
            pltpu.VMEM((panel_devs * blk_dev, vec_rows, size), f32),
            pltpu.VMEM((panel_devs, vec_rows, LANES), f32),
            pltpu.SemaphoreType.DMA((copies,)),
        ],
    )

    if shifted:
        parts = terms[:1]
        for d in range(1, panel_devs):
            pairs = [(i, (i + d) % panel_devs) for i in range(panel_devs)]
            parts.append(lax.ppermute(terms[d], "panels", pairs))
    else:
        parts = [lax.all_to_all(terms[0], "panels", split_axis=0, concat_axis=0, tiled=True)]

    swap = [(0, 1), (1, 0)]
    there = lax.ppermute(lines, "rhs", swap)
    node_pairs = [[(i, (i + s) % node_devs) for i in range(node_devs)] for s in range(node_devs)]
    packs = [pack] + [lax.ppermute(pack, "nodes", pairs) for pairs in node_pairs[1:]]

    product = call(
        functools.partial(product_kernel, (node_devs, nodes_all)),
        struct(residual.shape),
        (*parts, far_left.transpose(0, 1, 3, 2), pack, consts),
    )
    res_hi, res_lo, ahead, *onward = call(
        functools.partial(ahead_kernel, node_devs),
        [struct((span, rows_dev), bf16), struct((span, rows_dev), bf16), struct((3 * rhs_dev, LANES))]
        + [struct((res_rows, *field))] * (node_devs - 1),
        (*packs[1:], pack, lines, there),
    )
    others = [lax.ppermute(value, "rhs", swap) for value in onward]
    message, prod_hi, prod_lo = call(
        gram_kernel,
        [
            struct((3 * rhs_dev, LANES)),
            struct((span, rows_dev), bf16),
            struct((span, rows_dev), bf16),
        ],
        (product, lax.ppermute(product, "rhs", swap), res_hi, res_lo, ahead),
    )

    if shifted:
        total = message
        for d in range(panel_devs - 1, 0, -1):
            pairs = [(i, (i + d) % panel_devs) for i in range(panel_devs)]
            total = total + lax.ppermute(message, "panels", pairs)
    else:
        total = lax.psum(message, "panels")
    sums = [total] + [lax.ppermute(total, "nodes", pairs) for pairs in node_pairs[1:]]
    scale_factor = 1.0 / math.sqrt(rows_dev * panel_devs)
    residual_next, moments, hankel = call(
        functools.partial(finish_kernel, (1, node_devs, nodes_all, scale_factor)),
        [
            struct(residual.shape),
            struct((MOM_DEV, 2, rhs_dev, rows_dev)),
            struct((MOM_DEV, 2, rhs_dev, cols)),
        ],
        (*sums, *packs, *others, prod_hi, prod_lo, res_hi, res_lo, consts),
    )
    return residual_next, moments, hankel.transpose(0, 1, 3, 2)


def solution(mesh):
    return jax.shard_map(
        per_device,
        mesh=mesh,
        in_specs=(
            P(("groups", "nodes"), None, "rhs", "panels"),
            P(("groups", "nodes"), None, "rhs", "panels"),
            P("groups", "rhs", "panels"),
            P("groups"),
            P(("groups", "panels"), None, None, None),
            P(("groups", "panels")),
            P(("groups", "panels")),
            P(("groups", "panels"), None),
            P(("groups", "panels"), None, None, None),
            P(("groups", "panels")),
            P(("groups", "panels")),
            P(("groups", "panels")),
            P(("groups", "panels"), None, None, None),
        ),
        out_specs=(
            P(("groups", "nodes"), None, "rhs", "panels"),
            P(("groups", "nodes"), None, "rhs", "panels"),
            P(("groups", "nodes"), None, None, "rhs"),
        ),
        check_vma=False,
    )
```

```python
import functools
import math

import jax
import jax.numpy as jnp
import numpy as np
from jax import lax
from jax.experimental import pallas as pl
from jax.experimental.pallas import tpu as pltpu
from jax.sharding import PartitionSpec as P

MOM_DEV = 2
LANES = 128
TILE_CHUNK = 16
MOST_SHIFTS = 8

f32 = jnp.float32
bf16 = jnp.bfloat16

PARAMS = pltpu.CompilerParams(vmem_limit_bytes=40 * 1024 * 1024)
VMEM = pl.BlockSpec(memory_space=pltpu.VMEM)
HBM = pl.BlockSpec(memory_space=pltpu.HBM)


def dot_t(left, right):
    return lax.dot_general(left, right, (((1,), (1,)), ((), ())), preferred_element_type=f32)


def dot_n(left, right):
    return lax.dot_general(left, right, (((1,), (0,)), ((), ())), preferred_element_type=f32)


def split(value):
    high = value.astype(bf16)
    return high, (value - high.astype(f32)).astype(bf16)


def dot3_t(left, right):
    (l_hi, l_lo), (r_hi, r_lo) = left, right
    rows = l_hi.shape[0]
    both = dot_t(jnp.concatenate([l_hi, l_lo], axis=0), r_hi)
    return both[:rows] + both[rows:] + dot_t(l_hi, r_lo)


def dot3_n(left, right):
    (l_hi, l_lo), (r_hi, r_lo) = left, right
    rows = l_hi.shape[0]
    both = dot_n(jnp.concatenate([l_hi, l_lo], axis=0), r_hi)
    return both[:rows] + both[rows:] + dot_n(l_hi, r_lo)


def pick(index, values):
    result = f32(values[0])
    for i in range(1, len(values)):
        result = jnp.where(index == i, f32(values[i]), result)
    return result


def node_angle(node, nodes_all):
    return np.float32(2.0 * math.pi) * (np.float32(node) + np.float32(0.5)) / np.float32(nodes_all)


def terms_kernel(dims, *refs):
    panel_devs, blk_dev, shifted = dims
    n_out = panel_devs if shifted else 1
    indices, (contour_hbm, res_hbm, iter_hbm, probe_hbm, tiles_hbm, fr_hbm) = refs[:6], refs[6:12]
    outs, refs = refs[12 : 12 + n_out], refs[12 + n_out :]
    (pack, lines, consts), refs = refs[:3], refs[3:]
    held, (contour, tiles, fright, vec, terms, skel, acc, facc, sems) = refs[:6], refs[6:]
    tile_count = tiles.shape[0]
    far_count, _, rank, size = fright.shape
    res_rows, iter_rows = res_hbm.shape[0], iter_hbm.shape[0]
    node_dev = res_rows // 2
    chunk = TILE_CHUNK

    copies = []

    def start(source, target):
        copy = pltpu.make_async_copy(source, target, sems.at[len(copies)])
        copy.start()
        copies.append(copy)
        return copy

    res_copy = start(res_hbm, pack.at[pl.ds(0, res_rows)])
    small = [start(source, target) for source, target in zip(indices, held)]
    small.append(start(contour_hbm, contour))
    far_copy = start(fr_hbm, fright)
    tile_copies = []
    for i in range(tile_count // chunk):
        part = pl.ds(i * chunk, chunk)
        tile_copies.append(start(tiles_hbm.at[part], tiles.at[part]))
    rest = [
        start(iter_hbm, pack.at[pl.ds(res_rows, iter_rows)]),
        start(probe_hbm, lines.at[pl.ds(res_rows, 2)]),
    ]
    col, row, dest, fcol, frank, ftgt = held
    here = lax.axis_index("panels")

    def slot_of(owner):
        if shifted:
            owner = owner - here
            owner = jnp.where(owner < 0, owner + panel_devs, owner)
        return owner

    zero = jnp.zeros(acc.shape[1:], f32)
    for b in range(acc.shape[0]):
        acc[b] = zero
    for d in range(facc.shape[0]):
        facc[d] = zero

    res_copy.wait()
    for i in range(res_rows):
        lines[i] = pack[i]
    for b in range(blk_dev):
        lanes = slice(b * size, (b + 1) * size)
        re = jnp.concatenate([pack[2 * k, :, lanes] for k in range(node_dev)], axis=0)
        im = jnp.concatenate([pack[2 * k + 1, :, lanes] for k in range(node_dev)], axis=0)
        upper = jnp.concatenate([re, -im], axis=1)
        lower = jnp.concatenate([im, re], axis=1)
        vec[b] = jnp.concatenate([upper, lower], axis=0).astype(bf16)

    for copy in small:
        copy.wait()
    for i in range(consts.shape[0]):
        consts[i : i + 1, :] = jnp.full((1, LANES), contour[min(i, 2)], f32)

    rows = vec.shape[1]
    far_copy.wait()
    group = LANES // rank
    sources = vec[...].reshape(blk_dev * rows, 2 * size)
    for g in range(far_count // group):
        mats = [
            jnp.concatenate([fright[f, 0], fright[f, 1]], axis=1)
            for f in range(g * group, (g + 1) * group)
        ]
        skel[g] = dot_t(sources, jnp.concatenate(mats, axis=0)).reshape(blk_dev, rows, LANES)
    lane = lax.broadcasted_iota(jnp.int32, (rows, LANES), 1)

    def add_far(f):
        target = ftgt[f]
        owner = target // blk_dev
        place = (target - owner * blk_dev) * rank
        moved = pltpu.roll(
            skel[f // group, fcol[f]], lax.rem(place - (f % group) * rank + LANES, LANES), 1
        )
        kept = (lane >= place) & (lane < place + frank[f])
        slot = slot_of(owner)
        facc[slot] = facc[slot] + jnp.where(kept, moved, 0.0)

    def add_near(t):
        target = slot_of(dest[t]) * blk_dev + row[t]
        acc[target] = acc[target] + terms[t]

    chunks = len(tile_copies)
    for i in range(chunks + 1):
        if i < chunks:
            tile_copies[i].wait()
            for t in range(i * chunk, (i + 1) * chunk):
                tile = jnp.concatenate([tiles[t, 0], tiles[t, 1]], axis=1)
                terms[t] = dot_t(vec[col[t]], tile)
            for f in range(i * far_count // chunks, (i + 1) * far_count // chunks):
                add_far(f)
        if i:
            for t in range((i - 1) * chunk, i * chunk):
                add_near(t)

    near_rows = blk_dev * rows
    for d in range(panel_devs):
        out = outs[d] if shifted else outs[0].at[d]
        for b in range(blk_dev):
            out[b * rows : (b + 1) * rows, :] = acc[d * blk_dev + b]
        out[near_rows:, :] = facc[d]
    for copy in rest:
        copy.wait()


def product_kernel(dims, *refs):
    node_devs, nodes_all = dims
    parts, (left, pack, contour, out) = refs[:-4], refs[-4:]
    parts = [p for part in parts for p in ([part[d] for d in range(part.shape[0])] if len(part.shape) == 3 else [part[...]])]
    node_dev, _, rhs_dev, _ = out.shape
    blk_dev, _, rank, size = left.shape
    rows = 2 * node_dev * rhs_dev
    half = rows // 2

    total = parts[0]
    for part in parts[1:]:
        total = total + part
    near = total[: blk_dev * rows]
    summed = total[blk_dev * rows :]
    re, im = summed[:half], summed[half:]
    upper = jnp.concatenate([re, -im], axis=1)
    lower = jnp.concatenate([im, re], axis=1)
    whole = jnp.concatenate([upper, lower], axis=0)
    lane = lax.broadcasted_iota(jnp.int32, whole.shape, 1)
    block = lax.rem(lane, LANES) // rank
    picked = [jnp.where(block == b, whole, 0.0) for b in range(blk_dev)]
    mats = left[...]
    stacked = jnp.concatenate(
        [mats[:, 0].reshape(blk_dev * rank, size), mats[:, 1].reshape(blk_dev * rank, size)], axis=0
    )
    applied = near + dot_n(jnp.concatenate(picked, axis=0).astype(bf16), stacked)

    here = lax.axis_index("nodes")
    for k in range(node_dev):
        cosines, sines = [], []
        for x in range(node_devs):
            angle = node_angle(x * node_dev + k, nodes_all)
            cosines.append(float(np.cos(angle)))
            sines.append(float(np.sin(angle)))
        shift_re = contour[0:1, :] + contour[2:3, :] * pick(here, cosines)
        shift_im = contour[1:2, :] + contour[2:3, :] * pick(here, sines)
        for b in range(blk_dev):
            lanes = slice(b * size, (b + 1) * size)
            top = b * rows + k * rhs_dev
            r_re, r_im = pack[2 * k, :, lanes], pack[2 * k + 1, :, lanes]
            out[k, 0, :, lanes] = applied[top : top + rhs_dev] - (shift_re * r_re - shift_im * r_im)
            top = top + half
            out[k, 1, :, lanes] = applied[top : top + rhs_dev] - (shift_re * r_im + shift_im * r_re)


def side_by_side(pair, row, count):
    return jnp.concatenate([pair[row : row + count], pair[row + count : row + 2 * count]], axis=1)


def turned(pair, row, count):
    return jnp.concatenate([-pair[row + count : row + 2 * count], pair[row : row + count]], axis=1)


def joined(own, other, row):
    first = lax.axis_index("rhs") == 0
    mine, theirs = own[row], other[row]
    top = jnp.where(first, mine, theirs)
    bottom = jnp.where(first, theirs, mine)
    return jnp.concatenate([top, bottom], axis=0)


def ahead_kernel(node_devs, *refs):
    theirs, refs = refs[: node_devs - 1], refs[node_devs - 1 :]
    pack, own, other, res_hi, res_lo, message, *onward = refs
    _, rhs_dev, _ = own.shape
    cols = 2 * rhs_dev
    res_rows = own.shape[0] - 2
    node_dev = res_rows // 2

    for i in range(res_rows):
        high, low = split(joined(own, other, i))
        res_hi[i * cols : (i + 1) * cols, :] = high
        res_lo[i * cols : (i + 1) * cols, :] = low

    for there, out in zip(theirs, onward):
        for i in range(res_rows):
            out[i] = there[i]

    probe = [joined(own, other, res_rows + c) for c in range(2)]
    probe = split(jnp.concatenate(probe, axis=1))
    pair = []
    for held in (res_hi[...], res_lo[...]):
        rows = []
        for k in range(node_dev):
            rows.append(side_by_side(held, k * 2 * cols, cols))
            rows.append(-turned(held, k * 2 * cols, cols))
        pair.append(jnp.concatenate(rows, axis=0))
    probe_res = dot3_t(probe, tuple(pair))
    rows = []
    for k in range(node_dev):
        i_re, i_im = pack[res_rows + 2 * k], pack[res_rows + 2 * k + 1]
        rows.append(jnp.concatenate([i_re, i_im], axis=1))
        rows.append(jnp.concatenate([i_im, -i_re], axis=1))
    probe_iter = dot3_t(split(jnp.concatenate(rows, axis=0)), probe)

    message[:rhs_dev, :] = jnp.zeros((rhs_dev, LANES), f32)
    pieces = [jnp.zeros((rhs_dev, LANES // 2), f32)]
    pieces.extend(probe_iter[q * rhs_dev : (q + 1) * rhs_dev] for q in range(res_rows))
    message[rhs_dev:cols, :] = jnp.concatenate(pieces, axis=1)
    message[cols:, :] = jnp.concatenate([probe_res[:rhs_dev], probe_res[rhs_dev:]], axis=1)


def node_weight(here, scale, node_devs, node_dev, nodes_all, p, s, k):
    cosines, sines = [], []
    for x in range(node_devs):
        node = (x - s) % node_devs * node_dev + k
        power = x * MOM_DEV + p
        angle = np.float32(power + 1) * node_angle(node, nodes_all)
        cosines.append(float(np.cos(angle)))
        sines.append(float(np.sin(angle)))
    return scale * pick(here, cosines), scale * pick(here, sines)


def gram_kernel(own, other, res_hi, res_lo, ahead, message, prod_hi, prod_lo):
    node_dev, _, rhs_dev, _ = own.shape
    cols = 2 * rhs_dev
    for k in range(node_dev):
        for c in range(2):
            high, low = split(joined(own, other, (k, c)))
            top = (k * 2 + c) * cols
            prod_hi[top : top + cols, :] = high
            prod_lo[top : top + cols, :] = low
    sums = []
    for k in range(node_dev):
        top = k * 2 * cols
        left, right = [], []
        for p_ref, r_ref in ((prod_hi, res_hi), (prod_lo, res_lo)):
            product, source = p_ref[...], r_ref[: node_dev * 2 * cols, :]
            plain = side_by_side(product, top, cols)
            left.append(jnp.concatenate([plain, side_by_side(source, top, cols)], axis=0))
            right.append(jnp.concatenate([plain, turned(product, top, cols)], axis=0))
        sums.append(dot3_t(tuple(left), tuple(right)))
    gram = jnp.concatenate(sums, axis=1)
    half = LANES // 2
    first = lax.axis_index("rhs") == 0
    cross = jnp.where(first, gram[cols : cols + rhs_dev], gram[cols + rhs_dev :])
    message[:rhs_dev, :] = jnp.concatenate([gram[:rhs_dev], gram[rhs_dev:cols]], axis=1)
    message[rhs_dev:cols, :] = jnp.concatenate([cross, ahead[rhs_dev:cols, half:]], axis=1)
    message[cols:, :] = ahead[cols:, :]


def finish_kernel(dims, *refs):
    n_parts, node_devs, nodes_all, scale_factor = dims
    it = iter(refs)
    parts = [[next(it) for _ in range(n_parts)] for _ in range(node_devs)]
    packs = [next(it) for _ in range(node_devs)]
    others = [None] + [next(it) for _ in range(node_devs - 1)]
    prod_hi, prod_lo, res_hi, res_lo, contour, next_out, mom_out, hankel_out = it
    node_dev, _, rhs_dev, width = next_out.shape
    cols = 2 * rhs_dev
    half = LANES // 2
    res_rows = 2 * node_dev
    here = lax.axis_index("nodes")

    sums = [sum((part[...] for part in group[1:]), group[0][...]) for group in parts]
    if node_devs % 2:
        sums.append(sums[0])

    shape = (rhs_dev, LANES)
    lane = lax.broadcasted_iota(jnp.int32, shape, 1)
    low_half = lane < half
    base = (lane // (2 * cols)) * (2 * cols)
    spot = lax.rem(lane, cols)
    real_lane = lax.rem(lane, 2 * cols) < cols
    swapped = jnp.where(real_lane, lane + cols, lane - cols)
    sign = jnp.where(real_lane, -1.0, 1.0)

    def gathered(value, index):
        return jnp.take_along_axis(value, index, axis=1, mode="promise_in_bounds")

    solved, probe_res = [], []
    for g in range(len(sums) // 2):
        s0, s1 = sums[2 * g], sums[2 * g + 1]
        r0, r1 = pltpu.roll(s0, half, 1), pltpu.roll(s1, half, 1)
        v0, v1, v2 = [slice(i * rhs_dev, (i + 1) * rhs_dev) for i in range(3)]
        block = [
            jnp.where(low_half, s0[v0], r1[v0]),
            jnp.where(low_half, r0[v0], s1[v0]),
            jnp.where(low_half, s0[v1], r1[v1]),
        ]
        probe_res.append(
            jnp.concatenate(
                [jnp.where(low_half, s0[v2], r1[v2]), jnp.where(low_half, r0[v2], s1[v2])], axis=0
            )
        )
        for j in range(0, cols, 2):
            at, r = divmod(j, rhs_dev)
            line = block[at]
            crossed = gathered(line, swapped) * sign
            columns = [
                [gathered(value, base + spot_at) for value in block[at:]]
                for spot_at in (j, cols + j, j + 1, cols + j + 1)
            ]
            pivot = (spot == j) | (spot == j + 1)
            g, crossed_g = [], []
            for i in range(2):
                one = spot == j + i
                row = jnp.where(pivot[:1], 0.0, line[r + i : r + i + 1])
                g.append(jnp.where((one & real_lane)[:1], -1.0, row))
                row = jnp.where(pivot[:1], 0.0, crossed[r + i : r + i + 1])
                crossed_g.append(jnp.where((one & ~real_lane)[:1], -1.0, row))
            inverse_p = 1.0 / columns[0][0][r : r + 1]
            b_re, b_im = columns[0][0][r + 1 : r + 2], columns[1][0][r + 1 : r + 2]
            t_re, t_im = b_re * inverse_p, b_im * inverse_p
            inverse_s = 1.0 / (columns[2][0][r + 1 : r + 2] - (t_re * b_re + t_im * b_im))
            h = (g[1] - (g[0] * t_re + crossed_g[0] * t_im)) * inverse_s
            crossed_h = (crossed_g[1] - (crossed_g[0] * t_re - g[0] * t_im)) * inverse_s
            f = g[0] * inverse_p - (h * t_re - crossed_h * t_im)
            crossed_f = crossed_g[0] * inverse_p - (crossed_h * t_re + h * t_im)
            for i in range(at, 3):
                c0_re, c0_im, c1_re, c1_im = [value[i - at] for value in columns]
                change = (c0_re * f + c0_im * crossed_f) + (c1_re * h + c1_im * crossed_h)
                block[i] = jnp.where(pivot, 0.0, block[i]) - change
        solved.append(block[2])

    coef = solved[0]
    cross = gathered(coef, swapped)
    plain = jnp.where(real_lane, coef, -coef)
    node_of = lane // (2 * cols)
    rows = []
    for k in range(node_dev):
        rows.append(jnp.where(node_of == k, plain, 0.0))
        rows.append(jnp.where(node_of == k, cross, 0.0))
    used = node_dev * 2 * cols
    left = split(jnp.concatenate(rows, axis=0)[:, :used])
    change = dot3_n(left, (prod_hi[...], prod_lo[...]))
    for k in range(node_dev):
        for c in range(2):
            top = (k * 2 + c) * rhs_dev
            next_out[k, c] = packs[0][2 * k + c] - change[top : top + rhs_dev]

    scale = contour[2:3, :] / nodes_all
    weighted = []
    for g, coef in enumerate(solved):
        cross = gathered(coef, swapped)
        rows = []
        for p in range(MOM_DEV):
            w_re = jnp.zeros(shape, f32)
            w_im = jnp.zeros(shape, f32)
            for i in range(2):
                s = 2 * g + i
                if s >= node_devs:
                    continue
                for k in range(node_dev):
                    n_re, n_im = node_weight(here, scale, node_devs, node_dev, nodes_all, p, s, k)
                    mine = node_of == i * node_dev + k
                    w_re = jnp.where(mine, n_re, w_re)
                    w_im = jnp.where(mine, n_im, w_im)
            rows.append(-sign * w_re * coef - w_im * cross)
            rows.append(-sign * w_im * coef + w_re * cross)
        weighted.append(jnp.concatenate(rows, axis=0))
    hankel = None
    products = None
    for g, value in enumerate(weighted):
        depth = min(LANES, node_devs * used - g * LANES)
        left = split(value)
        cut = tuple(part[:, :depth] for part in left)
        highs, lows = [], []
        for i in range(depth // used):
            s = 2 * g + i
            if s == 0:
                highs.append(res_hi[...])
                lows.append(res_lo[...])
                continue
            for q in range(res_rows):
                high, low = split(joined(packs[s], others[s], q))
                highs.append(high)
                lows.append(low)
        term = dot3_n(cut, (jnp.concatenate(highs, axis=0), jnp.concatenate(lows, axis=0)))
        products = term if products is None else products + term
        term = dot3_t(left, split(probe_res[g]))
        hankel = term if hankel is None else hankel + term

    wide = jnp.concatenate([scale] * (width // LANES), axis=1)
    for p in range(MOM_DEV):
        mom = [products[(2 * p + c) * rhs_dev : (2 * p + c + 1) * rhs_dev] for c in range(2)]
        han = [hankel[(2 * p + c) * rhs_dev : (2 * p + c + 1) * rhs_dev] for c in range(2)]
        for s in range(node_devs):
            for k in range(node_dev):
                w_re, w_im = node_weight(here, wide, node_devs, node_dev, nodes_all, p, s, k)
                i_re, i_im = packs[s][res_rows + 2 * k], packs[s][res_rows + 2 * k + 1]
                mom[0] = mom[0] + (w_re * i_re - w_im * i_im)
                mom[1] = mom[1] + (w_re * i_im + w_im * i_re)
                i_re, i_im = [
                    pltpu.roll(sums[s][rhs_dev:cols], half - (2 * k + c) * cols, 1)[:, :cols]
                    for c in range(2)
                ]
                w_re, w_im = w_re[:, :cols], w_im[:, :cols]
                han[0] = han[0] + (w_re * i_re - w_im * i_im)
                han[1] = han[1] + (w_re * i_im + w_im * i_re)
        for c in range(2):
            mom_out[p, c] = mom[c]
            hankel_out[p, c] = han[c] * scale_factor


def call(kernel, out_shape, args, in_specs=None, scratch=(), cost=None):
    args = tuple(args)
    multiple = isinstance(out_shape, (list, tuple))
    return pl.pallas_call(
        kernel,
        out_shape=out_shape,
        in_specs=[VMEM] * len(args) if in_specs is None else in_specs,
        out_specs=[VMEM] * len(out_shape) if multiple else VMEM,
        scratch_shapes=list(scratch),
        compiler_params=PARAMS,
        cost_estimate=cost,
    )(*args)


def struct(shape, dtype=f32):
    return jax.ShapeDtypeStruct(shape, dtype)


def per_device(
    residual,
    iterate,
    probe,
    contour,
    near_tiles,
    near_col,
    near_row,
    near_dest,
    far_right,
    far_col,
    far_rank,
    far_target,
    far_left,
):
    node_dev, _, rhs_dev, rows_dev = residual.shape
    tile_count, _, size, _ = near_tiles.shape
    far_count, _, rank, _ = far_right.shape
    blk_dev = rows_dev // size
    panel_devs = lax.axis_size("panels")
    node_devs = lax.axis_size("nodes")
    nodes_all = node_dev * node_devs
    vec_rows = 2 * node_dev * rhs_dev
    cols = 2 * rhs_dev
    res_rows = 2 * node_dev
    span = res_rows * cols

    part_rows = blk_dev * vec_rows + vec_rows
    copies = 6 + 1 + tile_count // TILE_CHUNK + 4
    field = (rhs_dev, rows_dev)
    indices = (near_col, near_row, near_dest.reshape(tile_count), far_col, far_rank, far_target)
    shifted = panel_devs <= MOST_SHIFTS
    out_shape = [struct((part_rows, LANES))] * panel_devs if shifted else [struct((panel_devs, part_rows, LANES))]
    in_hbm = functools.partial(pltpu.with_memory_space_constraint, memory_space=pltpu.HBM)
    *terms, pack, lines, consts = call(
        functools.partial(terms_kernel, (panel_devs, blk_dev, shifted)),
        [
            *out_shape,
            struct((2 * res_rows, *field)),
            struct((res_rows + 2, *field)),
            struct((8, LANES)),
        ],
        map(in_hbm, (
            *indices,
            contour,
            residual.reshape(res_rows, rhs_dev, rows_dev),
            iterate.reshape(res_rows, rhs_dev, rows_dev),
            probe,
            near_tiles,
            far_right,
        )),
        in_specs=[HBM] * 12,
        scratch=[
            *[pltpu.SMEM(index.shape, jnp.int32) for index in indices],
            pltpu.SMEM(contour.shape, f32),
            pltpu.VMEM(near_tiles.shape, bf16),
            pltpu.VMEM(far_right.shape, bf16),
            pltpu.VMEM((blk_dev, vec_rows, 2 * size), bf16),
            pltpu.VMEM((tile_count, vec_rows, size), f32),
            pltpu.VMEM((far_count * rank // LANES, blk_dev, vec_rows, LANES), f32),
            pltpu.VMEM((panel_devs * blk_dev, vec_rows, size), f32),
            pltpu.VMEM((panel_devs, vec_rows, LANES), f32),
            pltpu.SemaphoreType.DMA((copies,)),
        ],
    )

    if shifted:
        parts = terms[:1]
        for d in range(1, panel_devs):
            pairs = [(i, (i + d) % panel_devs) for i in range(panel_devs)]
            parts.append(lax.ppermute(terms[d], "panels", pairs))
    else:
        parts = [lax.all_to_all(terms[0], "panels", split_axis=0, concat_axis=0, tiled=True)]

    swap = [(0, 1), (1, 0)]
    there = lax.ppermute(lines, "rhs", swap)
    node_pairs = [[(i, (i + s) % node_devs) for i in range(node_devs)] for s in range(node_devs)]
    packs = [pack] + [lax.ppermute(pack, "nodes", pairs) for pairs in node_pairs[1:]]

    product = call(
        functools.partial(product_kernel, (node_devs, nodes_all)),
        struct(residual.shape),
        (*parts, far_left.transpose(0, 1, 3, 2), pack, consts),
    )
    res_hi, res_lo, ahead, *onward = call(
        functools.partial(ahead_kernel, node_devs),
        [struct((span, rows_dev), bf16), struct((span, rows_dev), bf16), struct((3 * rhs_dev, LANES))]
        + [struct((res_rows, *field))] * (node_devs - 1),
        (*packs[1:], pack, lines, there),
    )
    others = [lax.ppermute(value, "rhs", swap) for value in onward]
    message, prod_hi, prod_lo = call(
        gram_kernel,
        [
            struct((3 * rhs_dev, LANES)),
            struct((span, rows_dev), bf16),
            struct((span, rows_dev), bf16),
        ],
        (product, lax.ppermute(product, "rhs", swap), res_hi, res_lo, ahead),
    )

    if shifted:
        total = message
        for d in range(panel_devs - 1, 0, -1):
            pairs = [(i, (i + d) % panel_devs) for i in range(panel_devs)]
            total = total + lax.ppermute(message, "panels", pairs)
    else:
        total = lax.psum(message, "panels")
    sums = [total] + [lax.ppermute(total, "nodes", pairs) for pairs in node_pairs[1:]]
    scale_factor = 1.0 / math.sqrt(rows_dev * panel_devs)
    residual_next, moments, hankel = call(
        functools.partial(finish_kernel, (1, node_devs, nodes_all, scale_factor)),
        [
            struct(residual.shape),
            struct((MOM_DEV, 2, rhs_dev, rows_dev)),
            struct((MOM_DEV, 2, rhs_dev, cols)),
        ],
        (*sums, *packs, *others, prod_hi, prod_lo, res_hi, res_lo, consts),
    )
    return residual_next, moments, hankel.transpose(0, 1, 3, 2)


def solution(mesh):
    return jax.shard_map(
        per_device,
        mesh=mesh,
        in_specs=(
            P(("groups", "nodes"), None, "rhs", "panels"),
            P(("groups", "nodes"), None, "rhs", "panels"),
            P("groups", "rhs", "panels"),
            P("groups"),
            P(("groups", "panels"), None, None, None),
            P(("groups", "panels")),
            P(("groups", "panels")),
            P(("groups", "panels"), None),
            P(("groups", "panels"), None, None, None),
            P(("groups", "panels")),
            P(("groups", "panels")),
            P(("groups", "panels")),
            P(("groups", "panels"), None, None, None),
        ),
        out_specs=(
            P(("groups", "nodes"), None, "rhs", "panels"),
            P(("groups", "nodes"), None, "rhs", "panels"),
            P(("groups", "nodes"), None, None, "rhs"),
        ),
        check_vma=False,
    )
```
